32 devices in a mesh: chan: 32 (over z, y, x, core), win: 1.
Axes of the slice: x: 2, y: 2, z: 4, core: 2. Of those that a mesh axis runs over, the one named last changes fastest.
Arguments:
- traces: bfloat16 [512, 48, 1500], P('chan', 'win'), may hold values from -6 to 6
- source_index: int32 [64], replicated, may hold values from 0 to 511
Outputs:
- stack: float32 [2, 64, 512, 256], P(None, 'win', 'chan')
The draws below stay inside these ranges and needn't reach their ends.
All inputs are finite; a program needn't handle non-finite values.
Results may differ from the reference program's by a relative error of at most 0.0058.
Values may be sent and summed in bfloat16 or wider, within the bound.
No kernel may reach another device: no remote copies, remote signals or barrier semaphores. Data moves between devices by JAX's collectives and lax.ppermute only.
A program may use at most 64 MiB of HBM per device.

```python
import math
import jax
import jax.numpy as jnp
from jax import lax

CH_DEV = 16
L = 1500
F = 256
F0 = 1
K = 64
GAUGE = 4
S = 64
C = 512
W = 48


def set_ends(array, rng, smallest, largest):
    place = [jax.random.randint(jax.random.fold_in(rng, axis), (), 0, length) for axis, length in enumerate(array.shape)]
    longest = array.shape.index(max(array.shape))
    neighbour = place[:longest] + [(place[longest] + 1) % array.shape[longest]] + place[longest + 1:]
    return array.at[tuple(place)].set(smallest).at[tuple(neighbour)].set(largest)


def block_levels(own_key, shape, cuts, low, high):
    loudness, own = 1.0, jax.random.fold_in(own_key, 6)
    for dim, blocks in cuts:
        heights = jnp.exp(jax.random.uniform(jax.random.fold_in(own, dim), (blocks,), jnp.float32, low / len(cuts), high / len(cuts)))
        loudness = loudness * jnp.repeat(heights, shape[dim] // blocks).reshape([-1 if axis == dim else 1 for axis in range(len(shape))])
    return loudness


def gaussian(stream_key, dims, deviation, most, shards=(), kind=jnp.bfloat16):
    values = deviation * jax.random.normal(stream_key, dims, jnp.float32)
    if shards:
        values = values * block_levels(stream_key, dims, shards, -0.22, 0.18)
    return jnp.clip(values, -most, most).astype(kind)


def setup_inputs(seed: int = 0) -> dict:
    key_list = jax.random.split(jax.random.key(seed), 3)
    traces = gaussian(key_list[0], (C, W, L), 1.0, 6.0, ((0, 32),))
    source_index = set_ends(jax.random.randint(key_list[1], (S,), 0, C), jax.random.fold_in(key_list[1], 1), 0, C - 1).astype(jnp.int32)
    return {"traces": traces, "source_index": source_index}


def make_table():
    times = jnp.arange(L, dtype=jnp.int32)[:, None]
    bins = jnp.arange(F, dtype=jnp.int32)[None, :] + F0
    phase = (times * bins % L).astype(jnp.float32) * (2.0 * math.pi / L)
    return jnp.concatenate([jnp.cos(phase), -jnp.sin(phase)], axis=1).astype(jnp.bfloat16)

def make_band():
    rows = jnp.arange(F, dtype=jnp.int32)[:, None]
    cols = jnp.arange(F, dtype=jnp.int32)[None, :]
    band = (jnp.abs(rows - cols) <= K).astype(jnp.float32)
    return (band, lax.optimization_barrier(jnp.sum(band, axis=0)))

def whiten(block, upper, table, band, counts):
    ext = jnp.concatenate([block, upper], axis=0).astype(jnp.float32)
    diff = ext[GAUGE:] - ext[:-GAUGE]
    scale = jnp.sqrt(lax.optimization_barrier(jnp.mean(diff * diff, axis=2, keepdims=True)) + 1e-05)
    normed = (diff / scale).astype(jnp.bfloat16)
    rows = normed.shape[0] * normed.shape[1]
    spec = jnp.dot(normed.reshape(rows, L).astype(jnp.float32), table.astype(jnp.float32), precision=lax.Precision.HIGHEST)
    real_part = spec[:, :F]
    imag_part = spec[:, F:]
    magnitude = jnp.sqrt(real_part * real_part + imag_part * imag_part)
    smooth = jnp.dot(magnitude, band, precision=lax.Precision.HIGHEST) / counts
    shape = (normed.shape[0], normed.shape[1], F)
    white_re = (real_part / (smooth + 1e-06)).astype(jnp.bfloat16).reshape(shape)
    white_im = (imag_part / (smooth + 1e-06)).astype(jnp.bfloat16).reshape(shape)
    return (white_re, white_im)

def reference(traces, source_index):
    table = make_table()
    band, counts = make_band()
    blocks = C // CH_DEV

    def one_block(index):
        block = lax.dynamic_slice_in_dim(traces, index * CH_DEV, CH_DEV, 0)
        start = jnp.minimum(index * CH_DEV + CH_DEV, C - GAUGE).astype(jnp.int32)
        upper = lax.dynamic_slice_in_dim(traces, start, GAUGE, 0)
        upper = jnp.where(index < blocks - 1, upper, jnp.zeros_like(upper))
        return whiten(block, upper, table, band, counts)
    white_re, white_im = lax.map(one_block, jnp.arange(blocks, dtype=jnp.int32))
    white_re = white_re.reshape(C, W, F)
    white_im = white_im.reshape(C, W, F)
    source_re = white_re[source_index].astype(jnp.float32)
    source_im = white_im[source_index].astype(jnp.float32)

    def correlate(index):
        chan_re = lax.dynamic_slice_in_dim(white_re, index * CH_DEV, CH_DEV, 0).astype(jnp.float32)
        chan_im = lax.dynamic_slice_in_dim(white_im, index * CH_DEV, CH_DEV, 0).astype(jnp.float32)
        real_out = jnp.einsum('swf,cwf->scf', source_re, chan_re) + jnp.einsum('swf,cwf->scf', source_im, chan_im)
        imag_out = jnp.einsum('swf,cwf->scf', source_im, chan_re) - jnp.einsum('swf,cwf->scf', source_re, chan_im)
        return jnp.stack([real_out, imag_out]) * (1.0 / W)
    parts = lax.map(correlate, jnp.arange(blocks, dtype=jnp.int32))
    return jnp.transpose(parts, (1, 2, 0, 3, 4)).reshape(2, S, C, F)
```

```python
import math

import jax
import jax.numpy as jnp
import ml_dtypes
import numpy as np
from jax import lax
from jax.experimental import pallas as pl
from jax.experimental.pallas import tpu as pltpu
from jax.sharding import PartitionSpec as P

F = 256
HALF = 128
F0 = 1
K = 64
GAUGE = 4
LANES = 128
VMEM_LIMIT = 48 * 1024 * 1024


def make_table(length):
    times = np.arange(length, dtype=np.int64)[:, None]
    bins = np.arange(F, dtype=np.int64)[None, :] + F0
    phase = (times * bins % length).astype(np.float32) * np.float32(2.0 * math.pi / length)
    phase = phase.astype(np.float64)
    return np.concatenate([np.cos(phase), -np.sin(phase)], axis=1).astype(ml_dtypes.bfloat16)


def make_band():
    rows = np.arange(F)[:, None]
    cols = np.arange(F)[None, :]
    band = np.abs(rows - cols) <= K
    return band.astype(ml_dtypes.bfloat16), (1.0 / band.sum(axis=0)).astype(np.float32)[None, :]


def whiten_kernel(
    steps, cur_ref, next_ref, halo_ref, table_ref, band_ref, inv_ref, rows_ref, left_ref, t_re, t_im
):
    step = pl.program_id(0)
    gauge, wins, length = cur_ref.shape
    is_last = step == steps - 1
    for c in range(gauge):
        upper = jnp.where(is_last, halo_ref[c], next_ref[c]).astype(jnp.float32)
        diff = upper - cur_ref[c].astype(jnp.float32)
        power = jnp.sum(diff * diff, axis=1, keepdims=True) * (1.0 / length)
        normed = (diff * lax.rsqrt(power + 1e-05)).astype(jnp.bfloat16)
        spec = jnp.dot(normed, table_ref[...], preferred_element_type=jnp.float32)
        real = spec[:, :F]
        imag = spec[:, F:]
        magnitude = jnp.sqrt(real * real + imag * imag).astype(jnp.bfloat16)
        smooth = jnp.dot(magnitude, band_ref[...], preferred_element_type=jnp.float32) * inv_ref[...]
        gain = 1.0 / (smooth + 1e-06)
        white_re = (real * gain).astype(jnp.bfloat16).astype(jnp.float32)
        white_im = (imag * gain).astype(jnp.bfloat16).astype(jnp.float32)
        pad = jnp.zeros((LANES - 2 * wins, F), jnp.float32)
        base = (step * gauge + c) * F
        t_re[pl.ds(base, F), :] = jnp.concatenate([white_re, white_im, pad], axis=0).T
        t_im[pl.ds(base, F), :] = jnp.concatenate([-white_im, white_re, pad], axis=0).T

    @pl.when(is_last)
    def _():
        chans = steps * gauge
        dests = rows_ref.shape[0]
        per_dest = HALF // dests
        lane = lax.broadcasted_iota(jnp.int32, (chans, LANES), 1)

        def relayout(dest, carry):
            for pair in range(per_dest // 2):
                piece = []
                for j in range(2):
                    g = dest * per_dest + pair * 2 + j
                    stack = []
                    for half in range(2):
                        re = t_re[pl.ds(half * HALF + g, chans, stride=F), :]
                        im = t_im[pl.ds(half * HALF + g, chans, stride=F), :]
                        stack += [re, im]
                        piece.append(re)
                    left_ref[g] = jnp.concatenate(stack, axis=0).astype(jnp.bfloat16)
                a, b, c, d = piece
                b = pltpu.roll(b, 96, 1)
                c = pltpu.roll(c, 64, 1)
                d = pltpu.roll(d, 32, 1)
                first = jnp.where(lane < 96, a, b)
                second = jnp.where(lane < 64, b, c)
                third = jnp.where(lane < 32, c, d)
                row = jnp.concatenate([first, second, third], axis=1).astype(jnp.bfloat16)
                rows_ref[dest, :, pair * 384 : (pair + 1) * 384] = row
            return carry

        lax.fori_loop(0, dests, relayout, 0)


def pick_kernel(index_ref, rows_ref, out_ref):
    sources = index_ref.shape[0]
    channels, width = rows_ref.shape
    ids = lax.broadcasted_iota(jnp.int32, (sources, channels), 1)
    onehot = jnp.where(ids == index_ref[...], 1.0, 0.0).astype(jnp.bfloat16)
    picked = jnp.dot(onehot, rows_ref[...], preferred_element_type=jnp.float32)
    turned = picked.T
    groups, depth, _ = out_ref.shape
    for g in range(groups):
        low = turned[(2 * g) * depth : (2 * g + 1) * depth]
        high = turned[(2 * g + 1) * depth : (2 * g + 2) * depth]
        out_ref[g] = jnp.concatenate([low, high], axis=1).astype(jnp.bfloat16)


def correlate_kernel(scale, left_ref, right_ref, out_ref, held, turned_ref, sems):
    step = pl.program_id(0)
    groups, rows, _ = left_ref.shape
    depth, width = right_ref.shape[1:]
    sources = width // 2
    outs = rows // 2
    lane = lax.broadcasted_iota(jnp.int32, (outs, width), 1)
    for g in range(groups):
        both = jnp.dot(left_ref[g][:, :depth], right_ref[g], preferred_element_type=jnp.float32)
        mine = jnp.where(lane < sources, both[:outs], both[outs:])
        held[pl.ds(step * groups + g, outs, stride=HALF), :] = mine

    @pl.when(step == pl.num_programs(0) - 1)
    def _():
        chans = outs // 2
        size = sources * chans
        copies = []
        for part in range(2):
            for c in range(chans):
                base = (part * chans + c) * HALF
                turned = held[base : base + HALF, :].T * scale
                rows_at = pl.ds(part * size + c, sources, stride=chans)
                for half in range(2):
                    turned_ref.at[half][rows_at, :] = turned[half * sources : (half + 1) * sources]
            for half in range(2):
                span = pl.ds(part * size, size)
                copy = pltpu.make_async_copy(
                    turned_ref.at[half, span],
                    out_ref.at[span, pl.ds(half * HALF, HALF)],
                    sems.at[part, half],
                )
                copy.start()
                copies.append(copy)
        for copy in copies:
            copy.wait()


def per_device(traces, source_index):
    chans, wins, length = traces.shape
    n = lax.axis_size("chan")
    sources = source_index.shape[0]
    route = [(i + 1, i) for i in range(n - 1)]
    halo = lax.ppermute(traces[:GAUGE], "chan", route)
    table = jnp.asarray(make_table(length))
    band, inv = make_band()
    steps = chans // GAUGE
    depth = 2 * wins
    row_width = HALF * 2 * depth // n
    block = (GAUGE, wins, length)
    whole = lambda *shape: pl.BlockSpec(shape, lambda i: (0,) * len(shape))
    rows, left = pl.pallas_call(
        lambda *refs: whiten_kernel(steps, *refs),
        grid=(steps,),
        in_specs=[
            pl.BlockSpec(block, lambda i: (i, 0, 0)),
            pl.BlockSpec(block, lambda i: (jnp.minimum(i + 1, steps - 1), 0, 0)),
            whole(*block),
            whole(length, 2 * F),
            whole(F, F),
            whole(1, F),
        ],
        out_specs=[whole(n, chans, row_width), whole(HALF, 4 * chans, LANES)],
        out_shape=[
            jax.ShapeDtypeStruct((n, chans, row_width), jnp.bfloat16),
            jax.ShapeDtypeStruct((HALF, 4 * chans, LANES), jnp.bfloat16),
        ],
        scratch_shapes=[pltpu.VMEM((chans * F, LANES), jnp.float32)] * 2,
        compiler_params=pltpu.CompilerParams(vmem_limit_bytes=VMEM_LIMIT),
        name="whiten",
    )(traces, traces, halo, table, jnp.asarray(band), jnp.asarray(inv))

    rows = lax.all_to_all(rows, "chan", 0, 0, tiled=True).reshape(n * chans, row_width)
    picked = pl.pallas_call(
        pick_kernel,
        out_shape=jax.ShapeDtypeStruct((HALF // n, depth, 2 * sources), jnp.bfloat16),
        compiler_params=pltpu.CompilerParams(vmem_limit_bytes=VMEM_LIMIT),
        name="pick",
    )(source_index.reshape(sources, 1), rows)

    right = lax.all_gather(picked, "chan", axis=0, tiled=True)

    groups = 16
    total_windows = wins * lax.axis_size("win")
    flat = pl.pallas_call(
        lambda *refs: correlate_kernel(1.0 / total_windows, *refs),
        grid=(HALF // groups,),
        in_specs=[
            pl.BlockSpec((groups, 4 * chans, LANES), lambda i: (i, 0, 0)),
            pl.BlockSpec((groups, depth, 2 * sources), lambda i: (i, 0, 0)),
        ],
        out_specs=pl.BlockSpec(memory_space=pl.ANY),
        out_shape=jax.ShapeDtypeStruct((2 * sources * chans, F), jnp.float32),
        scratch_shapes=[
            pltpu.VMEM((2 * chans * HALF, LANES), jnp.float32),
            pltpu.VMEM((2, 2 * sources * chans, HALF), jnp.float32),
            pltpu.SemaphoreType.DMA((2, 2)),
        ],
        compiler_params=pltpu.CompilerParams(vmem_limit_bytes=VMEM_LIMIT),
        name="correlate",
    )(left, right)
    stack = flat.reshape(2, sources, chans, F)
    if lax.axis_size("win") == 1:
        return stack
    return lax.psum_scatter(stack, "win", scatter_dimension=1, tiled=True)


def solution(mesh):
    return jax.shard_map(
        per_device,
        mesh=mesh,
        in_specs=(P("chan", "win", None), P()),
        out_specs=P(None, "win", "chan", None),
        check_vma=False,
    )
```

```python
import math

import jax
import jax.numpy as jnp
import ml_dtypes
import numpy as np
from jax import lax
from jax.experimental import pallas as pl
from jax.experimental.pallas import tpu as pltpu
from jax.sharding import PartitionSpec as P

F = 256
HALF = 128
F0 = 1
K = 64
GAUGE = 4
LANES = 128
VMEM_LIMIT = 24 * 1024 * 1024


def make_table(length):
    times = np.arange(length, dtype=np.int64)[:, None]
    bins = np.arange(F, dtype=np.int64)[None, :] + F0
    phase = (times * bins % length).astype(np.float32) * np.float32(2.0 * math.pi / length)
    phase = phase.astype(np.float64)
    return np.concatenate([np.cos(phase), -np.sin(phase)], axis=1).astype(ml_dtypes.bfloat16)


def make_band():
    rows = np.arange(F)[:, None]
    cols = np.arange(F)[None, :]
    band = np.abs(rows - cols) <= K
    return band.astype(ml_dtypes.bfloat16), (1.0 / band.sum(axis=0)).astype(np.float32)[None, :]


def whiten_block(cur, upper, table_ref, band_ref, inv_ref, t_re, t_im, first):
    chans, wins, length = cur.shape
    rows = chans * wins
    diff = (upper.astype(jnp.float32) - cur.astype(jnp.float32)).reshape(rows, length)
    power = jnp.sum(diff * diff, axis=1, keepdims=True) * (1.0 / length)
    normed = (diff * lax.rsqrt(power + 1e-05)).astype(jnp.bfloat16)
    spec = jnp.dot(normed, table_ref[...], preferred_element_type=jnp.float32)
    real = spec[:, :F]
    imag = spec[:, F:]
    magnitude = jnp.sqrt(real * real + imag * imag).astype(jnp.bfloat16)
    smooth = jnp.dot(magnitude, band_ref[...], preferred_element_type=jnp.float32) * inv_ref[...]
    gain = 1.0 / (smooth + 1e-06)
    white_re = (real * gain).astype(jnp.bfloat16).astype(jnp.float32)
    white_im = (imag * gain).astype(jnp.bfloat16).astype(jnp.float32)
    pad = jnp.zeros((LANES - 2 * wins, F), jnp.float32)
    for c in range(chans):
        mine_re = white_re[c * wins : (c + 1) * wins]
        mine_im = white_im[c * wins : (c + 1) * wins]
        span = pl.ds((first + c) * F, F)
        t_re[span, :] = jnp.concatenate([mine_re, mine_im, pad], axis=0).T
        t_im[span, :] = jnp.concatenate([-mine_im, mine_re, pad], axis=0).T


def whiten_kernel(cur_ref, upper_ref, table_ref, band_ref, inv_ref, t_re, t_im):
    first = pl.program_id(0) * GAUGE
    whiten_block(cur_ref[...], upper_ref[...], table_ref, band_ref, inv_ref, t_re, t_im, first)


def finish_kernel(
    cur_ref, halo_ref, table_ref, band_ref, inv_ref, in_re, in_im, rows_ref, left_ref, t_re, t_im
):
    whiten_block(cur_ref[...], halo_ref[...], table_ref, band_ref, inv_ref, t_re, t_im, 8 - GAUGE)
    chans = in_re.shape[0] // F
    dests = rows_ref.shape[0]
    per_dest = HALF // dests
    lane = lax.broadcasted_iota(jnp.int32, (chans, LANES), 1)
    sub = lax.broadcasted_iota(jnp.int32, (8, LANES), 0)

    def bin_rows(old, new, at):
        top = old[pl.ds(at, chans - 8, stride=F), :]
        mixed = old[pl.ds((chans - 8) * F + at, 8, stride=F), :]
        tail = new[pl.ds(at, 8, stride=F), :]
        return jnp.concatenate([top, jnp.where(sub < 8 - GAUGE, mixed, tail)], axis=0)

    def relayout(dest, carry):
        for pair in range(per_dest // 2):
            piece = []
            for j in range(2):
                g = dest * per_dest + pair * 2 + j
                stack = []
                for half in range(2):
                    re = bin_rows(in_re, t_re, half * HALF + g)
                    im = bin_rows(in_im, t_im, half * HALF + g)
                    stack += [re, im]
                    piece.append(re)
                left_ref[g] = jnp.concatenate(stack, axis=0).astype(jnp.bfloat16)
            a, b, c, d = piece
            b = pltpu.roll(b, 96, 1)
            c = pltpu.roll(c, 64, 1)
            d = pltpu.roll(d, 32, 1)
            first = jnp.where(lane < 96, a, b)
            second = jnp.where(lane < 64, b, c)
            third = jnp.where(lane < 32, c, d)
            row = jnp.concatenate([first, second, third], axis=1).astype(jnp.bfloat16)
            rows_ref[dest, :, pair * 384 : (pair + 1) * 384] = row
        return carry

    lax.fori_loop(0, dests, relayout, 0)


def pick_kernel(index_ref, rows_ref, out_ref):
    sources = index_ref.shape[0]
    channels, width = rows_ref.shape
    ids = lax.broadcasted_iota(jnp.int32, (sources, channels), 1)
    onehot = jnp.where(ids == index_ref[...], 1.0, 0.0).astype(jnp.bfloat16)
    picked = jnp.dot(onehot, rows_ref[...], preferred_element_type=jnp.float32)
    turned = picked.T
    groups, depth, _ = out_ref.shape
    for g in range(groups):
        low = turned[(2 * g) * depth : (2 * g + 1) * depth]
        high = turned[(2 * g + 1) * depth : (2 * g + 2) * depth]
        out_ref[g] = jnp.concatenate([low, high], axis=1).astype(jnp.bfloat16)


def correlate_kernel(scale, n, origins, me_ref, left_ref, *refs):
    pieces, (out_ref, held, turned_ref, sems) = refs[:-4], refs[-4:]
    rows = left_ref.shape[1]
    depth, width = pieces[0].shape[-2:]
    groups = HALF // n
    planes = n // 8
    sources = width // 2
    outs = rows // 2
    me = me_ref[0]
    lane = lax.broadcasted_iota(jnp.int32, (outs, width), 1)
    for piece, runs in zip(pieces, origins):
        for run, (flip, part, parts) in enumerate(runs):
            count = groups // parts

            def plane(back, carry, piece=piece, run=run, flip=flip, part=part, count=count):
                owner = lax.rem(me + n - 8 * back, n) ^ flip
                for j in range(count):
                    g = owner * groups + part * count + j
                    right = piece[(run * planes + back) * count + j]
                    both = jnp.dot(left_ref[g][:, :depth], right, preferred_element_type=jnp.float32)
                    mine = jnp.where(lane < sources, both[:outs], both[outs:])
                    held[pl.ds(g, outs, stride=HALF), :] = mine
                return carry

            lax.fori_loop(0, planes, plane, 0, unroll=2)
    chans = outs // 2
    size = sources * chans
    copies = []
    for part in range(2):
        for c in range(chans):
            base = (part * chans + c) * HALF
            turned = held[base : base + HALF, :].T * scale
            rows_at = pl.ds(part * size + c, sources, stride=chans)
            for half in range(2):
                turned_ref.at[half][rows_at, :] = turned[half * sources : (half + 1) * sources]
        for half in range(2):
            span = pl.ds(part * size, size)
            copy = pltpu.make_async_copy(
                turned_ref.at[half, span],
                out_ref.at[span, pl.ds(half * HALF, HALF)],
                sems.at[part, half],
            )
            copy.start()
            copies.append(copy)
    for copy in copies:
        copy.wait()


def gather_pieces(own):
    n = lax.axis_size("chan")
    planes = n // 8
    half = own.shape[0] // 2
    core, x, y = 1, 2, 4

    def send(block, flip):
        return lax.ppermute(block, "chan", [(i, i ^ flip) for i in range(n)])

    def column(shift):
        return lax.ppermute(own, "chan", [(i, (i + 8 * shift) % n) for i in range(n)])

    col = [own] + [column(shift) for shift in range(1, planes)]
    col_a = jnp.concatenate([p[:half] for p in col], axis=0)
    col_b = jnp.concatenate([p[half:] for p in col], axis=0)
    x_a = send(col_a, x)
    y_b = send(col_b, y)
    first = jnp.concatenate([col_a, col_b], axis=0)
    second = jnp.concatenate([x_a, y_b], axis=0)
    y_a = send(jnp.concatenate([col_a, x_a], axis=0), y)
    x_b = send(jnp.concatenate([col_b, y_b], axis=0), x)
    arrays = [first, second, y_a, x_b]
    origins = [
        [(0, 0, 2), (0, 1, 2)],
        [(x, 0, 2), (y, 1, 2)],
        [(y, 0, 2), (x ^ y, 0, 2)],
        [(x, 1, 2), (x ^ y, 1, 2)],
    ]
    traded = [[(flip ^ core, part, parts) for flip, part, parts in runs] for runs in origins]
    return arrays + [send(a, core) for a in arrays], origins + traded


def per_device(traces, source_index):
    chans, wins, length = traces.shape
    n = lax.axis_size("chan")
    sources = source_index.shape[0]
    route = [(i + 1, i) for i in range(n - 1)]
    halo = lax.ppermute(traces[:GAUGE], "chan", route)
    table = jnp.asarray(make_table(length))
    band, inv = make_band()
    band, inv = jnp.asarray(band), jnp.asarray(inv)
    steps = chans // GAUGE
    depth = 2 * wins
    row_width = HALF * 2 * depth // n
    block = (GAUGE, wins, length)
    vmem = pl.BlockSpec(memory_space=pltpu.VMEM)
    consts = [vmem] * 3
    params = pltpu.CompilerParams(vmem_limit_bytes=VMEM_LIMIT)
    turned = jax.ShapeDtypeStruct((chans * F, LANES), jnp.float32)
    t_re, t_im = pl.pallas_call(
        whiten_kernel,
        grid=(steps - 1,),
        in_specs=[
            pl.BlockSpec(block, lambda i: (i, 0, 0)),
            pl.BlockSpec(block, lambda i: (i + 1, 0, 0)),
            *consts,
        ],
        out_specs=[vmem] * 2,
        out_shape=[turned] * 2,
        compiler_params=params,
        cost_estimate=pl.CostEstimate(
            flops=2 * (chans - GAUGE) * wins * (length + F // 2) * 2 * F,
            bytes_accessed=8 * 1024 * 1024,
            transcendentals=0,
        ),
        name="whiten",
    )(traces, traces, table, band, inv)
    rows, left = pl.pallas_call(
        finish_kernel,
        grid=(1,),
        in_specs=[
            pl.BlockSpec(block, lambda i: (steps - 1, 0, 0)),
            vmem,
            *consts,
            vmem,
            vmem,
        ],
        out_specs=[vmem] * 2,
        out_shape=[
            jax.ShapeDtypeStruct((n, chans, row_width), jnp.bfloat16),
            jax.ShapeDtypeStruct((HALF, 4 * chans, LANES), jnp.bfloat16),
        ],
        scratch_shapes=[pltpu.VMEM((8 * F, LANES), jnp.float32)] * 2,
        compiler_params=params,
        name="finish",
    )(traces, halo, table, band, inv, t_re, t_im)

    rows = lax.all_to_all(rows, "chan", 0, 0, tiled=True).reshape(n * chans, row_width)
    picked = pl.pallas_call(
        pick_kernel,
        out_shape=jax.ShapeDtypeStruct((HALF // n, depth, 2 * sources), jnp.bfloat16),
        compiler_params=params,
        name="pick",
    )(source_index.reshape(sources, 1), rows)

    pieces, origins = gather_pieces(picked)
    me = lax.axis_index("chan").astype(jnp.int32).reshape(1)

    total_windows = wins * lax.axis_size("win")
    flat = pl.pallas_call(
        lambda *refs: correlate_kernel(1.0 / total_windows, n, origins, *refs),
        in_specs=[pl.BlockSpec(memory_space=pltpu.SMEM), vmem] + [vmem] * len(pieces),
        out_specs=pl.BlockSpec(memory_space=pl.ANY),
        out_shape=jax.ShapeDtypeStruct((2 * sources * chans, F), jnp.float32),
        scratch_shapes=[
            pltpu.VMEM((2 * chans * HALF, LANES), jnp.float32),
            pltpu.VMEM((2, 2 * sources * chans, HALF), jnp.float32),
            pltpu.SemaphoreType.DMA((2, 2)),
        ],
        compiler_params=params,
        name="correlate",
    )(me, left, *pieces)
    stack = flat.reshape(2, sources, chans, F)
    if lax.axis_size("win") == 1:
        return stack
    return lax.psum_scatter(stack, "win", scatter_dimension=1, tiled=True)


def solution(mesh):
    return jax.shard_map(
        per_device,
        mesh=mesh,
        in_specs=(P("chan", "win", None), P()),
        out_specs=P(None, "win", "chan", None),
        check_vma=False,
    )
```

```python
import functools
import math

import jax
import jax.numpy as jnp
import ml_dtypes
import numpy as np
from jax import lax
from jax.experimental import pallas as pl
from jax.experimental.pallas import tpu as pltpu
from jax.sharding import PartitionSpec as P

F = 256
HALF = 128
F0 = 1
K = 64
GAUGE = 4
LANES = 128
VMEM_LIMIT = 24 * 1024 * 1024


def make_table(length):
    times = np.arange(length, dtype=np.int64)[:, None]
    bins = np.arange(F, dtype=np.int64)[None, :] + F0
    phase = (times * bins % length).astype(np.float32) * np.float32(2.0 * math.pi / length)
    phase = phase.astype(np.float64)
    return np.concatenate([np.cos(phase), -np.sin(phase)], axis=1).astype(ml_dtypes.bfloat16)


def make_band():
    rows = np.arange(F)[:, None]
    cols = np.arange(F)[None, :]
    band = np.abs(rows - cols) <= K
    return band.astype(ml_dtypes.bfloat16), (1.0 / band.sum(axis=0)).astype(np.float32)[None, :]


def whiten_block(cur, upper, table_ref, band_ref, inv_ref, turned_ref, first):
    chans, wins, length = cur.shape
    rows = chans * wins
    diff = (upper.astype(jnp.float32) - cur.astype(jnp.float32)).reshape(rows, length)
    power = jnp.sum(diff * diff, axis=1, keepdims=True) * (1.0 / length)
    normed = (diff * lax.rsqrt(power + 1e-05)).astype(jnp.bfloat16)
    spec = jnp.dot(normed, table_ref[...], preferred_element_type=jnp.float32)
    real = spec[:, :F]
    imag = spec[:, F:]
    magnitude = jnp.sqrt(real * real + imag * imag).astype(jnp.bfloat16)
    smooth = jnp.dot(magnitude, band_ref[...], preferred_element_type=jnp.float32) * inv_ref[...]
    gain = 1.0 / (smooth + 1e-06)
    white_re = (real * gain).astype(jnp.bfloat16).astype(jnp.float32)
    white_im = (imag * gain).astype(jnp.bfloat16).astype(jnp.float32)
    pad = jnp.zeros((LANES - 2 * wins, F), jnp.float32)
    for c in range(chans):
        mine = slice(c * wins, (c + 1) * wins)
        both = jnp.concatenate([white_re[mine], white_im[mine], pad], axis=0)
        turned_ref[pl.ds((first + c) * F, F), :] = both.T


def whiten_kernel(cur_ref, upper_ref, table_ref, band_ref, inv_ref, turned_ref):
    first = pl.program_id(0) * GAUGE
    whiten_block(cur_ref[...], upper_ref[...], table_ref, band_ref, inv_ref, turned_ref, first)


def finish_kernel(
    chans, slots, slot_ref, cur_ref, halo_ref, table_ref, band_ref, inv_ref, _, *refs
):
    turned_ref, rounds, listed = refs[0], refs[1:-1], refs[-1]
    whiten_block(
        cur_ref[...], halo_ref[...], table_ref, band_ref, inv_ref, turned_ref, chans - GAUGE
    )
    dests, _, width = rounds[0].shape
    pairs = HALF // dests // 2
    lane = lax.broadcasted_iota(jnp.int32, (slots, LANES), 1)

    def fill(number, rows_ref):
        for k in range(slots):
            channel = slot_ref[number * slots + k]
            listed[k * F : (k + 1) * F, :] = turned_ref[pl.ds(channel * F, F), :]

        def relayout(dest, carry):
            block = []
            for pair in range(pairs):
                piece = []
                for j in range(2):
                    for half in range(2):
                        at = half * HALF + (dest * pairs + pair) * 2 + j
                        piece.append(listed[pl.ds(at, slots, stride=F), :])
                a, b, c, d = piece
                b = pltpu.roll(b, 96, 1)
                c = pltpu.roll(c, 64, 1)
                d = pltpu.roll(d, 32, 1)
                first = jnp.where(lane < 96, a, b)
                second = jnp.where(lane < 64, b, c)
                third = jnp.where(lane < 32, c, d)
                block.append(jnp.concatenate([first, second, third], axis=1))
            rows_ref[dest] = jnp.concatenate(block, axis=0).astype(jnp.bfloat16)
            return carry

        lax.fori_loop(0, dests, relayout, 0, unroll=4)

    fill(0, rounds[0])
    for number in range(1, len(rounds)):
        pl.when(slot_ref[chans] > number * slots)(
            functools.partial(fill, number, rounds[number])
        )


def left_kernel(chans, depth, turned_ref, left_ref):
    lane = lax.broadcasted_iota(jnp.int32, (chans, LANES), 1)

    def one(g, carry):
        stack = []
        for half in range(2):
            real = turned_ref[pl.ds(half * HALF + g, chans, stride=F), :]
            ahead = pltpu.roll(real, depth // 2, 1)
            back = pltpu.roll(real, LANES - depth // 2, 1)
            stack += [real, jnp.where(lane < depth // 2, -back, ahead)]
        left_ref[g] = jnp.concatenate(stack, axis=0).astype(jnp.bfloat16)
        return carry

    lax.fori_loop(0, HALF, one, 0, unroll=8)


def pick_kernel(slots, base, place_ref, rows_ref, out_ref):
    sources = place_ref.shape[0]
    dests, height, width = rows_ref.shape
    groups, depth, _ = out_ref.shape
    rows = rows_ref[...].reshape(dests * height, width)
    ids = lax.broadcasted_iota(jnp.int32, (sources, dests * height), 1)
    place = place_ref[...] - base
    inside = (place >= 0) & (place < dests * slots)
    spot = place // slots * height + place % slots
    for pair in range(groups // 2):
        hit = inside & (ids == spot + pair * slots)
        onehot = jnp.where(hit, 1.0, 0.0).astype(jnp.bfloat16)
        turned = jnp.dot(onehot, rows, preferred_element_type=jnp.float32).T
        for j in range(2):
            low = turned[(2 * j) * depth : (2 * j + 1) * depth]
            high = turned[(2 * j + 1) * depth : (2 * j + 2) * depth]
            out_ref[pair * 2 + j] = jnp.concatenate([low, high], axis=1).astype(jnp.bfloat16)


def products(n, origins, me_ref, left_ref, pieces, held):
    rows = left_ref.shape[1]
    depth, width = pieces[0].shape[-2:]
    groups = HALF // n
    sources = width // 2
    outs = rows // 2
    me = me_ref[0]
    lane = lax.broadcasted_iota(jnp.int32, (outs, width), 1)
    for piece, runs in zip(pieces, origins):
        place = 0
        for backs, flip, start, count in runs:
            for back in backs:
                owner = lax.rem(me + n - 8 * back, n) ^ flip
                for j in range(count):
                    g = owner * groups + start + j
                    both = jnp.dot(
                        left_ref[g][:, :depth], piece[place], preferred_element_type=jnp.float32
                    )
                    mine = jnp.where(lane < sources, both[:outs], both[outs:])
                    held[pl.ds(g, outs, stride=HALF), :] = mine
                    place += 1


def partial_kernel(n, origins, chained, me_ref, left_ref, *refs):
    products(n, origins, me_ref, left_ref, refs[chained:-1], refs[-1])


def correlate_kernel(scale, n, origins, sources, me_ref, left_ref, _, *refs):
    pieces, (out_ref, held, turned_ref, sems) = refs[:-4], refs[-4:]
    products(n, origins, me_ref, left_ref, pieces, held)
    outs = held.shape[0] // HALF
    chans = outs // 2
    size = sources * chans
    copies = []
    for part in range(2):
        for c in range(chans):
            base = (part * chans + c) * HALF
            turned = held[base : base + HALF, :].T * scale
            rows_at = pl.ds(part * size + c, sources, stride=chans)
            for half in range(2):
                turned_ref.at[half][rows_at, :] = turned[half * sources : (half + 1) * sources]
        for half in range(2):
            span = pl.ds(part * size, size)
            copy = pltpu.make_async_copy(
                turned_ref.at[half, span],
                out_ref.at[span, pl.ds(half * HALF, HALF)],
                sems.at[part, half],
            )
            copy.start()
            copies.append(copy)
    for copy in copies:
        copy.wait()


def gather_pieces(own):
    n = lax.axis_size("chan")
    planes = n // 8
    groups = own.shape[0]
    half = groups // 2
    core, x, y = 1, 2, 4

    def send(block, flip):
        return lax.ppermute(block, "chan", [(i, i ^ flip) for i in range(n)])

    def column(shift):
        return lax.ppermute(own, "chan", [(i, (i + 8 * shift) % n) for i in range(n)])

    def join(*blocks):
        return jnp.concatenate(blocks, axis=0)

    def traded(runs):
        return [(backs, flip ^ core, start, count) for backs, flip, start, count in runs]

    def both(arrays, origins):
        return arrays + [send(a, core) for a in arrays], origins + [traded(r) for r in origins]

    def go_round(a, b, whole, whole_origin, backs):
        x_a = send(a, x)
        y_b = send(b, y)
        y_a = send(join(a, x_a), y)
        x_b = send(join(b, y_b), x)
        first = both([whole], [whole_origin])
        second = both([join(x_a, y_b)], [[(backs, x, 0, half), (backs, y, half, half)]])
        third = both(
            [y_a, x_b],
            [
                [(backs, y, 0, half), (backs, x ^ y, 0, half)],
                [(backs, x, half, half), (backs, x ^ y, half, half)],
            ],
        )
        return first, second, third

    col = [column(shift) for shift in range(1, planes)]
    near = go_round(own[:half], own[half:], own, [((0,), 0, 0, groups)], (0,))
    backs = tuple(range(1, planes))
    col_a = join(*[p[:half] for p in col])
    col_b = join(*[p[half:] for p in col])
    origin = [(backs, 0, 0, half), (backs, 0, half, half)]
    far = go_round(col_a, col_b, join(col_a, col_b), origin, backs)
    merged = lambda *stages: (sum([s[0] for s in stages], []), sum([s[1] for s in stages], []))
    return [merged(*near), merged(far[0], far[1]), far[2]]


def plan_slots(source_index, chans, slots):
    n = lax.axis_size("chan")
    channels = jnp.arange(n * chans, dtype=jnp.int32)
    hits = source_index[:, None] == channels[None, :]
    listed = jnp.any(hits, axis=0).reshape(n, chans).astype(jnp.int32)
    below = (jnp.arange(chans)[:, None] < jnp.arange(chans)[None, :]).astype(jnp.int32)
    rank = jnp.sum(listed[:, :, None] * below[None], axis=1)
    device = jnp.arange(n, dtype=jnp.int32)[:, None]
    place = (rank // slots * n + device) * slots + rank % slots
    places = jnp.sum(jnp.where(hits, place.reshape(1, -1), 0), axis=1, keepdims=True)
    most = jnp.max(jnp.sum(listed, axis=1))
    mine = device == lax.axis_index("chan")
    order = jnp.arange(chans, dtype=jnp.int32)
    is_slot = (mine & (listed > 0))[:, :, None] & (rank[:, :, None] == order)
    held = jnp.sum(jnp.where(is_slot, order[None, :, None], 0), axis=(0, 1))
    return jnp.concatenate([held, most[None]]), places, most


def per_device(traces, source_index):
    chans, wins, length = traces.shape
    n = lax.axis_size("chan")
    sources = source_index.shape[0]
    route = [(i + 1, i) for i in range(n - 1)]
    halo = lax.ppermute(traces[:GAUGE], "chan", route)
    table = jnp.asarray(make_table(length))
    band, inv = make_band()
    band, inv = jnp.asarray(band), jnp.asarray(inv)
    steps = chans // GAUGE
    depth = 2 * wins
    row_width = HALF * 2 * depth // n
    block = (GAUGE, wins, length)
    vmem = pl.BlockSpec(memory_space=pltpu.VMEM)
    smem = pl.BlockSpec(memory_space=pltpu.SMEM)
    consts = [vmem] * 3
    params = pltpu.CompilerParams(vmem_limit_bytes=VMEM_LIMIT)
    pairs = HALF // n // 2
    slots = chans // pairs
    slot_list, places, most = plan_slots(source_index, chans, slots)
    turned = jax.ShapeDtypeStruct((chans * F, LANES), jnp.float32)
    some = pl.pallas_call(
        whiten_kernel,
        grid=(steps - 1,),
        in_specs=[
            pl.BlockSpec(block, lambda i: (i, 0, 0)),
            pl.BlockSpec(block, lambda i: (i + 1, 0, 0)),
            *consts,
        ],
        out_specs=vmem,
        out_shape=turned,
        compiler_params=params,
        cost_estimate=pl.CostEstimate(
            flops=2 * (chans - GAUGE) * wins * (length + F // 2) * 2 * F,
            bytes_accessed=8 * 1024 * 1024,
            transcendentals=0,
        ),
        name="whiten",
    )(traces, traces, table, band, inv)
    rows_shape = jax.ShapeDtypeStruct((n, chans, row_width // pairs), jnp.bfloat16)
    spectra, *rounds = pl.pallas_call(
        functools.partial(finish_kernel, chans, slots),
        grid=(1,),
        in_specs=[
            smem,
            pl.BlockSpec(block, lambda i: (steps - 1, 0, 0)),
            vmem,
            *consts,
            vmem,
        ],
        out_specs=[vmem] * (1 + pairs),
        out_shape=[turned] + [rows_shape] * pairs,
        scratch_shapes=[pltpu.VMEM((slots * F, LANES), jnp.float32)],
        input_output_aliases={6: 0},
        compiler_params=params,
        name="finish",
    )(slot_list, traces, halo, table, band, inv, some)

    def exchange(number, rows):
        rows = lax.all_to_all(rows, "chan", 0, 0, tiled=True)
        return pl.pallas_call(
            functools.partial(pick_kernel, slots, number * n * slots),
            out_shape=jax.ShapeDtypeStruct((HALF // n, depth, 2 * sources), jnp.bfloat16),
            compiler_params=params,
            name="pick",
        )(places, rows)

    picked = exchange(0, rounds[0])
    for number in range(1, pairs):
        picked = lax.cond(
            most > number * slots,
            lambda p, r, number=number: p + exchange(number, r),
            lambda p, r: p,
            picked,
            rounds[number],
        )
    left = pl.pallas_call(
        functools.partial(left_kernel, chans, depth),
        in_specs=[vmem],
        out_specs=vmem,
        out_shape=jax.ShapeDtypeStruct((HALF, 4 * chans, LANES), jnp.bfloat16),
        compiler_params=params,
        cost_estimate=pl.CostEstimate(
            flops=10 * 1000 * 1000, bytes_accessed=8 * 1024 * 1024, transcendentals=0
        ),
        name="left",
    )(spectra)

    stages = gather_pieces(picked)
    me = lax.axis_index("chan").astype(jnp.int32).reshape(1)
    total_windows = wins * lax.axis_size("win")
    held_shape = jax.ShapeDtypeStruct((2 * chans * HALF, LANES), jnp.float32)
    held = []
    for pieces, origins in stages[:-1]:
        held = [
            pl.pallas_call(
                functools.partial(partial_kernel, n, origins, len(held)),
                in_specs=[smem, vmem] + [vmem] * (len(held) + len(pieces)),
                out_specs=vmem,
                out_shape=held_shape,
                input_output_aliases={2: 0} if held else {},
                compiler_params=params,
                cost_estimate=pl.CostEstimate(
                    flops=100 * 1000 * 1000, bytes_accessed=4 * 1024 * 1024, transcendentals=0
                ),
                name="products",
            )(me, left, *held, *pieces)
        ]
    pieces, origins = stages[-1]
    flat, _ = pl.pallas_call(
        functools.partial(correlate_kernel, 1.0 / total_windows, n, origins, sources),
        in_specs=[smem, vmem, vmem] + [vmem] * len(pieces),
        out_specs=[pl.BlockSpec(memory_space=pl.ANY), vmem],
        out_shape=[jax.ShapeDtypeStruct((2 * sources * chans, F), jnp.float32), held_shape],
        scratch_shapes=[
            pltpu.VMEM((2, 2 * sources * chans, HALF), jnp.float32),
            pltpu.SemaphoreType.DMA((2, 2)),
        ],
        input_output_aliases={2: 1},
        compiler_params=params,
        name="correlate",
    )(me, left, *held, *pieces)
    stack = flat.reshape(2, sources, chans, F)
    if lax.axis_size("win") == 1:
        return stack
    return lax.psum_scatter(stack, "win", scatter_dimension=1, tiled=True)


def solution(mesh):
    return jax.shard_map(
        per_device,
        mesh=mesh,
        in_specs=(P("chan", "win", None), P()),
        out_specs=P(None, "win", "chan", None),
        check_vma=False,
    )
```

```python
import functools
import math

import jax
import jax.numpy as jnp
import ml_dtypes
import numpy as np
from jax import lax
from jax.experimental import pallas as pl
from jax.experimental.pallas import tpu as pltpu
from jax.sharding import PartitionSpec as P

F = 256
HALF = 128
F0 = 1
K = 64
GAUGE = 4
LANES = 128
VMEM_LIMIT = 24 * 1024 * 1024


def make_table(length):
    times = np.arange(length, dtype=np.int64)[:, None]
    bins = np.arange(F, dtype=np.int64)[None, :] + F0
    phase = (times * bins % length).astype(np.float32) * np.float32(2.0 * math.pi / length)
    phase = phase.astype(np.float64)
    return np.concatenate([np.cos(phase), -np.sin(phase)], axis=1).astype(ml_dtypes.bfloat16)


def make_band():
    rows = np.arange(F)[:, None]
    cols = np.arange(F)[None, :]
    band = np.abs(rows - cols) <= K
    return band.astype(ml_dtypes.bfloat16), (1.0 / band.sum(axis=0)).astype(np.float32)[None, :]


def whiten_block(cur, upper, table_ref, band_ref, inv_ref, turned_ref, first):
    chans, wins, length = cur.shape
    rows = chans * wins
    diff = (upper.astype(jnp.float32) - cur.astype(jnp.float32)).reshape(rows, length)
    power = jnp.sum(diff * diff, axis=1, keepdims=True) * (1.0 / length)
    normed = (diff * lax.rsqrt(power + 1e-05)).astype(jnp.bfloat16)
    spec = jnp.dot(normed, table_ref[...], preferred_element_type=jnp.float32)
    real = spec[:, :F]
    imag = spec[:, F:]
    magnitude = jnp.sqrt(real * real + imag * imag).astype(jnp.bfloat16)
    smooth = jnp.dot(magnitude, band_ref[...], preferred_element_type=jnp.float32) * inv_ref[...]
    gain = 1.0 / (smooth + 1e-06)
    white_re = (real * gain).astype(jnp.bfloat16).astype(jnp.float32)
    white_im = (imag * gain).astype(jnp.bfloat16).astype(jnp.float32)
    pad = jnp.zeros((LANES - 2 * wins, F), jnp.float32)
    for c in range(chans):
        mine = slice(c * wins, (c + 1) * wins)
        both = jnp.concatenate([white_re[mine], white_im[mine], pad], axis=0)
        turned_ref[pl.ds((first + c) * F, F), :] = both.T


def whiten_kernel(cur_ref, upper_ref, table_ref, band_ref, inv_ref, turned_ref):
    first = pl.program_id(0) * GAUGE
    whiten_block(cur_ref[...], upper_ref[...], table_ref, band_ref, inv_ref, turned_ref, first)


def finish_kernel(
    chans, slots, slot_ref, cur_ref, halo_ref, table_ref, band_ref, inv_ref, _, *refs
):
    turned_ref, rounds, listed = refs[0], refs[1:-1], refs[-1]
    whiten_block(
        cur_ref[...], halo_ref[...], table_ref, band_ref, inv_ref, turned_ref, chans - GAUGE
    )
    dests, _, width = rounds[0].shape
    pairs = HALF // dests // 2
    lane = lax.broadcasted_iota(jnp.int32, (slots, LANES), 1)

    def fill(number, rows_ref):
        for k in range(slots):
            channel = slot_ref[number * slots + k]
            listed[k * F : (k + 1) * F, :] = turned_ref[pl.ds(channel * F, F), :]

        def relayout(dest, carry):
            block = []
            for pair in range(pairs):
                piece = []
                for j in range(2):
                    for half in range(2):
                        at = half * HALF + (dest * pairs + pair) * 2 + j
                        piece.append(listed[pl.ds(at, slots, stride=F), :])
                a, b, c, d = piece
                b = pltpu.roll(b, 96, 1)
                c = pltpu.roll(c, 64, 1)
                d = pltpu.roll(d, 32, 1)
                first = jnp.where(lane < 96, a, b)
                second = jnp.where(lane < 64, b, c)
                third = jnp.where(lane < 32, c, d)
                block.append(jnp.concatenate([first, second, third], axis=1))
            rows_ref[dest] = jnp.concatenate(block, axis=0).astype(jnp.bfloat16)
            return carry

        lax.fori_loop(0, dests, relayout, 0, unroll=4)

    fill(0, rounds[0])
    for number in range(1, len(rounds)):
        pl.when(slot_ref[chans] > number * slots)(
            functools.partial(fill, number, rounds[number])
        )


def left_kernel(chans, depth, turned_ref, left_ref):
    lane = lax.broadcasted_iota(jnp.int32, (chans, LANES), 1)

    def one(g, carry):
        stack = []
        for half in range(2):
            real = turned_ref[pl.ds(half * HALF + g, chans, stride=F), :]
            ahead = pltpu.roll(real, depth // 2, 1)
            back = pltpu.roll(real, LANES - depth // 2, 1)
            stack += [real, jnp.where(lane < depth // 2, -back, ahead)]
        left_ref[g] = jnp.concatenate(stack, axis=0).astype(jnp.bfloat16)
        return carry

    lax.fori_loop(0, HALF, one, 0, unroll=8)


def pick_kernel(slots, base, place_ref, rows_ref, out_ref):
    sources = place_ref.shape[0]
    dests, height, width = rows_ref.shape
    groups, depth, _ = out_ref.shape
    rows = rows_ref[...].reshape(dests * height, width)
    ids = lax.broadcasted_iota(jnp.int32, (sources, dests * height), 1)
    place = place_ref[...] - base
    inside = (place >= 0) & (place < dests * slots)
    spot = place // slots * height + place % slots
    for pair in range(groups // 2):
        hit = inside & (ids == spot + pair * slots)
        onehot = jnp.where(hit, 1.0, 0.0).astype(jnp.bfloat16)
        turned = jnp.dot(onehot, rows, preferred_element_type=jnp.float32).T
        for j in range(2):
            low = turned[(2 * j) * depth : (2 * j + 1) * depth]
            high = turned[(2 * j + 1) * depth : (2 * j + 2) * depth]
            out_ref[pair * 2 + j] = jnp.concatenate([low, high], axis=1).astype(jnp.bfloat16)


def products(n, origins, me_ref, left_ref, pieces, held):
    rows = left_ref.shape[1]
    depth, width = pieces[0].shape[-2:]
    groups = HALF // n
    sources = width // 2
    outs = rows // 2
    me = me_ref[0]
    lane = lax.broadcasted_iota(jnp.int32, (outs, width), 1)
    for piece, runs in zip(pieces, origins):
        place = 0
        for flip, start, count in runs:
            owner = me ^ flip
            for j in range(count):
                g = owner * groups + start + j
                both = jnp.dot(
                    left_ref[g][:, :depth], piece[place], preferred_element_type=jnp.float32
                )
                mine = jnp.where(lane < sources, both[:outs], both[outs:])
                held[pl.ds(g, outs, stride=HALF), :] = mine
                place += 1


def partial_kernel(n, origins, chained, me_ref, left_ref, *refs):
    products(n, origins, me_ref, left_ref, refs[chained:-1], refs[-1])


def correlate_kernel(scale, n, origins, sources, me_ref, left_ref, _, *refs):
    pieces, (out_ref, held, turned_ref, sems) = refs[:-4], refs[-4:]
    products(n, origins, me_ref, left_ref, pieces, held)
    outs = held.shape[0] // HALF
    chans = outs // 2
    size = sources * chans
    copies = []
    for part in range(2):
        for c in range(chans):
            base = (part * chans + c) * HALF
            turned = held[base : base + HALF, :].T * scale
            rows_at = pl.ds(part * size + c, sources, stride=chans)
            for half in range(2):
                turned_ref.at[half][rows_at, :] = turned[half * sources : (half + 1) * sources]
        for half in range(2):
            span = pl.ds(part * size, size)
            copy = pltpu.make_async_copy(
                turned_ref.at[half, span],
                out_ref.at[span, pl.ds(half * HALF, HALF)],
                sems.at[part, half],
            )
            copy.start()
            copies.append(copy)
    for copy in copies:
        copy.wait()


def gather_pieces(own, multiply, after_products):
    n = lax.axis_size("chan")
    planes = n // 8
    groups = own.shape[0]
    half = groups // 2
    core, x, y = 1, 2, 4

    def send(block, flip):
        return lax.ppermute(block, "chan", [(i, i ^ flip) for i in range(n)])

    def join(*blocks):
        return jnp.concatenate(blocks, axis=0)

    def trade(arrays, origins):
        theirs = send(join(*arrays), core)
        runs = [(flip ^ core, start, count) for o in origins for flip, start, count in o]
        return list(arrays) + [theirs], list(origins) + [runs]

    pieces = [own] + [send(own, 8 * k) for k in range(1, planes)]
    ready, ready_from = [], []
    before = None
    for k in range(planes + 1):
        arrays, origins = [], []
        x_out, y_out, x_from, y_from = [], [], [], []
        if k > 0:
            old, x_a, y_b = before
            x_out += [old[half:], y_b]
            y_out += [old[:half], x_a]
            far = 8 * (k - 1)
            x_from += [(far ^ x, half, half), (far ^ x ^ y, half, half)]
            y_from += [(far ^ y, 0, half), (far ^ x ^ y, 0, half)]
        if k < planes:
            x_out.append(pieces[k][:half])
            y_out.append(pieces[k][half:])
            x_from.append((8 * k ^ x, 0, half))
            y_from.append((8 * k ^ y, half, half))
            arrays.append(pieces[k])
            origins.append([(8 * k, 0, groups)])
        x_in = send(join(*x_out), x)
        y_in = send(join(*y_out), y)
        if k < planes:
            before = pieces[k], x_in[-half:], y_in[-half:]
        if k == planes:
            last = trade(after_products(x_in, y_in), [x_from, y_from])
            return ready + last[0], ready_from + last[1]
        arrays, origins = trade(arrays + [x_in, y_in], origins + [x_from, y_from])
        ready, ready_from = ready + arrays, ready_from + origins
        if k == planes - 2:
            multiply(ready, ready_from)
            ready, ready_from = [], []


def plan_slots(source_index, chans, slots):
    n = lax.axis_size("chan")
    channels = jnp.arange(n * chans, dtype=jnp.int32)
    hits = source_index[:, None] == channels[None, :]
    listed = jnp.any(hits, axis=0).reshape(n, chans).astype(jnp.int32)
    below = (jnp.arange(chans)[:, None] < jnp.arange(chans)[None, :]).astype(jnp.int32)
    rank = jnp.sum(listed[:, :, None] * below[None], axis=1)
    device = jnp.arange(n, dtype=jnp.int32)[:, None]
    place = (rank // slots * n + device) * slots + rank % slots
    places = jnp.sum(jnp.where(hits, place.reshape(1, -1), 0), axis=1, keepdims=True)
    most = jnp.max(jnp.sum(listed, axis=1))
    mine = device == lax.axis_index("chan")
    order = jnp.arange(chans, dtype=jnp.int32)
    is_slot = (mine & (listed > 0))[:, :, None] & (rank[:, :, None] == order)
    held = jnp.sum(jnp.where(is_slot, order[None, :, None], 0), axis=(0, 1))
    return jnp.concatenate([held, most[None]]), places, most


def per_device(traces, source_index):
    chans, wins, length = traces.shape
    n = lax.axis_size("chan")
    sources = source_index.shape[0]
    route = [(i + 1, i) for i in range(n - 1)]
    halo = lax.ppermute(traces[:GAUGE], "chan", route)
    table = jnp.asarray(make_table(length))
    band, inv = make_band()
    band, inv = jnp.asarray(band), jnp.asarray(inv)
    steps = chans // GAUGE
    depth = 2 * wins
    row_width = HALF * 2 * depth // n
    block = (GAUGE, wins, length)
    vmem = pl.BlockSpec(memory_space=pltpu.VMEM)
    smem = pl.BlockSpec(memory_space=pltpu.SMEM)
    consts = [vmem] * 3
    params = pltpu.CompilerParams(vmem_limit_bytes=VMEM_LIMIT)
    pairs = HALF // n // 2
    slots = chans // pairs
    slot_list, places, most = plan_slots(source_index, chans, slots)
    turned = jax.ShapeDtypeStruct((chans * F, LANES), jnp.float32)
    some = pl.pallas_call(
        whiten_kernel,
        grid=(steps - 1,),
        in_specs=[
            pl.BlockSpec(block, lambda i: (i, 0, 0)),
            pl.BlockSpec(block, lambda i: (i + 1, 0, 0)),
            *consts,
        ],
        out_specs=vmem,
        out_shape=turned,
        compiler_params=params,
        cost_estimate=pl.CostEstimate(
            flops=2 * (chans - GAUGE) * wins * (length + F // 2) * 2 * F,
            bytes_accessed=8 * 1024 * 1024,
            transcendentals=0,
        ),
        name="whiten",
    )(traces, traces, table, band, inv)
    rows_shape = jax.ShapeDtypeStruct((n, chans, row_width // pairs), jnp.bfloat16)
    spectra, *rounds = pl.pallas_call(
        functools.partial(finish_kernel, chans, slots),
        grid=(1,),
        in_specs=[
            smem,
            pl.BlockSpec(block, lambda i: (steps - 1, 0, 0)),
            vmem,
            *consts,
            vmem,
        ],
        out_specs=[vmem] * (1 + pairs),
        out_shape=[turned] + [rows_shape] * pairs,
        scratch_shapes=[pltpu.VMEM((slots * F, LANES), jnp.float32)],
        input_output_aliases={6: 0},
        compiler_params=params,
        name="finish",
    )(slot_list, traces, halo, table, band, inv, some)

    def exchange(number, rows, *beside):
        rows = lax.all_to_all(rows, "chan", 0, 0, tiled=True)
        rows = lax.optimization_barrier((rows, *beside))[0]
        return pl.pallas_call(
            functools.partial(pick_kernel, slots, number * n * slots),
            out_shape=jax.ShapeDtypeStruct((HALF // n, depth, 2 * sources), jnp.bfloat16),
            compiler_params=params,
            name="pick",
        )(places, rows)

    left = pl.pallas_call(
        functools.partial(left_kernel, chans, depth),
        in_specs=[vmem],
        out_specs=vmem,
        out_shape=jax.ShapeDtypeStruct((HALF, 4 * chans, LANES), jnp.bfloat16),
        compiler_params=params,
        cost_estimate=pl.CostEstimate(
            flops=10 * 1000 * 1000, bytes_accessed=8 * 1024 * 1024, transcendentals=0
        ),
        name="left",
    )(spectra)
    picked = exchange(0, rounds[0], left)
    for number in range(1, pairs):
        picked = lax.cond(
            most > number * slots,
            lambda p, r, number=number: p + exchange(number, r),
            lambda p, r: p,
            picked,
            rounds[number],
        )
    me = lax.axis_index("chan").astype(jnp.int32).reshape(1)
    total_windows = wins * lax.axis_size("win")
    held_shape = jax.ShapeDtypeStruct((2 * chans * HALF, LANES), jnp.float32)
    held = []

    def multiply(pieces, origins):
        held[:] = [
            pl.pallas_call(
                functools.partial(partial_kernel, n, origins, len(held)),
                in_specs=[smem, vmem] + [vmem] * (len(held) + len(pieces)),
                out_specs=vmem,
                out_shape=held_shape,
                input_output_aliases={2: 0} if held else {},
                compiler_params=params,
                cost_estimate=pl.CostEstimate(
                    flops=100 * 1000 * 1000, bytes_accessed=4 * 1024 * 1024, transcendentals=0
                ),
                name="products",
            )(me, left, *held, *pieces)
        ]

    def after_products(*arrays):
        *arrays, held[0] = lax.optimization_barrier((*arrays, held[0]))
        return arrays

    pieces, origins = gather_pieces(picked, multiply, after_products)
    flat, _ = pl.pallas_call(
        functools.partial(correlate_kernel, 1.0 / total_windows, n, origins, sources),
        in_specs=[smem, vmem, vmem] + [vmem] * len(pieces),
        out_specs=[pl.BlockSpec(memory_space=pl.ANY), vmem],
        out_shape=[jax.ShapeDtypeStruct((2 * sources * chans, F), jnp.float32), held_shape],
        scratch_shapes=[
            pltpu.VMEM((2, 2 * sources * chans, HALF), jnp.float32),
            pltpu.SemaphoreType.DMA((2, 2)),
        ],
        input_output_aliases={2: 1},
        compiler_params=params,
        name="correlate",
    )(me, left, *held, *pieces)
    stack = flat.reshape(2, sources, chans, F)
    if lax.axis_size("win") == 1:
        return stack
    return lax.psum_scatter(stack, "win", scatter_dimension=1, tiled=True)


def solution(mesh):
    return jax.shard_map(
        per_device,
        mesh=mesh,
        in_specs=(P("chan", "win", None), P()),
        out_specs=P(None, "win", "chan", None),
        check_vma=False,
    )
```

```python
import functools
import math

import jax
import jax.numpy as jnp
import ml_dtypes
import numpy as np
from jax import lax
from jax.experimental import pallas as pl
from jax.experimental.pallas import tpu as pltpu
from jax.sharding import PartitionSpec as P

F = 256
HALF = 128
F0 = 1
K = 64
GAUGE = 4
LANES = 128
VMEM_LIMIT = 24 * 1024 * 1024


def make_table(length):
    times = np.arange(length, dtype=np.int64)[:, None]
    bins = np.arange(F, dtype=np.int64)[None, :] + F0
    phase = (times * bins % length).astype(np.float32) * np.float32(2.0 * math.pi / length)
    phase = phase.astype(np.float64)
    return np.concatenate([np.cos(phase), -np.sin(phase)], axis=1).astype(ml_dtypes.bfloat16)


def make_band():
    rows = np.arange(F)[:, None]
    cols = np.arange(F)[None, :]
    band = np.abs(rows - cols) <= K
    return band.astype(ml_dtypes.bfloat16), (1.0 / band.sum(axis=0)).astype(np.float32)[None, :]


def whiten_block(cur, upper, table_ref, band_ref, inv_ref, turned_ref, first):
    chans, wins, length = cur.shape
    rows = chans * wins
    diff = (upper.astype(jnp.float32) - cur.astype(jnp.float32)).reshape(rows, length)
    power = jnp.sum(diff * diff, axis=1, keepdims=True) * (1.0 / length)
    normed = (diff * lax.rsqrt(power + 1e-05)).astype(jnp.bfloat16)
    spec = jnp.dot(normed, table_ref[...], preferred_element_type=jnp.float32)
    real = spec[:, :F]
    imag = spec[:, F:]
    magnitude = jnp.sqrt(real * real + imag * imag).astype(jnp.bfloat16)
    smooth = jnp.dot(magnitude, band_ref[...], preferred_element_type=jnp.float32) * inv_ref[...]
    gain = 1.0 / (smooth + 1e-06)
    white_re = (real * gain).astype(jnp.bfloat16).astype(jnp.float32)
    white_im = (imag * gain).astype(jnp.bfloat16).astype(jnp.float32)
    pad = jnp.zeros((LANES - 2 * wins, F), jnp.float32)
    for c in range(chans):
        mine = slice(c * wins, (c + 1) * wins)
        both = jnp.concatenate([white_re[mine], white_im[mine], pad], axis=0)
        turned_ref[pl.ds((first + c) * F, F), :] = both.T


def whiten_kernel(cur_ref, upper_ref, table_ref, band_ref, inv_ref, turned_ref):
    first = pl.program_id(0) * GAUGE
    whiten_block(cur_ref[...], upper_ref[...], table_ref, band_ref, inv_ref, turned_ref, first)


def finish_kernel(
    chans, slots, slot_ref, cur_ref, halo_ref, table_ref, band_ref, inv_ref, _, *refs
):
    turned_ref, rounds, listed = refs[0], refs[1:-1], refs[-1]
    whiten_block(
        cur_ref[...], halo_ref[...], table_ref, band_ref, inv_ref, turned_ref, chans - GAUGE
    )
    dests, _, width = rounds[0].shape
    pairs = HALF // dests // 2
    lane = lax.broadcasted_iota(jnp.int32, (slots, LANES), 1)

    def fill(number, rows_ref):
        for k in range(slots):
            channel = slot_ref[number * slots + k]
            listed[k * F : (k + 1) * F, :] = turned_ref[pl.ds(channel * F, F), :]

        def relayout(dest, carry):
            block = []
            for pair in range(pairs):
                piece = []
                for j in range(2):
                    for half in range(2):
                        at = half * HALF + (dest * pairs + pair) * 2 + j
                        piece.append(listed[pl.ds(at, slots, stride=F), :])
                a, b, c, d = piece
                b = pltpu.roll(b, 96, 1)
                c = pltpu.roll(c, 64, 1)
                d = pltpu.roll(d, 32, 1)
                first = jnp.where(lane < 96, a, b)
                second = jnp.where(lane < 64, b, c)
                third = jnp.where(lane < 32, c, d)
                block.append(jnp.concatenate([first, second, third], axis=1))
            rows_ref[dest] = jnp.concatenate(block, axis=0).astype(jnp.bfloat16)
            return carry

        lax.fori_loop(0, dests, relayout, 0, unroll=4)

    fill(0, rounds[0])
    for number in range(1, len(rounds)):
        pl.when(slot_ref[chans] > number * slots)(
            functools.partial(fill, number, rounds[number])
        )


def left_kernel(chans, depth, turned_ref, left_ref):
    lane = lax.broadcasted_iota(jnp.int32, (chans, LANES), 1)

    def one(g, carry):
        stack = []
        for half in range(2):
            real = turned_ref[pl.ds(half * HALF + g, chans, stride=F), :]
            ahead = pltpu.roll(real, depth // 2, 1)
            back = pltpu.roll(real, LANES - depth // 2, 1)
            stack += [real, jnp.where(lane < depth // 2, -back, ahead)]
        left_ref[g] = jnp.concatenate(stack, axis=0).astype(jnp.bfloat16)
        return carry

    lax.fori_loop(0, HALF, one, 0, unroll=8)


def pick_kernel(slots, base, place_ref, rows_ref, out_ref):
    sources = place_ref.shape[0]
    dests, height, width = rows_ref.shape
    groups, depth, _ = out_ref.shape
    rows = rows_ref[...].reshape(dests * height, width)
    ids = lax.broadcasted_iota(jnp.int32, (sources, dests * height), 1)
    place = place_ref[...] - base
    inside = (place >= 0) & (place < dests * slots)
    spot = place // slots * height + place % slots
    for pair in range(groups // 2):
        hit = inside & (ids == spot + pair * slots)
        onehot = jnp.where(hit, 1.0, 0.0).astype(jnp.bfloat16)
        turned = jnp.dot(onehot, rows, preferred_element_type=jnp.float32).T
        for j in range(2):
            low = turned[(2 * j) * depth : (2 * j + 1) * depth]
            high = turned[(2 * j + 1) * depth : (2 * j + 2) * depth]
            out_ref[pair * 2 + j] = jnp.concatenate([low, high], axis=1).astype(jnp.bfloat16)


def products(n, origins, me_ref, left_ref, pieces, held):
    rows = left_ref.shape[1]
    depth, width = pieces[0].shape[-2:]
    groups = HALF // n
    sources = width // 2
    outs = rows // 2
    me = me_ref[0]
    lane = lax.broadcasted_iota(jnp.int32, (outs, width), 1)
    for piece, runs in zip(pieces, origins):
        place = 0
        for flip, start, count in runs:
            owner = me ^ flip
            for j in range(count):
                g = owner * groups + start + j
                both = jnp.dot(
                    left_ref[g][:, :depth], piece[place], preferred_element_type=jnp.float32
                )
                mine = jnp.where(lane < sources, both[:outs], both[outs:])
                held[pl.ds(g, outs, stride=HALF), :] = mine
                place += 1


def partial_kernel(n, origins, me_ref, left_ref, *refs):
    products(n, origins, me_ref, left_ref, refs[:-1], refs[-1])


def correlate_kernel(scale, n, origins, sources, me_ref, left_ref, _, *refs):
    pieces, (out_ref, held, turned_ref, sems) = refs[:-4], refs[-4:]
    products(n, origins, me_ref, left_ref, pieces, held)
    outs = held.shape[0] // HALF
    chans = outs // 2
    size = sources * chans
    copies = []
    for part in range(2):
        for c in range(chans):
            base = (part * chans + c) * HALF
            turned = held[base : base + HALF, :].T * scale
            rows_at = pl.ds(part * size + c, sources, stride=chans)
            for half in range(2):
                turned_ref.at[half][rows_at, :] = turned[half * sources : (half + 1) * sources]
        for half in range(2):
            span = pl.ds(part * size, size)
            copy = pltpu.make_async_copy(
                turned_ref.at[half, span],
                out_ref.at[span, pl.ds(half * HALF, HALF)],
                sems.at[part, half],
            )
            copy.start()
            copies.append(copy)
    for copy in copies:
        copy.wait()


def gather_pieces(own, multiply, tie_left, tie_products):
    n = lax.axis_size("chan")
    planes = n // 8
    groups = own.shape[0]
    most = max(1, groups * 3 // 4)
    rest = groups - most
    core = 1
    square = (2, 4, 6)
    column = [8 * k for k in range(1, planes)]

    def send(block, flip):
        return lax.ppermute(block, "chan", [(i, i ^ flip) for i in range(n)])

    def join(*blocks):
        return jnp.concatenate(blocks, axis=0)

    def trade(arrays, origins):
        theirs = send(join(*arrays), core)
        runs = [(flip ^ core, start, count) for o in origins for flip, start, count in o]
        return list(arrays) + [theirs], list(origins) + [runs]

    cols = [send(own[:most], flip) for flip in column]
    near = [send(own, flip) for flip in square]
    *tied, left = tie_left(*cols, *near)
    cols, near = tied[: len(cols)], tied[len(cols) :]
    far_block = join(*cols)
    rest_block = join(own[most:], *[p[most:] for p in near])
    far = [send(far_block, flip) for flip in square]
    planes_in = [send(rest_block, flip) for flip in column]
    near_from = [[(0, 0, groups)]] + [[(flip, 0, groups)] for flip in square]
    far_from = [(flip, 0, most) for flip in column]
    first = trade([own, *near, far_block], near_from + [far_from])
    multiply(left, *first)
    *tied, _ = tie_products(*far, *planes_in)
    far, planes_in = tied[: len(far)], tied[len(far) :]
    arrays, origins = [], []
    for block, flip in zip(far, square):
        more = trade([block], [[(f ^ flip, start, count) for f, start, count in far_from]])
        arrays, origins = arrays + more[0], origins + more[1]
    runs = [[(flip ^ m, most, rest) for m in (0, *square)] for flip in column]
    more = trade(planes_in, runs)
    return left, arrays + more[0], origins + more[1]


def plan_slots(source_index, chans, slots):
    n = lax.axis_size("chan")
    channels = jnp.arange(n * chans, dtype=jnp.int32)
    hits = source_index[:, None] == channels[None, :]
    listed = jnp.any(hits, axis=0).reshape(n, chans).astype(jnp.int32)
    below = (jnp.arange(chans)[:, None] < jnp.arange(chans)[None, :]).astype(jnp.int32)
    rank = jnp.sum(listed[:, :, None] * below[None], axis=1)
    device = jnp.arange(n, dtype=jnp.int32)[:, None]
    place = (rank // slots * n + device) * slots + rank % slots
    places = jnp.sum(jnp.where(hits, place.reshape(1, -1), 0), axis=1, keepdims=True)
    most = jnp.max(jnp.sum(listed, axis=1))
    mine = device == lax.axis_index("chan")
    order = jnp.arange(chans, dtype=jnp.int32)
    is_slot = (mine & (listed > 0))[:, :, None] & (rank[:, :, None] == order)
    held = jnp.sum(jnp.where(is_slot, order[None, :, None], 0), axis=(0, 1))
    return jnp.concatenate([held, most[None]]), places, most


def per_device(traces, source_index):
    chans, wins, length = traces.shape
    n = lax.axis_size("chan")
    sources = source_index.shape[0]
    route = [(i + 1, i) for i in range(n - 1)]
    halo = lax.ppermute(traces[:GAUGE], "chan", route)
    table = jnp.asarray(make_table(length))
    band, inv = make_band()
    band, inv = jnp.asarray(band), jnp.asarray(inv)
    steps = chans // GAUGE
    depth = 2 * wins
    row_width = HALF * 2 * depth // n
    block = (GAUGE, wins, length)
    vmem = pl.BlockSpec(memory_space=pltpu.VMEM)
    smem = pl.BlockSpec(memory_space=pltpu.SMEM)
    consts = [vmem] * 3
    params = pltpu.CompilerParams(vmem_limit_bytes=VMEM_LIMIT)
    pairs = HALF // n // 2
    slots = chans // pairs
    slot_list, places, most = plan_slots(source_index, chans, slots)
    turned = jax.ShapeDtypeStruct((chans * F, LANES), jnp.float32)
    some = pl.pallas_call(
        whiten_kernel,
        grid=(steps - 1,),
        in_specs=[
            pl.BlockSpec(block, lambda i: (i, 0, 0)),
            pl.BlockSpec(block, lambda i: (i + 1, 0, 0)),
            *consts,
        ],
        out_specs=vmem,
        out_shape=turned,
        compiler_params=params,
        cost_estimate=pl.CostEstimate(
            flops=2 * (chans - GAUGE) * wins * (length + F // 2) * 2 * F,
            bytes_accessed=8 * 1024 * 1024,
            transcendentals=0,
        ),
        name="whiten",
    )(traces, traces, table, band, inv)
    rows_shape = jax.ShapeDtypeStruct((n, chans, row_width // pairs), jnp.bfloat16)
    spectra, *rounds = pl.pallas_call(
        functools.partial(finish_kernel, chans, slots),
        grid=(1,),
        in_specs=[
            smem,
            pl.BlockSpec(block, lambda i: (steps - 1, 0, 0)),
            vmem,
            *consts,
            vmem,
        ],
        out_specs=[vmem] * (1 + pairs),
        out_shape=[turned] + [rows_shape] * pairs,
        scratch_shapes=[pltpu.VMEM((slots * F, LANES), jnp.float32)],
        input_output_aliases={6: 0},
        compiler_params=params,
        name="finish",
    )(slot_list, traces, halo, table, band, inv, some)

    def exchange(number, rows):
        rows = lax.all_to_all(rows, "chan", 0, 0, tiled=True)
        return pl.pallas_call(
            functools.partial(pick_kernel, slots, number * n * slots),
            out_shape=jax.ShapeDtypeStruct((HALF // n, depth, 2 * sources), jnp.bfloat16),
            compiler_params=params,
            name="pick",
        )(places, rows)

    left = pl.pallas_call(
        functools.partial(left_kernel, chans, depth),
        in_specs=[vmem],
        out_specs=vmem,
        out_shape=jax.ShapeDtypeStruct((HALF, 4 * chans, LANES), jnp.bfloat16),
        compiler_params=params,
        cost_estimate=pl.CostEstimate(
            flops=10 * 1000 * 1000, bytes_accessed=8 * 1024 * 1024, transcendentals=0
        ),
        name="left",
    )(spectra)
    picked = exchange(0, rounds[0])
    for number in range(1, pairs):
        picked = lax.cond(
            most > number * slots,
            lambda p, r, number=number: p + exchange(number, r),
            lambda p, r: p,
            picked,
            rounds[number],
        )
    me = lax.axis_index("chan").astype(jnp.int32).reshape(1)
    total_windows = wins * lax.axis_size("win")
    held_shape = jax.ShapeDtypeStruct((2 * chans * HALF, LANES), jnp.float32)
    held = []

    def multiply(left, pieces, origins):
        held.append(
            pl.pallas_call(
                functools.partial(partial_kernel, n, origins),
                in_specs=[smem, vmem] + [vmem] * len(pieces),
                out_specs=vmem,
                out_shape=held_shape,
                compiler_params=params,
                cost_estimate=pl.CostEstimate(
                    flops=100 * 1000 * 1000, bytes_accessed=4 * 1024 * 1024, transcendentals=0
                ),
                name="products",
            )(me, left, *pieces)
        )

    def tie_left(*arrays):
        return lax.optimization_barrier((*arrays, left))

    def tie_products(*arrays):
        *arrays, held[0] = lax.optimization_barrier((*arrays, held[0]))
        return (*arrays, held[0])

    tied, pieces, origins = gather_pieces(picked, multiply, tie_left, tie_products)
    flat, _ = pl.pallas_call(
        functools.partial(correlate_kernel, 1.0 / total_windows, n, origins, sources),
        in_specs=[smem, vmem, vmem] + [vmem] * len(pieces),
        out_specs=[pl.BlockSpec(memory_space=pl.ANY), vmem],
        out_shape=[jax.ShapeDtypeStruct((2 * sources * chans, F), jnp.float32), held_shape],
        scratch_shapes=[
            pltpu.VMEM((2, 2 * sources * chans, HALF), jnp.float32),
            pltpu.SemaphoreType.DMA((2, 2)),
        ],
        input_output_aliases={2: 1},
        compiler_params=params,
        name="correlate",
    )(me, tied, *held, *pieces)
    stack = flat.reshape(2, sources, chans, F)
    if lax.axis_size("win") == 1:
        return stack
    return lax.psum_scatter(stack, "win", scatter_dimension=1, tiled=True)


def solution(mesh):
    return jax.shard_map(
        per_device,
        mesh=mesh,
        in_specs=(P("chan", "win", None), P()),
        out_specs=P(None, "win", "chan", None),
        check_vma=False,
    )
```

```python
import functools
import math

import jax
import jax.numpy as jnp
import ml_dtypes
import numpy as np
from jax import lax
from jax.experimental import pallas as pl
from jax.experimental.pallas import tpu as pltpu
from jax.sharding import PartitionSpec as P

F = 256
HALF = 128
F0 = 1
K = 64
GAUGE = 4
LANES = 128
VMEM_LIMIT = 24 * 1024 * 1024


def make_table(length):
    times = np.arange(length, dtype=np.int64)[:, None]
    bins = np.arange(F, dtype=np.int64)[None, :] + F0
    phase = (times * bins % length).astype(np.float32) * np.float32(2.0 * math.pi / length)
    phase = phase.astype(np.float64)
    return np.concatenate([np.cos(phase), -np.sin(phase)], axis=1).astype(ml_dtypes.bfloat16)


def make_band():
    rows = np.arange(F)[:, None]
    cols = np.arange(F)[None, :]
    band = np.abs(rows - cols) <= K
    return band.astype(ml_dtypes.bfloat16), (1.0 / band.sum(axis=0)).astype(np.float32)[None, :]


def whiten_block(cur, upper, table_ref, band_ref, inv_ref, turned_ref, first):
    chans, wins, length = cur.shape
    rows = chans * wins
    diff = (upper.astype(jnp.float32) - cur.astype(jnp.float32)).reshape(rows, length)
    power = jnp.sum(diff * diff, axis=1, keepdims=True) * (1.0 / length)
    normed = (diff * lax.rsqrt(power + 1e-05)).astype(jnp.bfloat16)
    spec = jnp.dot(normed, table_ref[...], preferred_element_type=jnp.float32)
    real = spec[:, :F]
    imag = spec[:, F:]
    magnitude = jnp.sqrt(real * real + imag * imag).astype(jnp.bfloat16)
    smooth = jnp.dot(magnitude, band_ref[...], preferred_element_type=jnp.float32) * inv_ref[...]
    gain = 1.0 / (smooth + 1e-06)
    white_re = (real * gain).astype(jnp.bfloat16).astype(jnp.float32)
    white_im = (imag * gain).astype(jnp.bfloat16).astype(jnp.float32)
    pad = jnp.zeros((LANES - 2 * wins, F), jnp.float32)
    for c in range(chans):
        mine = slice(c * wins, (c + 1) * wins)
        both = jnp.concatenate([white_re[mine], white_im[mine], pad], axis=0)
        turned_ref[pl.ds((first + c) * F, F), :] = both.T


def whiten_kernel(cur_ref, upper_ref, table_ref, band_ref, inv_ref, turned_ref):
    first = pl.program_id(0) * GAUGE
    whiten_block(cur_ref[...], upper_ref[...], table_ref, band_ref, inv_ref, turned_ref, first)


def finish_kernel(
    chans, slots, slot_ref, cur_ref, halo_ref, table_ref, band_ref, inv_ref, _, *refs
):
    turned_ref, rounds, listed = refs[0], refs[1:-1], refs[-1]
    whiten_block(
        cur_ref[...], halo_ref[...], table_ref, band_ref, inv_ref, turned_ref, chans - GAUGE
    )
    dests, _, width = rounds[0].shape
    pairs = HALF // dests // 2
    lane = lax.broadcasted_iota(jnp.int32, (slots, LANES), 1)

    def fill(number, rows_ref):
        for k in range(slots):
            channel = slot_ref[number * slots + k]
            listed[k * F : (k + 1) * F, :] = turned_ref[pl.ds(channel * F, F), :]

        def relayout(dest, carry):
            block = []
            for pair in range(pairs):
                piece = []
                for j in range(2):
                    for half in range(2):
                        at = half * HALF + (dest * pairs + pair) * 2 + j
                        piece.append(listed[pl.ds(at, slots, stride=F), :])
                a, b, c, d = piece
                b = pltpu.roll(b, 96, 1)
                c = pltpu.roll(c, 64, 1)
                d = pltpu.roll(d, 32, 1)
                first = jnp.where(lane < 96, a, b)
                second = jnp.where(lane < 64, b, c)
                third = jnp.where(lane < 32, c, d)
                block.append(jnp.concatenate([first, second, third], axis=1))
            rows_ref[dest] = jnp.concatenate(block, axis=0).astype(jnp.bfloat16)
            return carry

        lax.fori_loop(0, dests, relayout, 0, unroll=4)

    fill(0, rounds[0])
    for number in range(1, len(rounds)):
        pl.when(slot_ref[chans] > number * slots)(
            functools.partial(fill, number, rounds[number])
        )


def left_kernel(chans, depth, turned_ref, left_ref):
    lane = lax.broadcasted_iota(jnp.int32, (chans, LANES), 1)

    def one(g, carry):
        stack = []
        for half in range(2):
            real = turned_ref[pl.ds(half * HALF + g, chans, stride=F), :]
            ahead = pltpu.roll(real, depth // 2, 1)
            back = pltpu.roll(real, LANES - depth // 2, 1)
            stack += [real, jnp.where(lane < depth // 2, -back, ahead)]
        left_ref[g] = jnp.concatenate(stack, axis=0).astype(jnp.bfloat16)
        return carry

    lax.fori_loop(0, HALF, one, 0, unroll=8)


def pick_kernel(slots, base, place_ref, rows_ref, out_ref):
    sources = place_ref.shape[0]
    dests, height, width = rows_ref.shape
    groups, depth, _ = out_ref.shape
    rows = rows_ref[...].reshape(dests * height, width)
    ids = lax.broadcasted_iota(jnp.int32, (sources, dests * height), 1)
    place = place_ref[...] - base
    inside = (place >= 0) & (place < dests * slots)
    spot = place // slots * height + place % slots
    for pair in range(groups // 2):
        hit = inside & (ids == spot + pair * slots)
        onehot = jnp.where(hit, 1.0, 0.0).astype(jnp.bfloat16)
        turned = jnp.dot(onehot, rows, preferred_element_type=jnp.float32).T
        for j in range(2):
            low = turned[(2 * j) * depth : (2 * j + 1) * depth]
            high = turned[(2 * j + 1) * depth : (2 * j + 2) * depth]
            out_ref[pair * 2 + j] = jnp.concatenate([low, high], axis=1).astype(jnp.bfloat16)


def products(n, origins, me_ref, left_ref, pieces, held):
    rows = left_ref.shape[1]
    depth, width = pieces[0].shape[-2:]
    groups = HALF // n
    sources = width // 2
    outs = rows // 2
    me = me_ref[0]
    lane = lax.broadcasted_iota(jnp.int32, (outs, width), 1)
    for piece, runs in zip(pieces, origins):
        place = 0
        for owner_of, start, count in runs:
            owner = owner_of(me)
            for j in range(count):
                g = owner * groups + start + j
                both = jnp.dot(
                    left_ref[g][:, :depth], piece[place], preferred_element_type=jnp.float32
                )
                mine = jnp.where(lane < sources, both[:outs], both[outs:])
                held[pl.ds(g, outs, stride=HALF), :] = mine
                place += 1


def partial_kernel(n, origins, me_ref, left_ref, *refs):
    products(n, origins, me_ref, left_ref, refs[:-1], refs[-1])


def correlate_kernel(scale, n, origins, sources, me_ref, left_ref, _, *refs):
    pieces, (out_ref, held, turned_ref, sems) = refs[:-4], refs[-4:]
    products(n, origins, me_ref, left_ref, pieces, held)
    outs = held.shape[0] // HALF
    chans = outs // 2
    size = sources * chans
    copies = []
    for part in range(2):
        for c in range(chans):
            base = (part * chans + c) * HALF
            turned = held[base : base + HALF, :].T * scale
            rows_at = pl.ds(part * size + c, sources, stride=chans)
            for half in range(2):
                turned_ref.at[half][rows_at, :] = turned[half * sources : (half + 1) * sources]
        for half in range(2):
            span = pl.ds(part * size, size)
            copy = pltpu.make_async_copy(
                turned_ref.at[half, span],
                out_ref.at[span, pl.ds(half * HALF, HALF)],
                sems.at[part, half],
            )
            copy.start()
            copies.append(copy)
    for copy in copies:
        copy.wait()


def gather_pieces(own, multiply, tie_left, tie_products):
    n = lax.axis_size("chan")
    planes = n // 8
    groups = own.shape[0]
    most = max(1, groups * 3 // 4)
    rest = groups - most
    core = 1
    square = (2, 4, 6)
    columns = [[q + 8 * z for z in range(planes)] for q in range(8)]

    def send(block, flip):
        return lax.ppermute(block, "chan", [(i, i ^ flip) for i in range(n)])

    def join(*blocks):
        return jnp.concatenate(blocks, axis=0)

    def column(block):
        copies = jnp.broadcast_to(block[None], (planes, *block.shape))
        return lax.all_to_all(copies, "chan", 0, 0, axis_index_groups=columns, tiled=True)

    def trade(arrays, origins):
        theirs = send(join(*arrays), core)
        runs = [(lambda me, f=f: f(me ^ core), start, count) for o in origins for f, start, count in o]
        return list(arrays) + [theirs], list(origins) + [runs]

    def ahead(k, flip=0):
        return lambda me: lax.rem(me + 8 * k, n) ^ flip

    def plane_of(z, flip):
        return lambda me: ((me & 7) ^ flip) + 8 * z

    cols = column(own[:most])
    near = [send(own, flip) for flip in square]
    cols, *near, left = tie_left(cols, *near)
    plane = lax.axis_index("chan") // 8
    far_block = lax.dynamic_slice_in_dim(join(cols, cols), plane + 1, planes - 1, axis=0)
    far_block = far_block.reshape((planes - 1) * most, *own.shape[1:])
    rest_block = join(own[most:], *[p[most:] for p in near])
    far = [send(far_block, flip) for flip in square]
    planes_in = column(rest_block).reshape(planes * 4 * rest, *own.shape[1:])
    near_from = [[(ahead(0, flip), 0, groups)] for flip in (0, *square)]
    first = trade([own, *near], near_from)
    multiply(left, *first)
    *far, planes_in, _ = tie_products(*far, planes_in)
    far_from = [
        [(ahead(k, flip), 0, most) for k in range(1, planes)] for flip in (0, *square)
    ]
    arrays, origins = [], []
    for block, runs in zip([far_block, *far], far_from):
        more = trade([block], [runs])
        arrays, origins = arrays + more[0], origins + more[1]
    runs = [(plane_of(z, flip), most, rest) for z in range(planes) for flip in (0, *square)]
    more = trade([planes_in], [runs])
    return left, arrays + more[0], origins + more[1]


def plan_slots(source_index, chans, slots):
    n = lax.axis_size("chan")
    channels = jnp.arange(n * chans, dtype=jnp.int32)
    hits = source_index[:, None] == channels[None, :]
    listed = jnp.any(hits, axis=0).reshape(n, chans).astype(jnp.int32)
    below = (jnp.arange(chans)[:, None] < jnp.arange(chans)[None, :]).astype(jnp.int32)
    rank = jnp.sum(listed[:, :, None] * below[None], axis=1)
    device = jnp.arange(n, dtype=jnp.int32)[:, None]
    place = (rank // slots * n + device) * slots + rank % slots
    places = jnp.sum(jnp.where(hits, place.reshape(1, -1), 0), axis=1, keepdims=True)
    most = jnp.max(jnp.sum(listed, axis=1))
    mine = device == lax.axis_index("chan")
    order = jnp.arange(chans, dtype=jnp.int32)
    is_slot = (mine & (listed > 0))[:, :, None] & (rank[:, :, None] == order)
    held = jnp.sum(jnp.where(is_slot, order[None, :, None], 0), axis=(0, 1))
    return jnp.concatenate([held, most[None]]), places, most


def per_device(traces, source_index):
    chans, wins, length = traces.shape
    n = lax.axis_size("chan")
    sources = source_index.shape[0]
    route = [(i + 1, i) for i in range(n - 1)]
    halo = lax.ppermute(traces[:GAUGE], "chan", route)
    table = jnp.asarray(make_table(length))
    band, inv = make_band()
    band, inv = jnp.asarray(band), jnp.asarray(inv)
    steps = chans // GAUGE
    depth = 2 * wins
    row_width = HALF * 2 * depth // n
    block = (GAUGE, wins, length)
    vmem = pl.BlockSpec(memory_space=pltpu.VMEM)
    smem = pl.BlockSpec(memory_space=pltpu.SMEM)
    consts = [vmem] * 3
    params = pltpu.CompilerParams(vmem_limit_bytes=VMEM_LIMIT)
    pairs = HALF // n // 2
    slots = chans // pairs
    slot_list, places, most = plan_slots(source_index, chans, slots)
    turned = jax.ShapeDtypeStruct((chans * F, LANES), jnp.float32)
    some = pl.pallas_call(
        whiten_kernel,
        grid=(steps - 1,),
        in_specs=[
            pl.BlockSpec(block, lambda i: (i, 0, 0)),
            pl.BlockSpec(block, lambda i: (i + 1, 0, 0)),
            *consts,
        ],
        out_specs=vmem,
        out_shape=turned,
        compiler_params=params,
        cost_estimate=pl.CostEstimate(
            flops=2 * (chans - GAUGE) * wins * (length + F // 2) * 2 * F,
            bytes_accessed=8 * 1024 * 1024,
            transcendentals=0,
        ),
        name="whiten",
    )(traces, traces, table, band, inv)
    rows_shape = jax.ShapeDtypeStruct((n, chans, row_width // pairs), jnp.bfloat16)
    spectra, *rounds = pl.pallas_call(
        functools.partial(finish_kernel, chans, slots),
        grid=(1,),
        in_specs=[
            smem,
            pl.BlockSpec(block, lambda i: (steps - 1, 0, 0)),
            vmem,
            *consts,
            vmem,
        ],
        out_specs=[vmem] * (1 + pairs),
        out_shape=[turned] + [rows_shape] * pairs,
        scratch_shapes=[pltpu.VMEM((slots * F, LANES), jnp.float32)],
        input_output_aliases={6: 0},
        compiler_params=params,
        name="finish",
    )(slot_list, traces, halo, table, band, inv, some)

    def exchange(number, rows):
        rows = lax.all_to_all(rows, "chan", 0, 0, tiled=True)
        return pl.pallas_call(
            functools.partial(pick_kernel, slots, number * n * slots),
            out_shape=jax.ShapeDtypeStruct((HALF // n, depth, 2 * sources), jnp.bfloat16),
            compiler_params=params,
            name="pick",
        )(places, rows)

    left = pl.pallas_call(
        functools.partial(left_kernel, chans, depth),
        in_specs=[vmem],
        out_specs=vmem,
        out_shape=jax.ShapeDtypeStruct((HALF, 4 * chans, LANES), jnp.bfloat16),
        compiler_params=params,
        cost_estimate=pl.CostEstimate(
            flops=10 * 1000 * 1000, bytes_accessed=8 * 1024 * 1024, transcendentals=0
        ),
        name="left",
    )(spectra)
    picked = exchange(0, rounds[0])
    for number in range(1, pairs):
        picked = lax.cond(
            most > number * slots,
            lambda p, r, number=number: p + exchange(number, r),
            lambda p, r: p,
            picked,
            rounds[number],
        )
    me = lax.axis_index("chan").astype(jnp.int32).reshape(1)
    total_windows = wins * lax.axis_size("win")
    held_shape = jax.ShapeDtypeStruct((2 * chans * HALF, LANES), jnp.float32)
    held = []

    def multiply(left, pieces, origins):
        held.append(
            pl.pallas_call(
                functools.partial(partial_kernel, n, origins),
                in_specs=[smem, vmem] + [vmem] * len(pieces),
                out_specs=vmem,
                out_shape=held_shape,
                compiler_params=params,
                cost_estimate=pl.CostEstimate(
                    flops=100 * 1000 * 1000, bytes_accessed=4 * 1024 * 1024, transcendentals=0
                ),
                name="products",
            )(me, left, *pieces)
        )

    def tie_left(*arrays):
        return lax.optimization_barrier((*arrays, left))

    def tie_products(*arrays):
        *arrays, held[0] = lax.optimization_barrier((*arrays, held[0]))
        return (*arrays, held[0])

    tied, pieces, origins = gather_pieces(picked, multiply, tie_left, tie_products)
    flat, _ = pl.pallas_call(
        functools.partial(correlate_kernel, 1.0 / total_windows, n, origins, sources),
        in_specs=[smem, vmem, vmem] + [vmem] * len(pieces),
        out_specs=[pl.BlockSpec(memory_space=pl.ANY), vmem],
        out_shape=[jax.ShapeDtypeStruct((2 * sources * chans, F), jnp.float32), held_shape],
        scratch_shapes=[
            pltpu.VMEM((2, 2 * sources * chans, HALF), jnp.float32),
            pltpu.SemaphoreType.DMA((2, 2)),
        ],
        input_output_aliases={2: 1},
        compiler_params=params,
        name="correlate",
    )(me, tied, *held, *pieces)
    stack = flat.reshape(2, sources, chans, F)
    if lax.axis_size("win") == 1:
        return stack
    return lax.psum_scatter(stack, "win", scatter_dimension=1, tiled=True)


def solution(mesh):
    return jax.shard_map(
        per_device,
        mesh=mesh,
        in_specs=(P("chan", "win", None), P()),
        out_specs=P(None, "win", "chan", None),
        check_vma=False,
    )
```

```python
import functools
import math

import jax
import jax.numpy as jnp
import ml_dtypes
import numpy as np
from jax import lax
from jax.experimental import pallas as pl
from jax.experimental.pallas import tpu as pltpu
from jax.sharding import PartitionSpec as P

F = 256
HALF = 128
F0 = 1
K = 64
GAUGE = 4
LANES = 128
VMEM_LIMIT = 24 * 1024 * 1024


def make_table(length):
    times = np.arange(length, dtype=np.int64)[:, None]
    bins = np.arange(F, dtype=np.int64)[None, :] + F0
    phase = (times * bins % length).astype(np.float32) * np.float32(2.0 * math.pi / length)
    phase = phase.astype(np.float64)
    return np.concatenate([np.cos(phase), -np.sin(phase)], axis=1).astype(ml_dtypes.bfloat16)


def make_band():
    rows = np.arange(F)[:, None]
    cols = np.arange(F)[None, :]
    band = np.abs(rows - cols) <= K
    return band.astype(ml_dtypes.bfloat16), (1.0 / band.sum(axis=0)).astype(np.float32)[None, :]


def whiten_block(cur, upper, table_ref, band_ref, inv_ref, turned_ref, first):
    chans, wins, length = cur.shape
    rows = chans * wins
    diff = (upper.astype(jnp.float32) - cur.astype(jnp.float32)).reshape(rows, length)
    power = jnp.sum(diff * diff, axis=1, keepdims=True) * (1.0 / length)
    normed = (diff * lax.rsqrt(power + 1e-05)).astype(jnp.bfloat16)
    spec = jnp.dot(normed, table_ref[...], preferred_element_type=jnp.float32)
    real = spec[:, :F]
    imag = spec[:, F:]
    magnitude = jnp.sqrt(real * real + imag * imag).astype(jnp.bfloat16)
    smooth = jnp.dot(magnitude, band_ref[...], preferred_element_type=jnp.float32) * inv_ref[...]
    gain = 1.0 / (smooth + 1e-06)
    white_re = (real * gain).astype(jnp.bfloat16).astype(jnp.float32)
    white_im = (imag * gain).astype(jnp.bfloat16).astype(jnp.float32)
    pad = jnp.zeros((LANES - 2 * wins, F), jnp.float32)
    for c in range(chans):
        mine = slice(c * wins, (c + 1) * wins)
        both = jnp.concatenate([white_re[mine], white_im[mine], pad], axis=0)
        turned_ref[pl.ds((first + c) * F, F), :] = both.T


def whiten_kernel(cur_ref, upper_ref, table_ref, band_ref, inv_ref, turned_ref):
    first = pl.program_id(0) * GAUGE
    whiten_block(cur_ref[...], upper_ref[...], table_ref, band_ref, inv_ref, turned_ref, first)


def finish_kernel(
    chans, slots, slot_ref, cur_ref, halo_ref, table_ref, band_ref, inv_ref, turned_ref, *refs
):
    stored_ref, rounds, (listed, sem) = refs[0], refs[1:-2], refs[-2:]
    whiten_block(
        cur_ref[...], halo_ref[...], table_ref, band_ref, inv_ref, turned_ref, chans - GAUGE
    )
    copy = pltpu.make_async_copy(turned_ref, stored_ref, sem)
    copy.start()
    dests, _, width = rounds[0].shape
    pairs = HALF // dests // 2
    lane = lax.broadcasted_iota(jnp.int32, (slots, LANES), 1)

    def fill(number, rows_ref):
        for k in range(slots):
            channel = slot_ref[number * slots + k]
            listed[k * F : (k + 1) * F, :] = turned_ref[pl.ds(channel * F, F), :]

        def relayout(dest, carry):
            block = []
            for pair in range(pairs):
                piece = []
                for j in range(2):
                    for half in range(2):
                        at = half * HALF + (dest * pairs + pair) * 2 + j
                        piece.append(listed[pl.ds(at, slots, stride=F), :])
                a, b, c, d = piece
                b = pltpu.roll(b, 96, 1)
                c = pltpu.roll(c, 64, 1)
                d = pltpu.roll(d, 32, 1)
                first = jnp.where(lane < 96, a, b)
                second = jnp.where(lane < 64, b, c)
                third = jnp.where(lane < 32, c, d)
                block.append(jnp.concatenate([first, second, third], axis=1))
            rows_ref[dest] = jnp.concatenate(block, axis=0).astype(jnp.bfloat16)
            return carry

        lax.fori_loop(0, dests, relayout, 0, unroll=4)

    fill(0, rounds[0])
    for number in range(1, len(rounds)):
        pl.when(slot_ref[chans] > number * slots)(
            functools.partial(fill, number, rounds[number])
        )
    copy.wait()


def left_kernel(chans, depth, stored_ref, left_ref, turned_ref, sem):
    copy = pltpu.make_async_copy(stored_ref, turned_ref, sem)
    copy.start()
    copy.wait()
    lane = lax.broadcasted_iota(jnp.int32, (chans, LANES), 1)

    def one(g, carry):
        stack = []
        for half in range(2):
            real = turned_ref[pl.ds(half * HALF + g, chans, stride=F), :]
            ahead = pltpu.roll(real, depth // 2, 1)
            back = pltpu.roll(real, LANES - depth // 2, 1)
            stack += [real, jnp.where(lane < depth // 2, -back, ahead)]
        left_ref[g] = jnp.concatenate(stack, axis=0).astype(jnp.bfloat16)
        return carry

    lax.fori_loop(0, HALF, one, 0, unroll=8)


def pick_kernel(slots, base, place_ref, rows_ref, out_ref):
    sources = place_ref.shape[0]
    dests, height, width = rows_ref.shape
    groups, depth, _ = out_ref.shape
    rows = rows_ref[...].reshape(dests * height, width)
    ids = lax.broadcasted_iota(jnp.int32, (sources, dests * height), 1)
    place = place_ref[...] - base
    inside = (place >= 0) & (place < dests * slots)
    spot = place // slots * height + place % slots
    for pair in range(groups // 2):
        hit = inside & (ids == spot + pair * slots)
        onehot = jnp.where(hit, 1.0, 0.0).astype(jnp.bfloat16)
        turned = jnp.dot(onehot, rows, preferred_element_type=jnp.float32).T
        for j in range(2):
            low = turned[(2 * j) * depth : (2 * j + 1) * depth]
            high = turned[(2 * j + 1) * depth : (2 * j + 2) * depth]
            out_ref[pair * 2 + j] = jnp.concatenate([low, high], axis=1).astype(jnp.bfloat16)


def products(n, origins, me_ref, left_ref, pieces, held):
    rows = left_ref.shape[1]
    depth, width = pieces[0].shape[-2:]
    groups = HALF // n
    sources = width // 2
    outs = rows // 2
    me = me_ref[0]
    lane = lax.broadcasted_iota(jnp.int32, (outs, width), 1)
    for piece, runs in zip(pieces, origins):
        place = 0
        for flip, start, count in runs:
            owner = me ^ flip
            for j in range(count):
                g = owner * groups + start + j
                both = jnp.dot(
                    left_ref[g][:, :depth], piece[place], preferred_element_type=jnp.float32
                )
                mine = jnp.where(lane < sources, both[:outs], both[outs:])
                held[pl.ds(g, outs, stride=HALF), :] = mine
                place += 1


def partial_kernel(n, origins, me_ref, left_ref, *refs):
    products(n, origins, me_ref, left_ref, refs[:-1], refs[-1])


def correlate_kernel(scale, n, origins, sources, me_ref, left_ref, _, *refs):
    pieces, (out_ref, held, turned_ref, sems) = refs[:-4], refs[-4:]
    products(n, origins, me_ref, left_ref, pieces, held)
    outs = held.shape[0] // HALF
    chans = outs // 2
    size = sources * chans
    copies = []
    for part in range(2):
        for c in range(chans):
            base = (part * chans + c) * HALF
            turned = held[base : base + HALF, :].T * scale
            rows_at = pl.ds(part * size + c, sources, stride=chans)
            for half in range(2):
                turned_ref.at[half][rows_at, :] = turned[half * sources : (half + 1) * sources]
        for half in range(2):
            span = pl.ds(part * size, size)
            copy = pltpu.make_async_copy(
                turned_ref.at[half, span],
                out_ref.at[span, pl.ds(half * HALF, HALF)],
                sems.at[part, half],
            )
            copy.start()
            copies.append(copy)
    for copy in copies:
        copy.wait()


def gather_pieces(own, multiply, after_products):
    n = lax.axis_size("chan")
    planes = n // 8
    groups = own.shape[0]
    half = groups // 2
    core, x, y = 1, 2, 4

    def send(block, flip):
        return lax.ppermute(block, "chan", [(i, i ^ flip) for i in range(n)])

    def join(*blocks):
        return jnp.concatenate(blocks, axis=0)

    def traded(origins):
        return [[(flip ^ core, start, count) for runs in origins for flip, start, count in runs]]

    pieces = [own] + [send(own, 8 * k) for k in range(1, min(planes, 3))]
    have, have_from = [], []
    for k in range(planes + 1):
        x_out, y_out, x_from, y_from = [], [], [], []
        if k < planes:
            x_out.append(pieces[k])
            y_out.append(pieces[k])
            x_from.append((8 * k ^ x, 0, groups))
            y_from.append((8 * k ^ y, 0, groups))
            have.append(pieces[k])
            have_from.append([(8 * k, 0, groups)])
        if k > 0:
            far = 8 * (k - 1) ^ x ^ y
            x_out.append(y_in[half:groups])
            y_out.append(x_in[:half])
            x_from.append((far, half, half))
            y_from.append((far, 0, half))
        x_in, y_in = send(join(*x_out), x), send(join(*y_out), y)
        if k < planes:
            have += [x_in, y_in]
            have_from += [x_from, y_from]
        if len(pieces) < planes:
            later, x_in, y_in = lax.optimization_barrier((own, x_in, y_in))
            pieces.append(send(later, 8 * len(pieces)))
    theirs = send(join(*have), core)
    multiply(have, have_from)
    last = after_products(x_in, y_in)
    last_from = [x_from, y_from]
    arrays = [theirs, *last, send(join(*last), core)]
    return arrays, traded(have_from) + last_from + traded(last_from)


def plan_slots(source_index, chans, slots):
    n = lax.axis_size("chan")
    channels = jnp.arange(n * chans, dtype=jnp.int32)
    hits = source_index[:, None] == channels[None, :]
    listed = jnp.any(hits, axis=0).reshape(n, chans).astype(jnp.int32)
    below = (jnp.arange(chans)[:, None] < jnp.arange(chans)[None, :]).astype(jnp.int32)
    rank = jnp.sum(listed[:, :, None] * below[None], axis=1)
    device = jnp.arange(n, dtype=jnp.int32)[:, None]
    place = (rank // slots * n + device) * slots + rank % slots
    places = jnp.sum(jnp.where(hits, place.reshape(1, -1), 0), axis=1, keepdims=True)
    most = jnp.max(jnp.sum(listed, axis=1))
    mine = device == lax.axis_index("chan")
    order = jnp.arange(chans, dtype=jnp.int32)
    is_slot = (mine & (listed > 0))[:, :, None] & (rank[:, :, None] == order)
    held = jnp.sum(jnp.where(is_slot, order[None, :, None], 0), axis=(0, 1))
    return jnp.concatenate([held, most[None]]), places, most


def per_device(traces, source_index):
    chans, wins, length = traces.shape
    n = lax.axis_size("chan")
    sources = source_index.shape[0]
    route = [(i + 1, i) for i in range(n - 1)]
    halo = lax.ppermute(traces[:GAUGE], "chan", route)
    table = jnp.asarray(make_table(length))
    band, inv = make_band()
    band, inv = jnp.asarray(band), jnp.asarray(inv)
    steps = chans // GAUGE
    depth = 2 * wins
    row_width = HALF * 2 * depth // n
    block = (GAUGE, wins, length)
    vmem = pl.BlockSpec(memory_space=pltpu.VMEM)
    smem = pl.BlockSpec(memory_space=pltpu.SMEM)
    hbm = pl.BlockSpec(memory_space=pltpu.HBM)
    consts = [vmem] * 3
    params = pltpu.CompilerParams(vmem_limit_bytes=VMEM_LIMIT)
    pairs = HALF // n // 2
    slots = chans // pairs
    slot_list, places, most = plan_slots(source_index, chans, slots)
    turned = jax.ShapeDtypeStruct((chans * F, LANES), jnp.float32)
    some = pl.pallas_call(
        whiten_kernel,
        grid=(steps - 1,),
        in_specs=[
            pl.BlockSpec(block, lambda i: (i, 0, 0)),
            pl.BlockSpec(block, lambda i: (i + 1, 0, 0)),
            *consts,
        ],
        out_specs=vmem,
        out_shape=turned,
        compiler_params=params,
        cost_estimate=pl.CostEstimate(
            flops=2 * (chans - GAUGE) * wins * (length + F // 2) * 2 * F,
            bytes_accessed=8 * 1024 * 1024,
            transcendentals=0,
        ),
        name="whiten",
    )(traces, traces, table, band, inv)
    rows_shape = jax.ShapeDtypeStruct((n, chans, row_width // pairs), jnp.bfloat16)
    spectra, *rounds = pl.pallas_call(
        functools.partial(finish_kernel, chans, slots),
        grid=(1,),
        in_specs=[
            smem,
            pl.BlockSpec(block, lambda i: (steps - 1, 0, 0)),
            vmem,
            *consts,
            vmem,
        ],
        out_specs=[hbm] + [vmem] * pairs,
        out_shape=[turned] + [rows_shape] * pairs,
        scratch_shapes=[
            pltpu.VMEM((slots * F, LANES), jnp.float32),
            pltpu.SemaphoreType.DMA(()),
        ],
        compiler_params=params,
        name="finish",
    )(slot_list, traces, halo, table, band, inv, some)

    def exchange(number, rows, *beside):
        rows = lax.all_to_all(rows, "chan", 0, 0, tiled=True)
        rows = lax.optimization_barrier((rows, *beside))[0]
        return pl.pallas_call(
            functools.partial(pick_kernel, slots, number * n * slots),
            out_shape=jax.ShapeDtypeStruct((HALF // n, depth, 2 * sources), jnp.bfloat16),
            compiler_params=params,
            name="pick",
        )(places, rows)

    left = pl.pallas_call(
        functools.partial(left_kernel, chans, depth),
        in_specs=[hbm],
        out_specs=vmem,
        out_shape=jax.ShapeDtypeStruct((HALF, 4 * chans, LANES), jnp.bfloat16),
        scratch_shapes=[
            pltpu.VMEM((chans * F, LANES), jnp.float32),
            pltpu.SemaphoreType.DMA(()),
        ],
        compiler_params=params,
        cost_estimate=pl.CostEstimate(
            flops=10 * 1000 * 1000, bytes_accessed=8 * 1024 * 1024, transcendentals=0
        ),
        name="left",
    )(spectra)
    picked = exchange(0, rounds[0], left)
    for number in range(1, pairs):
        picked = lax.cond(
            most > number * slots,
            lambda p, r, number=number: p + exchange(number, r),
            lambda p, r: p,
            picked,
            rounds[number],
        )
    me = lax.axis_index("chan").astype(jnp.int32).reshape(1)
    total_windows = wins * lax.axis_size("win")
    held_shape = jax.ShapeDtypeStruct((2 * chans * HALF, LANES), jnp.float32)
    held = []

    def multiply(pieces, origins):
        held.append(
            pl.pallas_call(
                functools.partial(partial_kernel, n, origins),
                in_specs=[smem, vmem] + [vmem] * len(pieces),
                out_specs=vmem,
                out_shape=held_shape,
                compiler_params=params,
                cost_estimate=pl.CostEstimate(
                    flops=100 * 1000 * 1000, bytes_accessed=4 * 1024 * 1024, transcendentals=0
                ),
                name="products",
            )(me, left, *pieces)
        )

    def after_products(*arrays):
        *arrays, held[0] = lax.optimization_barrier((*arrays, held[0]))
        return arrays

    pieces, origins = gather_pieces(picked, multiply, after_products)
    flat, _ = pl.pallas_call(
        functools.partial(correlate_kernel, 1.0 / total_windows, n, origins, sources),
        in_specs=[smem, vmem, vmem] + [vmem] * len(pieces),
        out_specs=[pl.BlockSpec(memory_space=pl.ANY), vmem],
        out_shape=[jax.ShapeDtypeStruct((2 * sources * chans, F), jnp.float32), held_shape],
        scratch_shapes=[
            pltpu.VMEM((2, 2 * sources * chans, HALF), jnp.float32),
            pltpu.SemaphoreType.DMA((2, 2)),
        ],
        input_output_aliases={2: 1},
        compiler_params=params,
        name="correlate",
    )(me, left, *held, *pieces)
    stack = flat.reshape(2, sources, chans, F)
    if lax.axis_size("win") == 1:
        return stack
    return lax.psum_scatter(stack, "win", scatter_dimension=1, tiled=True)


def solution(mesh):
    return jax.shard_map(
        per_device,
        mesh=mesh,
        in_specs=(P("chan", "win", None), P()),
        out_specs=P(None, "win", "chan", None),
        check_vma=False,
    )
```

```python
import functools
import math

import jax
import jax.numpy as jnp
import ml_dtypes
import numpy as np
from jax import lax
from jax.experimental import pallas as pl
from jax.experimental.pallas import tpu as pltpu
from jax.sharding import PartitionSpec as P

F = 256
HALF = 128
F0 = 1
K = 64
GAUGE = 4
LANES = 128
PITCH = F + 8
HALF_PITCH = HALF + 8
VMEM_LIMIT = 24 * 1024 * 1024


def make_table(length):
    times = np.arange(length, dtype=np.int64)[:, None]
    bins = np.arange(F, dtype=np.int64)[None, :] + F0
    phase = (times * bins % length).astype(np.float32) * np.float32(2.0 * math.pi / length)
    phase = phase.astype(np.float64)
    return np.concatenate([np.cos(phase), -np.sin(phase)], axis=1).astype(ml_dtypes.bfloat16)


def make_band():
    rows = np.arange(F)[:, None]
    cols = np.arange(F)[None, :]
    band = np.abs(rows - cols) <= K
    return band.astype(ml_dtypes.bfloat16), (1.0 / band.sum(axis=0)).astype(np.float32)[None, :]


def whiten_block(cur, upper, table_ref, band_ref, inv_ref, turned_ref, first):
    chans, wins, length = cur.shape
    rows = chans * wins
    diff = (upper.astype(jnp.float32) - cur.astype(jnp.float32)).reshape(rows, length)
    power = jnp.sum(diff * diff, axis=1, keepdims=True) * (1.0 / length)
    normed = (diff * lax.rsqrt(power + 1e-05)).astype(jnp.bfloat16)
    spec = jnp.dot(normed, table_ref[...], preferred_element_type=jnp.float32)
    real = spec[:, :F]
    imag = spec[:, F:]
    magnitude = jnp.sqrt(real * real + imag * imag).astype(jnp.bfloat16)
    smooth = jnp.dot(magnitude, band_ref[...], preferred_element_type=jnp.float32) * inv_ref[...]
    gain = 1.0 / (smooth + 1e-06)
    white_re = (real * gain).astype(jnp.bfloat16).astype(jnp.float32)
    white_im = (imag * gain).astype(jnp.bfloat16).astype(jnp.float32)
    pad = jnp.zeros((LANES - 2 * wins, F), jnp.float32)
    for c in range(chans):
        mine = slice(c * wins, (c + 1) * wins)
        both = jnp.concatenate([white_re[mine], white_im[mine], pad], axis=0)
        turned_ref[pl.ds((first + c) * PITCH, F), :] = both.T


def whiten_kernel(cur_ref, upper_ref, table_ref, band_ref, inv_ref, turned_ref):
    first = pl.program_id(0) * GAUGE
    whiten_block(cur_ref[...], upper_ref[...], table_ref, band_ref, inv_ref, turned_ref, first)


def finish_kernel(
    chans, slots, slot_ref, cur_ref, halo_ref, table_ref, band_ref, inv_ref, _, *refs
):
    turned_ref, rounds, listed = refs[0], refs[1:-1], refs[-1]
    whiten_block(
        cur_ref[...], halo_ref[...], table_ref, band_ref, inv_ref, turned_ref, chans - GAUGE
    )
    dests, _, width = rounds[0].shape
    pairs = HALF // dests // 2
    lane = lax.broadcasted_iota(jnp.int32, (slots, LANES), 1)

    def fill(number, rows_ref):
        for k in range(slots):
            channel = slot_ref[number * slots + k]
            listed[k * PITCH : k * PITCH + F, :] = turned_ref[pl.ds(channel * PITCH, F), :]

        def relayout(dest, carry):
            block = []
            for pair in range(pairs):
                piece = []
                for j in range(2):
                    for half in range(2):
                        at = half * HALF + (dest * pairs + pair) * 2 + j
                        piece.append(listed[pl.ds(at, slots, stride=PITCH), :])
                a, b, c, d = piece
                b = pltpu.roll(b, 96, 1)
                c = pltpu.roll(c, 64, 1)
                d = pltpu.roll(d, 32, 1)
                first = jnp.where(lane < 96, a, b)
                second = jnp.where(lane < 64, b, c)
                third = jnp.where(lane < 32, c, d)
                block.append(jnp.concatenate([first, second, third], axis=1))
            rows_ref[dest] = jnp.concatenate(block, axis=0).astype(jnp.bfloat16)
            return carry

        lax.fori_loop(0, dests, relayout, 0, unroll=4)

    fill(0, rounds[0])
    for number in range(1, len(rounds)):
        pl.when(slot_ref[chans] > number * slots)(
            functools.partial(fill, number, rounds[number])
        )


def left_kernel(chans, depth, turned_ref, left_ref):
    lane = lax.broadcasted_iota(jnp.int32, (chans, LANES), 1)

    def one(g, carry):
        stack = []
        for half in range(2):
            real = turned_ref[pl.ds(half * HALF + g, chans, stride=PITCH), :]
            ahead = pltpu.roll(real, depth // 2, 1)
            back = pltpu.roll(real, LANES - depth // 2, 1)
            stack += [real, jnp.where(lane < depth // 2, -back, ahead)]
        left_ref[g] = jnp.concatenate(stack, axis=0).astype(jnp.bfloat16)
        return carry

    lax.fori_loop(0, HALF, one, 0, unroll=8)


def pick_kernel(slots, base, place_ref, rows_ref, out_ref):
    sources = place_ref.shape[0]
    dests, height, width = rows_ref.shape
    groups, depth, _ = out_ref.shape
    rows = rows_ref[...].reshape(dests * height, width)
    ids = lax.broadcasted_iota(jnp.int32, (sources, dests * height), 1)
    place = place_ref[...] - base
    inside = (place >= 0) & (place < dests * slots)
    spot = place // slots * height + place % slots
    for pair in range(groups // 2):
        hit = inside & (ids == spot + pair * slots)
        onehot = jnp.where(hit, 1.0, 0.0).astype(jnp.bfloat16)
        turned = jnp.dot(onehot, rows, preferred_element_type=jnp.float32).T
        for j in range(2):
            low = turned[(2 * j) * depth : (2 * j + 1) * depth]
            high = turned[(2 * j + 1) * depth : (2 * j + 2) * depth]
            out_ref[pair * 2 + j] = jnp.concatenate([low, high], axis=1).astype(jnp.bfloat16)


def products(n, origins, me_ref, left_ref, pieces, held):
    rows = left_ref.shape[1]
    depth, width = pieces[0].shape[-2:]
    groups = HALF // n
    sources = width // 2
    outs = rows // 2
    me = me_ref[0]
    lane = lax.broadcasted_iota(jnp.int32, (outs, width), 1)
    for piece, runs in zip(pieces, origins):
        place = 0
        for flip, start, count in runs:
            owner = me ^ flip
            for j in range(count):
                g = owner * groups + start + j
                both = jnp.dot(
                    left_ref[g][:, :depth], piece[place], preferred_element_type=jnp.float32
                )
                mine = jnp.where(lane < sources, both[:outs], both[outs:])
                held[pl.ds(g, outs, stride=HALF_PITCH), :] = mine
                place += 1


def partial_kernel(n, origins, chained, me_ref, left_ref, *refs):
    products(n, origins, me_ref, left_ref, refs[chained:-1], refs[-1])


def correlate_kernel(scale, n, origins, sources, me_ref, left_ref, _, *refs):
    pieces, (out_ref, held, turned_ref, sems) = refs[:-4], refs[-4:]
    products(n, origins, me_ref, left_ref, pieces, held)
    outs = held.shape[0] // HALF_PITCH
    chans = outs // 2
    size = sources * chans
    copies = []
    for part in range(2):
        for c in range(chans):
            base = (part * chans + c) * HALF_PITCH
            turned = held[base : base + HALF, :].T * scale
            rows_at = pl.ds(part * size + c, sources, stride=chans)
            for half in range(2):
                turned_ref.at[half][rows_at, :] = turned[half * sources : (half + 1) * sources]
        for half in range(2):
            span = pl.ds(part * size, size)
            copy = pltpu.make_async_copy(
                turned_ref.at[half, span],
                out_ref.at[span, pl.ds(half * HALF, HALF)],
                sems.at[part, half],
            )
            copy.start()
            copies.append(copy)
    for copy in copies:
        copy.wait()


def gather_pieces(own, multiply, after_products):
    n = lax.axis_size("chan")
    planes = n // 8
    groups = own.shape[0]
    most = max(1, groups * 3 // 4)
    rest = groups - most
    core, square = 1, (2, 4, 6)
    column = [8 * k for k in range(1, planes)]

    def send(block, flip):
        return lax.ppermute(block, "chan", [(i, i ^ flip) for i in range(n)])

    def join(*blocks):
        return jnp.concatenate(blocks, axis=0)

    def flipped(flip, runs):
        return [(f ^ flip, start, count) for f, start, count in runs]

    cols = [send(own[:most], flip) for flip in column]
    near = [send(own, flip) for flip in square]
    far = join(*cols)
    far_from = [(flip, 0, most) for flip in column]
    have = [own, *near, far]
    have_from = [[(flip, 0, groups)] for flip in (0, *square)] + [far_from]

    last = [send(far, flip) for flip in square]
    last_from = [flipped(flip, far_from) for flip in square]
    block = join(own[most:], *[p[most:] for p in near])
    block_from = [(flip, most, rest) for flip in (0, *square)]
    last += [send(block, flip) for flip in column]
    last_from += [flipped(flip, block_from) for flip in column]

    multiply(have, have_from)
    tied = after_products(join(*have), *last)
    squares, planes_in = tied[1:4], tied[4:]
    theirs = [send(array, core) for array in (tied[0], *squares, join(*planes_in))]
    theirs_from = [sum(have_from, []), *last_from[:3], sum(last_from[3:], [])]
    multiply(tied[1:], last_from)
    return theirs, [flipped(core, runs) for runs in theirs_from]


def plan_slots(source_index, chans, slots):
    n = lax.axis_size("chan")
    channels = jnp.arange(n * chans, dtype=jnp.int32)
    hits = source_index[:, None] == channels[None, :]
    listed = jnp.any(hits, axis=0).reshape(n, chans).astype(jnp.int32)
    below = (jnp.arange(chans)[:, None] < jnp.arange(chans)[None, :]).astype(jnp.int32)
    rank = jnp.sum(listed[:, :, None] * below[None], axis=1)
    device = jnp.arange(n, dtype=jnp.int32)[:, None]
    place = (rank // slots * n + device) * slots + rank % slots
    places = jnp.sum(jnp.where(hits, place.reshape(1, -1), 0), axis=1, keepdims=True)
    most = jnp.max(jnp.sum(listed, axis=1))
    mine = device == lax.axis_index("chan")
    order = jnp.arange(chans, dtype=jnp.int32)
    is_slot = (mine & (listed > 0))[:, :, None] & (rank[:, :, None] == order)
    held = jnp.sum(jnp.where(is_slot, order[None, :, None], 0), axis=(0, 1))
    return jnp.concatenate([held, most[None]]), places, most


def per_device(traces, source_index):
    chans, wins, length = traces.shape
    n = lax.axis_size("chan")
    sources = source_index.shape[0]
    route = [(i + 1, i) for i in range(n - 1)]
    halo = lax.ppermute(traces[:GAUGE], "chan", route)
    table = jnp.asarray(make_table(length))
    band, inv = make_band()
    band, inv = jnp.asarray(band), jnp.asarray(inv)
    steps = chans // GAUGE
    depth = 2 * wins
    row_width = HALF * 2 * depth // n
    block = (GAUGE, wins, length)
    vmem = pl.BlockSpec(memory_space=pltpu.VMEM)
    smem = pl.BlockSpec(memory_space=pltpu.SMEM)
    consts = [vmem] * 3
    params = pltpu.CompilerParams(vmem_limit_bytes=VMEM_LIMIT)
    pairs = HALF // n // 2
    slots = chans // pairs
    slot_list, places, most = plan_slots(source_index, chans, slots)
    turned = jax.ShapeDtypeStruct((chans * PITCH, LANES), jnp.float32)
    some = pl.pallas_call(
        whiten_kernel,
        grid=(steps - 1,),
        in_specs=[
            pl.BlockSpec(block, lambda i: (i, 0, 0)),
            pl.BlockSpec(block, lambda i: (i + 1, 0, 0)),
            *consts,
        ],
        out_specs=vmem,
        out_shape=turned,
        compiler_params=params,
        cost_estimate=pl.CostEstimate(
            flops=2 * (chans - GAUGE) * wins * (length + F // 2) * 2 * F,
            bytes_accessed=8 * 1024 * 1024,
            transcendentals=0,
        ),
        name="whiten",
    )(traces, traces, table, band, inv)
    rows_shape = jax.ShapeDtypeStruct((n, chans, row_width // pairs), jnp.bfloat16)
    spectra, *rounds = pl.pallas_call(
        functools.partial(finish_kernel, chans, slots),
        grid=(1,),
        in_specs=[
            smem,
            pl.BlockSpec(block, lambda i: (steps - 1, 0, 0)),
            vmem,
            *consts,
            vmem,
        ],
        out_specs=[vmem] * (1 + pairs),
        out_shape=[turned] + [rows_shape] * pairs,
        scratch_shapes=[pltpu.VMEM((slots * PITCH, LANES), jnp.float32)],
        input_output_aliases={6: 0},
        compiler_params=params,
        name="finish",
    )(slot_list, traces, halo, table, band, inv, some)

    def exchange(number, rows):
        rows = lax.all_to_all(rows, "chan", 0, 0, tiled=True)
        return pl.pallas_call(
            functools.partial(pick_kernel, slots, number * n * slots),
            out_shape=jax.ShapeDtypeStruct((HALF // n, depth, 2 * sources), jnp.bfloat16),
            compiler_params=params,
            name="pick",
        )(places, rows)

    left = pl.pallas_call(
        functools.partial(left_kernel, chans, depth),
        in_specs=[vmem],
        out_specs=vmem,
        out_shape=jax.ShapeDtypeStruct((HALF, 4 * chans, LANES), jnp.bfloat16),
        compiler_params=params,
        cost_estimate=pl.CostEstimate(
            flops=10 * 1000 * 1000, bytes_accessed=8 * 1024 * 1024, transcendentals=0
        ),
        name="left",
    )(spectra)
    picked = exchange(0, rounds[0])
    for number in range(1, pairs):
        picked = lax.cond(
            most > number * slots,
            lambda p, r, number=number: p + exchange(number, r),
            lambda p, r: p,
            picked,
            rounds[number],
        )
    me = lax.axis_index("chan").astype(jnp.int32).reshape(1)
    total_windows = wins * lax.axis_size("win")
    held_shape = jax.ShapeDtypeStruct((2 * chans * HALF_PITCH, LANES), jnp.float32)
    held = []

    def multiply(pieces, origins):
        held[:] = [
            pl.pallas_call(
                functools.partial(partial_kernel, n, origins, len(held)),
                in_specs=[smem, vmem] + [vmem] * (len(held) + len(pieces)),
                out_specs=vmem,
                out_shape=held_shape,
                input_output_aliases={2: 0} if held else {},
                compiler_params=params,
                cost_estimate=pl.CostEstimate(
                    flops=100 * 1000 * 1000, bytes_accessed=4 * 1024 * 1024, transcendentals=0
                ),
                name="products",
            )(me, left, *held, *pieces)
        ]

    def after_products(*arrays):
        *arrays, held[0] = lax.optimization_barrier((*arrays, held[0]))
        return arrays

    pieces, origins = gather_pieces(picked, multiply, after_products)
    flat, _ = pl.pallas_call(
        functools.partial(correlate_kernel, 1.0 / total_windows, n, origins, sources),
        in_specs=[smem, vmem, vmem] + [vmem] * len(pieces),
        out_specs=[pl.BlockSpec(memory_space=pl.ANY), vmem],
        out_shape=[jax.ShapeDtypeStruct((2 * sources * chans, F), jnp.float32), held_shape],
        scratch_shapes=[
            pltpu.VMEM((2, 2 * sources * chans, HALF), jnp.float32),
            pltpu.SemaphoreType.DMA((2, 2)),
        ],
        input_output_aliases={2: 1},
        compiler_params=params,
        name="correlate",
    )(me, left, *held, *pieces)
    stack = flat.reshape(2, sources, chans, F)
    if lax.axis_size("win") == 1:
        return stack
    return lax.psum_scatter(stack, "win", scatter_dimension=1, tiled=True)


def solution(mesh):
    return jax.shard_map(
        per_device,
        mesh=mesh,
        in_specs=(P("chan", "win", None), P()),
        out_specs=P(None, "win", "chan", None),
        check_vma=False,
    )
```

```python
import functools
import math

import jax
import jax.numpy as jnp
import ml_dtypes
import numpy as np
from jax import lax
from jax.experimental import pallas as pl
from jax.experimental.pallas import tpu as pltpu
from jax.sharding import PartitionSpec as P

F = 256
HALF = 128
F0 = 1
K = 64
GAUGE = 4
LANES = 128
PITCH = F + 8
HALF_PITCH = HALF + 8
VMEM_LIMIT = 24 * 1024 * 1024


def make_table(length):
    times = np.arange(length, dtype=np.int64)[:, None]
    bins = np.arange(F, dtype=np.int64)[None, :] + F0
    phase = (times * bins % length).astype(np.float32) * np.float32(2.0 * math.pi / length)
    phase = phase.astype(np.float64)
    return np.concatenate([np.cos(phase), -np.sin(phase)], axis=1).astype(ml_dtypes.bfloat16)


def make_band():
    rows = np.arange(F)[:, None]
    cols = np.arange(F)[None, :]
    band = np.abs(rows - cols) <= K
    return band.astype(ml_dtypes.bfloat16), (1.0 / band.sum(axis=0)).astype(np.float32)[None, :]


def whiten_block(cur, upper, table_ref, band_ref, inv_ref, turned_ref, first):
    chans, wins, length = cur.shape
    rows = chans * wins
    diff = (upper.astype(jnp.float32) - cur.astype(jnp.float32)).reshape(rows, length)
    power = jnp.sum(diff * diff, axis=1, keepdims=True) * (1.0 / length)
    normed = (diff * lax.rsqrt(power + 1e-05)).astype(jnp.bfloat16)
    spec = jnp.dot(normed, table_ref[...], preferred_element_type=jnp.float32)
    real = spec[:, :F]
    imag = spec[:, F:]
    magnitude = jnp.sqrt(real * real + imag * imag).astype(jnp.bfloat16)
    smooth = jnp.dot(magnitude, band_ref[...], preferred_element_type=jnp.float32) * inv_ref[...]
    gain = 1.0 / (smooth + 1e-06)
    white_re = (real * gain).astype(jnp.bfloat16).astype(jnp.float32)
    white_im = (imag * gain).astype(jnp.bfloat16).astype(jnp.float32)
    pad = jnp.zeros((LANES - 2 * wins, F), jnp.float32)
    for c in range(chans):
        mine = slice(c * wins, (c + 1) * wins)
        both = jnp.concatenate([white_re[mine], white_im[mine], pad], axis=0)
        turned_ref[pl.ds((first + c) * PITCH, F), :] = both.T


def whiten_kernel(cur_ref, upper_ref, table_ref, band_ref, inv_ref, turned_ref):
    first = pl.program_id(0) * GAUGE
    whiten_block(cur_ref[...], upper_ref[...], table_ref, band_ref, inv_ref, turned_ref, first)


def finish_kernel(
    chans, slots, slot_ref, cur_ref, halo_ref, table_ref, band_ref, inv_ref, _, *refs
):
    turned_ref, rounds, listed = refs[0], refs[1:-1], refs[-1]
    whiten_block(
        cur_ref[...], halo_ref[...], table_ref, band_ref, inv_ref, turned_ref, chans - GAUGE
    )
    dests, _, width = rounds[0].shape
    pairs = HALF // dests // 2
    lane = lax.broadcasted_iota(jnp.int32, (slots, LANES), 1)

    def fill(number, rows_ref):
        for k in range(slots):
            channel = slot_ref[number * slots + k]
            listed[k * PITCH : k * PITCH + F, :] = turned_ref[pl.ds(channel * PITCH, F), :]

        def relayout(dest, carry):
            block = []
            for pair in range(pairs):
                piece = []
                for j in range(2):
                    for half in range(2):
                        at = half * HALF + (dest * pairs + pair) * 2 + j
                        piece.append(listed[pl.ds(at, slots, stride=PITCH), :])
                a, b, c, d = piece
                b = pltpu.roll(b, 96, 1)
                c = pltpu.roll(c, 64, 1)
                d = pltpu.roll(d, 32, 1)
                first = jnp.where(lane < 96, a, b)
                second = jnp.where(lane < 64, b, c)
                third = jnp.where(lane < 32, c, d)
                block.append(jnp.concatenate([first, second, third], axis=1))
            rows_ref[dest] = jnp.concatenate(block, axis=0).astype(jnp.bfloat16)
            return carry

        lax.fori_loop(0, dests, relayout, 0, unroll=4)

    fill(0, rounds[0])
    for number in range(1, len(rounds)):
        pl.when(slot_ref[chans] > number * slots)(
            functools.partial(fill, number, rounds[number])
        )


def left_kernel(chans, depth, turned_ref, left_ref):
    lane = lax.broadcasted_iota(jnp.int32, (chans, LANES), 1)

    def one(g, carry):
        stack = []
        for half in range(2):
            real = turned_ref[pl.ds(half * HALF + g, chans, stride=PITCH), :]
            ahead = pltpu.roll(real, depth // 2, 1)
            back = pltpu.roll(real, LANES - depth // 2, 1)
            stack += [real, jnp.where(lane < depth // 2, -back, ahead)]
        left_ref[g] = jnp.concatenate(stack, axis=0).astype(jnp.bfloat16)
        return carry

    lax.fori_loop(0, HALF, one, 0, unroll=8)


def pick_kernel(slots, base, place_ref, rows_ref, out_ref):
    sources = place_ref.shape[0]
    dests, height, width = rows_ref.shape
    groups, depth, _ = out_ref.shape
    rows = rows_ref[...].reshape(dests * height, width)
    ids = lax.broadcasted_iota(jnp.int32, (sources, dests * height), 1)
    place = place_ref[...] - base
    inside = (place >= 0) & (place < dests * slots)
    spot = place // slots * height + place % slots
    for pair in range(groups // 2):
        hit = inside & (ids == spot + pair * slots)
        onehot = jnp.where(hit, 1.0, 0.0).astype(jnp.bfloat16)
        turned = jnp.dot(onehot, rows, preferred_element_type=jnp.float32).T
        for j in range(2):
            low = turned[(2 * j) * depth : (2 * j + 1) * depth]
            high = turned[(2 * j + 1) * depth : (2 * j + 2) * depth]
            out_ref[pair * 2 + j] = jnp.concatenate([low, high], axis=1).astype(jnp.bfloat16)


def products(n, origins, me_ref, left_ref, pieces, held):
    rows = left_ref.shape[1]
    depth, width = pieces[0].shape[-2:]
    groups = HALF // n
    sources = width // 2
    outs = rows // 2
    me = me_ref[0]
    lane = lax.broadcasted_iota(jnp.int32, (outs, width), 1)
    for piece, runs in zip(pieces, origins):
        place = 0
        for flip, start, count in runs:
            owner = me ^ flip
            for j in range(count):
                g = owner * groups + start + j
                both = jnp.dot(
                    left_ref[g][:, :depth], piece[place], preferred_element_type=jnp.float32
                )
                mine = jnp.where(lane < sources, both[:outs], both[outs:])
                held[pl.ds(g, outs, stride=HALF_PITCH), :] = mine
                place += 1


def partial_kernel(n, origins, chained, me_ref, left_ref, *refs):
    products(n, origins, me_ref, left_ref, refs[chained:-1], refs[-1])


def correlate_kernel(scale, n, origins, sources, me_ref, left_ref, _, *refs):
    pieces, (out_ref, held, turned_ref, sems) = refs[:-4], refs[-4:]
    products(n, origins, me_ref, left_ref, pieces, held)
    outs = held.shape[0] // HALF_PITCH
    chans = outs // 2
    size = sources * chans
    copies = []
    for part in range(2):
        for c in range(chans):
            base = (part * chans + c) * HALF_PITCH
            turned = held[base : base + HALF, :].T * scale
            rows_at = pl.ds(part * size + c, sources, stride=chans)
            for half in range(2):
                turned_ref.at[half][rows_at, :] = turned[half * sources : (half + 1) * sources]
        for half in range(2):
            span = pl.ds(part * size, size)
            copy = pltpu.make_async_copy(
                turned_ref.at[half, span],
                out_ref.at[span, pl.ds(half * HALF, HALF)],
                sems.at[part, half],
            )
            copy.start()
            copies.append(copy)
    for copy in copies:
        copy.wait()


def gather_pieces(own, multiply, after_products):
    n = lax.axis_size("chan")
    groups = own.shape[0]
    half = groups // 2
    core, x, y = 1, 2, 4
    column = [8 * k for k in range(1, n // 8)]

    def send(block, flip):
        return lax.ppermute(block, "chan", [(i, i ^ flip) for i in range(n)])

    def join(*blocks):
        return jnp.concatenate(blocks, axis=0)

    def flipped(flip, runs):
        return [(f ^ flip, start, count) for f, start, count in runs]

    def halves(block, start):
        return join(*[block[k * groups + start :][:half] for k in range(len(column))])

    cols = [send(own, flip) for flip in column]
    own_x, own_y = send(own, x), send(own, y)
    far = join(*cols)
    far_from = [(flip, 0, groups) for flip in column]
    far_x = send(join(far, own_y[half:]), x)
    far_y = send(join(far, own_x[:half]), y)
    near = [own, own_x, own_y, far]
    near_from = [[(0, 0, groups)], [(x, 0, groups)], [(y, 0, groups)], far_from]
    multiply(near, near_from)
    far_x, far_y = after_products(far_x, far_y)
    mid = [far_x, far_y]
    mid_from = [
        flipped(x, far_from + [(y, half, half)]),
        flipped(y, far_from + [(x, 0, half)]),
    ]
    last = [send(halves(far_y, half), x), send(halves(far_x, 0), y)]
    last_from = [
        [(flip ^ x ^ y, half, half) for flip in column],
        [(flip ^ x ^ y, 0, half) for flip in column],
    ]
    theirs = send(join(*near, *mid), core)
    theirs_from = flipped(core, sum(near_from + mid_from, []))
    multiply(mid, mid_from)
    last = after_products(*last)
    arrays = [theirs, *last, send(join(*last), core)]
    return arrays, [theirs_from, *last_from, flipped(core, sum(last_from, []))]


def plan_slots(source_index, chans, slots):
    n = lax.axis_size("chan")
    channels = jnp.arange(n * chans, dtype=jnp.int32)
    hits = source_index[:, None] == channels[None, :]
    listed = jnp.any(hits, axis=0).reshape(n, chans).astype(jnp.int32)
    below = (jnp.arange(chans)[:, None] < jnp.arange(chans)[None, :]).astype(jnp.int32)
    rank = jnp.sum(listed[:, :, None] * below[None], axis=1)
    device = jnp.arange(n, dtype=jnp.int32)[:, None]
    place = (rank // slots * n + device) * slots + rank % slots
    places = jnp.sum(jnp.where(hits, place.reshape(1, -1), 0), axis=1, keepdims=True)
    most = jnp.max(jnp.sum(listed, axis=1))
    mine = device == lax.axis_index("chan")
    order = jnp.arange(chans, dtype=jnp.int32)
    is_slot = (mine & (listed > 0))[:, :, None] & (rank[:, :, None] == order)
    held = jnp.sum(jnp.where(is_slot, order[None, :, None], 0), axis=(0, 1))
    return jnp.concatenate([held, most[None]]), places, most


def per_device(traces, source_index):
    chans, wins, length = traces.shape
    n = lax.axis_size("chan")
    sources = source_index.shape[0]
    route = [(i + 1, i) for i in range(n - 1)]
    halo = lax.ppermute(traces[:GAUGE], "chan", route)
    table = jnp.asarray(make_table(length))
    band, inv = make_band()
    band, inv = jnp.asarray(band), jnp.asarray(inv)
    steps = chans // GAUGE
    depth = 2 * wins
    row_width = HALF * 2 * depth // n
    block = (GAUGE, wins, length)
    vmem = pl.BlockSpec(memory_space=pltpu.VMEM)
    smem = pl.BlockSpec(memory_space=pltpu.SMEM)
    consts = [vmem] * 3
    params = pltpu.CompilerParams(vmem_limit_bytes=VMEM_LIMIT)
    pairs = HALF // n // 2
    slots = chans // pairs
    slot_list, places, most = plan_slots(source_index, chans, slots)
    turned = jax.ShapeDtypeStruct((chans * PITCH, LANES), jnp.float32)
    some = pl.pallas_call(
        whiten_kernel,
        grid=(steps - 1,),
        in_specs=[
            pl.BlockSpec(block, lambda i: (i, 0, 0)),
            pl.BlockSpec(block, lambda i: (i + 1, 0, 0)),
            *consts,
        ],
        out_specs=vmem,
        out_shape=turned,
        compiler_params=params,
        cost_estimate=pl.CostEstimate(
            flops=2 * (chans - GAUGE) * wins * (length + F // 2) * 2 * F,
            bytes_accessed=8 * 1024 * 1024,
            transcendentals=0,
        ),
        name="whiten",
    )(traces, traces, table, band, inv)
    rows_shape = jax.ShapeDtypeStruct((n, chans, row_width // pairs), jnp.bfloat16)
    spectra, *rounds = pl.pallas_call(
        functools.partial(finish_kernel, chans, slots),
        grid=(1,),
        in_specs=[
            smem,
            pl.BlockSpec(block, lambda i: (steps - 1, 0, 0)),
            vmem,
            *consts,
            vmem,
        ],
        out_specs=[vmem] * (1 + pairs),
        out_shape=[turned] + [rows_shape] * pairs,
        scratch_shapes=[pltpu.VMEM((slots * PITCH, LANES), jnp.float32)],
        input_output_aliases={6: 0},
        compiler_params=params,
        name="finish",
    )(slot_list, traces, halo, table, band, inv, some)

    def exchange(number, rows):
        rows = lax.all_to_all(rows, "chan", 0, 0, tiled=True)
        return pl.pallas_call(
            functools.partial(pick_kernel, slots, number * n * slots),
            out_shape=jax.ShapeDtypeStruct((HALF // n, depth, 2 * sources), jnp.bfloat16),
            compiler_params=params,
            name="pick",
        )(places, rows)

    left = pl.pallas_call(
        functools.partial(left_kernel, chans, depth),
        in_specs=[vmem],
        out_specs=vmem,
        out_shape=jax.ShapeDtypeStruct((HALF, 4 * chans, LANES), jnp.bfloat16),
        compiler_params=params,
        cost_estimate=pl.CostEstimate(
            flops=10 * 1000 * 1000, bytes_accessed=8 * 1024 * 1024, transcendentals=0
        ),
        name="left",
    )(spectra)
    picked = exchange(0, rounds[0])
    for number in range(1, pairs):
        picked = lax.cond(
            most > number * slots,
            lambda p, r, number=number: p + exchange(number, r),
            lambda p, r: p,
            picked,
            rounds[number],
        )
    me = lax.axis_index("chan").astype(jnp.int32).reshape(1)
    total_windows = wins * lax.axis_size("win")
    held_shape = jax.ShapeDtypeStruct((2 * chans * HALF_PITCH, LANES), jnp.float32)
    held = []

    def multiply(pieces, origins):
        held[:] = [
            pl.pallas_call(
                functools.partial(partial_kernel, n, origins, len(held)),
                in_specs=[smem, vmem] + [vmem] * (len(held) + len(pieces)),
                out_specs=vmem,
                out_shape=held_shape,
                input_output_aliases={2: 0} if held else {},
                compiler_params=params,
                cost_estimate=pl.CostEstimate(
                    flops=100 * 1000 * 1000, bytes_accessed=4 * 1024 * 1024, transcendentals=0
                ),
                name="products",
            )(me, left, *held, *pieces)
        ]

    def after_products(*arrays):
        *arrays, held[0] = lax.optimization_barrier((*arrays, held[0]))
        return arrays

    pieces, origins = gather_pieces(picked, multiply, after_products)
    flat, _ = pl.pallas_call(
        functools.partial(correlate_kernel, 1.0 / total_windows, n, origins, sources),
        in_specs=[smem, vmem, vmem] + [vmem] * len(pieces),
        out_specs=[pl.BlockSpec(memory_space=pl.ANY), vmem],
        out_shape=[jax.ShapeDtypeStruct((2 * sources * chans, F), jnp.float32), held_shape],
        scratch_shapes=[
            pltpu.VMEM((2, 2 * sources * chans, HALF), jnp.float32),
            pltpu.SemaphoreType.DMA((2, 2)),
        ],
        input_output_aliases={2: 1},
        compiler_params=params,
        name="correlate",
    )(me, left, *held, *pieces)
    stack = flat.reshape(2, sources, chans, F)
    if lax.axis_size("win") == 1:
        return stack
    return lax.psum_scatter(stack, "win", scatter_dimension=1, tiled=True)


def solution(mesh):
    return jax.shard_map(
        per_device,
        mesh=mesh,
        in_specs=(P("chan", "win", None), P()),
        out_specs=P(None, "win", "chan", None),
        check_vma=False,
    )
```

```python
import functools
import math

import jax
import jax.numpy as jnp
import ml_dtypes
import numpy as np
from jax import lax
from jax.experimental import pallas as pl
from jax.experimental.pallas import tpu as pltpu
from jax.sharding import PartitionSpec as P

F = 256
HALF = 128
F0 = 1
K = 64
GAUGE = 4
LANES = 128
PITCH = F + 8
HALF_PITCH = HALF + 8
VMEM_LIMIT = 24 * 1024 * 1024


def make_table(length):
    times = np.arange(length, dtype=np.int64)[:, None]
    bins = np.arange(F, dtype=np.int64)[None, :] + F0
    phase = (times * bins % length).astype(np.float32) * np.float32(2.0 * math.pi / length)
    phase = phase.astype(np.float64)
    return np.concatenate([np.cos(phase), -np.sin(phase)], axis=1).astype(ml_dtypes.bfloat16)


def make_band():
    rows = np.arange(F)[:, None]
    cols = np.arange(F)[None, :]
    band = np.abs(rows - cols) <= K
    return band.astype(ml_dtypes.bfloat16), (1.0 / band.sum(axis=0)).astype(np.float32)[None, :]


def whiten_block(cur, upper, table_ref, band_ref, inv_ref, turned_ref, first):
    chans, wins, length = cur.shape
    rows = chans * wins
    diff = (upper.astype(jnp.float32) - cur.astype(jnp.float32)).reshape(rows, length)
    power = jnp.sum(diff * diff, axis=1, keepdims=True) * (1.0 / length)
    normed = (diff * lax.rsqrt(power + 1e-05)).astype(jnp.bfloat16)
    spec = jnp.dot(normed, table_ref[...], preferred_element_type=jnp.float32)
    real = spec[:, :F]
    imag = spec[:, F:]
    magnitude = jnp.sqrt(real * real + imag * imag).astype(jnp.bfloat16)
    smooth = jnp.dot(magnitude, band_ref[...], preferred_element_type=jnp.float32) * inv_ref[...]
    gain = 1.0 / (smooth + 1e-06)
    white_re = (real * gain).astype(jnp.bfloat16).astype(jnp.float32)
    white_im = (imag * gain).astype(jnp.bfloat16).astype(jnp.float32)
    pad = jnp.zeros((LANES - 2 * wins, F), jnp.float32)
    for c in range(chans):
        mine = slice(c * wins, (c + 1) * wins)
        both = jnp.concatenate([white_re[mine], white_im[mine], pad], axis=0)
        turned_ref[pl.ds((first + c) * PITCH, F), :] = both.T


def whiten_kernel(cur_ref, upper_ref, table_ref, band_ref, inv_ref, turned_ref):
    first = pl.program_id(0) * GAUGE
    whiten_block(cur_ref[...], upper_ref[...], table_ref, band_ref, inv_ref, turned_ref, first)


def finish_kernel(
    chans, slots, slot_ref, cur_ref, halo_ref, table_ref, band_ref, inv_ref, _, *refs
):
    turned_ref, rounds, listed = refs[0], refs[1:-1], refs[-1]
    whiten_block(
        cur_ref[...], halo_ref[...], table_ref, band_ref, inv_ref, turned_ref, chans - GAUGE
    )
    dests, _, width = rounds[0].shape
    pairs = HALF // dests // 2
    lane = lax.broadcasted_iota(jnp.int32, (slots, LANES), 1)

    def fill(number, rows_ref):
        for k in range(slots):
            channel = slot_ref[number * slots + k]
            listed[k * PITCH : k * PITCH + F, :] = turned_ref[pl.ds(channel * PITCH, F), :]

        def relayout(dest, carry):
            block = []
            for pair in range(pairs):
                piece = []
                for j in range(2):
                    for half in range(2):
                        at = half * HALF + (dest * pairs + pair) * 2 + j
                        piece.append(listed[pl.ds(at, slots, stride=PITCH), :])
                a, b, c, d = piece
                b = pltpu.roll(b, 96, 1)
                c = pltpu.roll(c, 64, 1)
                d = pltpu.roll(d, 32, 1)
                first = jnp.where(lane < 96, a, b)
                second = jnp.where(lane < 64, b, c)
                third = jnp.where(lane < 32, c, d)
                block.append(jnp.concatenate([first, second, third], axis=1))
            rows_ref[dest] = jnp.concatenate(block, axis=0).astype(jnp.bfloat16)
            return carry

        lax.fori_loop(0, dests, relayout, 0, unroll=4)

    fill(0, rounds[0])
    for number in range(1, len(rounds)):
        pl.when(slot_ref[chans] > number * slots)(
            functools.partial(fill, number, rounds[number])
        )


def left_kernel(chans, depth, turned_ref, left_ref):
    lane = lax.broadcasted_iota(jnp.int32, (chans, LANES), 1)

    def one(g, carry):
        stack = []
        for half in range(2):
            real = turned_ref[pl.ds(half * HALF + g, chans, stride=PITCH), :]
            ahead = pltpu.roll(real, depth // 2, 1)
            back = pltpu.roll(real, LANES - depth // 2, 1)
            stack += [real, jnp.where(lane < depth // 2, -back, ahead)]
        left_ref[g] = jnp.concatenate(stack, axis=0).astype(jnp.bfloat16)
        return carry

    lax.fori_loop(0, HALF, one, 0, unroll=8)


def pick_kernel(slots, base, place_ref, rows_ref, out_ref):
    sources = place_ref.shape[0]
    dests, height, width = rows_ref.shape
    groups, depth, _ = out_ref.shape
    rows = rows_ref[...].reshape(dests * height, width)
    ids = lax.broadcasted_iota(jnp.int32, (sources, dests * height), 1)
    place = place_ref[...] - base
    inside = (place >= 0) & (place < dests * slots)
    spot = place // slots * height + place % slots
    for pair in range(groups // 2):
        hit = inside & (ids == spot + pair * slots)
        onehot = jnp.where(hit, 1.0, 0.0).astype(jnp.bfloat16)
        turned = jnp.dot(onehot, rows, preferred_element_type=jnp.float32).T
        for j in range(2):
            low = turned[(2 * j) * depth : (2 * j + 1) * depth]
            high = turned[(2 * j + 1) * depth : (2 * j + 2) * depth]
            out_ref[pair * 2 + j] = jnp.concatenate([low, high], axis=1).astype(jnp.bfloat16)


def products(n, origins, me_ref, left_ref, pieces, held):
    rows = left_ref.shape[1]
    depth, width = pieces[0].shape[-2:]
    groups = HALF // n
    sources = width // 2
    outs = rows // 2
    me = me_ref[0]
    lane = lax.broadcasted_iota(jnp.int32, (outs, width), 1)
    for piece, runs in zip(pieces, origins):
        place = 0
        for flip, start, count in runs:
            owner = me ^ flip
            for j in range(count):
                g = owner * groups + start + j
                both = jnp.dot(
                    left_ref[g][:, :depth], piece[place], preferred_element_type=jnp.float32
                )
                mine = jnp.where(lane < sources, both[:outs], both[outs:])
                held[pl.ds(g, outs, stride=HALF_PITCH), :] = mine
                place += 1


def partial_kernel(n, origins, chained, me_ref, left_ref, *refs):
    products(n, origins, me_ref, left_ref, refs[chained:-1], refs[-1])


def correlate_kernel(scale, n, origins, sources, me_ref, left_ref, _, *refs):
    pieces, (out_ref, held, turned_ref, sems) = refs[:-4], refs[-4:]
    products(n, origins, me_ref, left_ref, pieces, held)
    outs = held.shape[0] // HALF_PITCH
    chans = outs // 2
    size = sources * chans
    copies = []
    for part in range(2):
        for c in range(chans):
            base = (part * chans + c) * HALF_PITCH
            turned = held[base : base + HALF, :].T * scale
            rows_at = pl.ds(part * size + c, sources, stride=chans)
            for half in range(2):
                turned_ref.at[half][rows_at, :] = turned[half * sources : (half + 1) * sources]
        for half in range(2):
            span = pl.ds(part * size, size)
            copy = pltpu.make_async_copy(
                turned_ref.at[half, span],
                out_ref.at[span, pl.ds(half * HALF, HALF)],
                sems.at[part, half],
            )
            copy.start()
            copies.append(copy)
    for copy in copies:
        copy.wait()


def gather_pieces(own, multiply, after_products):
    n = lax.axis_size("chan")
    groups = own.shape[0]
    half = groups // 2
    core, x, y = 1, 2, 4
    column = [8 * k for k in range(1, n // 8)]

    def send(block, flip):
        return lax.ppermute(block, "chan", [(i, i ^ flip) for i in range(n)])

    def join(*blocks):
        return jnp.concatenate(blocks, axis=0)

    def flipped(flip, runs):
        return [(f ^ flip, start, count) for f, start, count in runs]

    def halves(block, start):
        return join(*[block[k * groups + start :][:half] for k in range(len(column))])

    cols = [send(own, flip) for flip in column]
    own_x, own_y = send(own[:half], x), send(own[half:], y)
    far = join(*cols)
    far_from = [(flip, 0, groups) for flip in column]
    far_x, far_y = send(join(far, own[half:]), x), send(join(far, own[:half]), y)
    near = [own, own_x, own_y, far]
    near_from = [[(0, 0, groups)], [(x, 0, half)], [(y, half, half)], far_from]
    multiply(near, near_from)
    far_x, far_y = after_products(far_x, far_y)
    mid = [far_x, far_y]
    mid_from = [
        flipped(x, far_from + [(0, half, half)]),
        flipped(y, far_from + [(0, 0, half)]),
    ]
    last = [
        send(join(halves(far_y, half), own_y), x),
        send(join(halves(far_x, 0), own_x), y),
    ]
    last_from = [
        [(flip ^ x ^ y, half, half) for flip in (*column, 0)],
        [(flip ^ x ^ y, 0, half) for flip in (*column, 0)],
    ]
    theirs = send(join(*near, *mid), core)
    theirs_from = flipped(core, sum(near_from + mid_from, []))
    multiply(mid, mid_from)
    last = after_products(*last)
    final = send(join(*last), core)
    multiply([theirs, *last], [theirs_from, *last_from])
    return [final], [flipped(core, sum(last_from, []))]


def plan_slots(source_index, chans, slots):
    n = lax.axis_size("chan")
    channels = jnp.arange(n * chans, dtype=jnp.int32)
    hits = source_index[:, None] == channels[None, :]
    listed = jnp.any(hits, axis=0).reshape(n, chans).astype(jnp.int32)
    below = (jnp.arange(chans)[:, None] < jnp.arange(chans)[None, :]).astype(jnp.int32)
    rank = jnp.sum(listed[:, :, None] * below[None], axis=1)
    device = jnp.arange(n, dtype=jnp.int32)[:, None]
    place = (rank // slots * n + device) * slots + rank % slots
    places = jnp.sum(jnp.where(hits, place.reshape(1, -1), 0), axis=1, keepdims=True)
    most = jnp.max(jnp.sum(listed, axis=1))
    mine = device == lax.axis_index("chan")
    order = jnp.arange(chans, dtype=jnp.int32)
    is_slot = (mine & (listed > 0))[:, :, None] & (rank[:, :, None] == order)
    held = jnp.sum(jnp.where(is_slot, order[None, :, None], 0), axis=(0, 1))
    return jnp.concatenate([held, most[None]]), places, most


def per_device(traces, source_index):
    chans, wins, length = traces.shape
    n = lax.axis_size("chan")
    sources = source_index.shape[0]
    route = [(i + 1, i) for i in range(n - 1)]
    halo = lax.ppermute(traces[:GAUGE], "chan", route)
    table = jnp.asarray(make_table(length))
    band, inv = make_band()
    band, inv = jnp.asarray(band), jnp.asarray(inv)
    steps = chans // GAUGE
    depth = 2 * wins
    row_width = HALF * 2 * depth // n
    block = (GAUGE, wins, length)
    vmem = pl.BlockSpec(memory_space=pltpu.VMEM)
    smem = pl.BlockSpec(memory_space=pltpu.SMEM)
    consts = [vmem] * 3
    params = pltpu.CompilerParams(vmem_limit_bytes=VMEM_LIMIT)
    pairs = HALF // n // 2
    slots = chans // pairs
    slot_list, places, most = plan_slots(source_index, chans, slots)
    turned = jax.ShapeDtypeStruct((chans * PITCH, LANES), jnp.float32)
    some = pl.pallas_call(
        whiten_kernel,
        grid=(steps - 1,),
        in_specs=[
            pl.BlockSpec(block, lambda i: (i, 0, 0)),
            pl.BlockSpec(block, lambda i: (i + 1, 0, 0)),
            *consts,
        ],
        out_specs=vmem,
        out_shape=turned,
        compiler_params=params,
        cost_estimate=pl.CostEstimate(
            flops=2 * (chans - GAUGE) * wins * (length + F // 2) * 2 * F,
            bytes_accessed=8 * 1024 * 1024,
            transcendentals=0,
        ),
        name="whiten",
    )(traces, traces, table, band, inv)
    rows_shape = jax.ShapeDtypeStruct((n, chans, row_width // pairs), jnp.bfloat16)
    spectra, *rounds = pl.pallas_call(
        functools.partial(finish_kernel, chans, slots),
        grid=(1,),
        in_specs=[
            smem,
            pl.BlockSpec(block, lambda i: (steps - 1, 0, 0)),
            vmem,
            *consts,
            vmem,
        ],
        out_specs=[vmem] * (1 + pairs),
        out_shape=[turned] + [rows_shape] * pairs,
        scratch_shapes=[pltpu.VMEM((slots * PITCH, LANES), jnp.float32)],
        input_output_aliases={6: 0},
        compiler_params=params,
        name="finish",
    )(slot_list, traces, halo, table, band, inv, some)

    def exchange(number, rows):
        rows = lax.all_to_all(rows, "chan", 0, 0, tiled=True)
        return pl.pallas_call(
            functools.partial(pick_kernel, slots, number * n * slots),
            out_shape=jax.ShapeDtypeStruct((HALF // n, depth, 2 * sources), jnp.bfloat16),
            compiler_params=params,
            name="pick",
        )(places, rows)

    picked = exchange(0, rounds[0])
    for number in range(1, pairs):
        picked = lax.cond(
            most > number * slots,
            lambda p, r, number=number: p + exchange(number, r),
            lambda p, r: p,
            picked,
            rounds[number],
        )
    picked, spectra = lax.optimization_barrier((picked, spectra))
    left = pl.pallas_call(
        functools.partial(left_kernel, chans, depth),
        in_specs=[vmem],
        out_specs=vmem,
        out_shape=jax.ShapeDtypeStruct((HALF, 4 * chans, LANES), jnp.bfloat16),
        compiler_params=params,
        cost_estimate=pl.CostEstimate(
            flops=10 * 1000 * 1000, bytes_accessed=8 * 1024 * 1024, transcendentals=0
        ),
        name="left",
    )(spectra)
    me = lax.axis_index("chan").astype(jnp.int32).reshape(1)
    total_windows = wins * lax.axis_size("win")
    held_shape = jax.ShapeDtypeStruct((2 * chans * HALF_PITCH, LANES), jnp.float32)
    held = []

    def multiply(pieces, origins):
        held[:] = [
            pl.pallas_call(
                functools.partial(partial_kernel, n, origins, len(held)),
                in_specs=[smem, vmem] + [vmem] * (len(held) + len(pieces)),
                out_specs=vmem,
                out_shape=held_shape,
                input_output_aliases={2: 0} if held else {},
                compiler_params=params,
                cost_estimate=pl.CostEstimate(
                    flops=100 * 1000 * 1000, bytes_accessed=4 * 1024 * 1024, transcendentals=0
                ),
                name="products",
            )(me, left, *held, *pieces)
        ]

    def after_products(*arrays):
        *arrays, held[0] = lax.optimization_barrier((*arrays, held[0]))
        return arrays

    pieces, origins = gather_pieces(picked, multiply, after_products)
    flat, _ = pl.pallas_call(
        functools.partial(correlate_kernel, 1.0 / total_windows, n, origins, sources),
        in_specs=[smem, vmem, vmem] + [vmem] * len(pieces),
        out_specs=[pl.BlockSpec(memory_space=pl.ANY), vmem],
        out_shape=[jax.ShapeDtypeStruct((2 * sources * chans, F), jnp.float32), held_shape],
        scratch_shapes=[
            pltpu.VMEM((2, 2 * sources * chans, HALF), jnp.float32),
            pltpu.SemaphoreType.DMA((2, 2)),
        ],
        input_output_aliases={2: 1},
        compiler_params=params,
        name="correlate",
    )(me, left, *held, *pieces)
    stack = flat.reshape(2, sources, chans, F)
    if lax.axis_size("win") == 1:
        return stack
    return lax.psum_scatter(stack, "win", scatter_dimension=1, tiled=True)


def solution(mesh):
    return jax.shard_map(
        per_device,
        mesh=mesh,
        in_specs=(P("chan", "win", None), P()),
        out_specs=P(None, "win", "chan", None),
        check_vma=False,
    )
```

```python
import functools
import math

import jax
import jax.numpy as jnp
import ml_dtypes
import numpy as np
from jax import lax
from jax.experimental import pallas as pl
from jax.experimental.pallas import tpu as pltpu
from jax.sharding import PartitionSpec as P

F = 256
HALF = 128
F0 = 1
K = 64
GAUGE = 4
LANES = 128
PITCH = F + 8
HALF_PITCH = HALF + 8
VMEM_LIMIT = 24 * 1024 * 1024


def make_table(length):
    times = np.arange(length, dtype=np.int64)[:, None]
    bins = np.arange(F, dtype=np.int64)[None, :] + F0
    phase = (times * bins % length).astype(np.float32) * np.float32(2.0 * math.pi / length)
    phase = phase.astype(np.float64)
    return np.concatenate([np.cos(phase), -np.sin(phase)], axis=1).astype(ml_dtypes.bfloat16)


def make_band():
    rows = np.arange(F)[:, None]
    cols = np.arange(F)[None, :]
    band = np.abs(rows - cols) <= K
    return band.astype(ml_dtypes.bfloat16), (1.0 / band.sum(axis=0)).astype(np.float32)[None, :]


def whiten_block(cur, upper, table_ref, band_ref, inv_ref, turned_ref, first):
    chans, wins, length = cur.shape
    rows = chans * wins
    diff = (upper.astype(jnp.float32) - cur.astype(jnp.float32)).reshape(rows, length)
    power = jnp.sum(diff * diff, axis=1, keepdims=True) * (1.0 / length)
    normed = (diff * lax.rsqrt(power + 1e-05)).astype(jnp.bfloat16)
    spec = jnp.dot(normed, table_ref[...], preferred_element_type=jnp.float32)
    real = spec[:, :F]
    imag = spec[:, F:]
    magnitude = jnp.sqrt(real * real + imag * imag).astype(jnp.bfloat16)
    smooth = jnp.dot(magnitude, band_ref[...], preferred_element_type=jnp.float32) * inv_ref[...]
    gain = 1.0 / (smooth + 1e-06)
    white_re = (real * gain).astype(jnp.bfloat16).astype(jnp.float32)
    white_im = (imag * gain).astype(jnp.bfloat16).astype(jnp.float32)
    pad = jnp.zeros((LANES - 2 * wins, F), jnp.float32)
    for c in range(chans):
        mine = slice(c * wins, (c + 1) * wins)
        both = jnp.concatenate([white_re[mine], white_im[mine], pad], axis=0)
        turned_ref[pl.ds((first + c) * PITCH, F), :] = both.T


def whiten_kernel(cur_ref, upper_ref, table_ref, band_ref, inv_ref, turned_ref):
    first = pl.program_id(0) * GAUGE
    whiten_block(cur_ref[...], upper_ref[...], table_ref, band_ref, inv_ref, turned_ref, first)


def finish_kernel(
    chans, slots, slot_ref, cur_ref, halo_ref, table_ref, band_ref, inv_ref, _, *refs
):
    turned_ref, rounds, listed = refs[0], refs[1:-1], refs[-1]
    whiten_block(
        cur_ref[...], halo_ref[...], table_ref, band_ref, inv_ref, turned_ref, chans - GAUGE
    )
    dests, _, width = rounds[0].shape
    pairs = HALF // dests // 2
    lane = lax.broadcasted_iota(jnp.int32, (slots, LANES), 1)

    def fill(number, rows_ref):
        for k in range(slots):
            channel = slot_ref[number * slots + k]
            listed[k * PITCH : k * PITCH + F, :] = turned_ref[pl.ds(channel * PITCH, F), :]

        def relayout(dest, carry):
            block = []
            for pair in range(pairs):
                piece = []
                for j in range(2):
                    for half in range(2):
                        at = half * HALF + (dest * pairs + pair) * 2 + j
                        piece.append(listed[pl.ds(at, slots, stride=PITCH), :])
                a, b, c, d = piece
                b = pltpu.roll(b, 96, 1)
                c = pltpu.roll(c, 64, 1)
                d = pltpu.roll(d, 32, 1)
                first = jnp.where(lane < 96, a, b)
                second = jnp.where(lane < 64, b, c)
                third = jnp.where(lane < 32, c, d)
                block.append(jnp.concatenate([first, second, third], axis=1))
            rows_ref[dest] = jnp.concatenate(block, axis=0).astype(jnp.bfloat16)
            return carry

        lax.fori_loop(0, dests, relayout, 0, unroll=4)

    fill(0, rounds[0])
    for number in range(1, len(rounds)):
        pl.when(slot_ref[chans] > number * slots)(
            functools.partial(fill, number, rounds[number])
        )


def left_kernel(chans, depth, turned_ref, left_ref):
    lane = lax.broadcasted_iota(jnp.int32, (chans, LANES), 1)

    def one(g, carry):
        stack = []
        for half in range(2):
            real = turned_ref[pl.ds(half * HALF + g, chans, stride=PITCH), :]
            ahead = pltpu.roll(real, depth // 2, 1)
            back = pltpu.roll(real, LANES - depth // 2, 1)
            stack += [real, jnp.where(lane < depth // 2, -back, ahead)]
        left_ref[g] = jnp.concatenate(stack, axis=0).astype(jnp.bfloat16)
        return carry

    lax.fori_loop(0, HALF, one, 0, unroll=8)


def pick_kernel(slots, base, place_ref, rows_ref, out_ref):
    sources = place_ref.shape[0]
    dests, height, width = rows_ref.shape
    groups, depth, _ = out_ref.shape
    rows = rows_ref[...].reshape(dests * height, width)
    ids = lax.broadcasted_iota(jnp.int32, (sources, dests * height), 1)
    place = place_ref[...] - base
    inside = (place >= 0) & (place < dests * slots)
    spot = place // slots * height + place % slots
    for pair in range(groups // 2):
        hit = inside & (ids == spot + pair * slots)
        onehot = jnp.where(hit, 1.0, 0.0).astype(jnp.bfloat16)
        turned = jnp.dot(onehot, rows, preferred_element_type=jnp.float32).T
        for j in range(2):
            low = turned[(2 * j) * depth : (2 * j + 1) * depth]
            high = turned[(2 * j + 1) * depth : (2 * j + 2) * depth]
            out_ref[pair * 2 + j] = jnp.concatenate([low, high], axis=1).astype(jnp.bfloat16)


def products(n, origins, me_ref, left_ref, pieces, held):
    rows = left_ref.shape[1]
    depth, width = pieces[0].shape[-2:]
    groups = HALF // n
    sources = width // 2
    outs = rows // 2
    me = me_ref[0]
    lane = lax.broadcasted_iota(jnp.int32, (outs, width), 1)
    for piece, names in zip(pieces, origins):
        for place, (flip, index) in enumerate(names):
            g = (me ^ flip) * groups + index
            both = jnp.dot(left_ref[g][:, :depth], piece[place], preferred_element_type=jnp.float32)
            mine = jnp.where(lane < sources, both[:outs], both[outs:])
            held[pl.ds(g, outs, stride=HALF_PITCH), :] = mine


def partial_kernel(n, origins, chained, me_ref, left_ref, *refs):
    products(n, origins, me_ref, left_ref, refs[chained:-1], refs[-1])


def correlate_kernel(scale, n, origins, sources, me_ref, left_ref, _, *refs):
    pieces, (out_ref, held, turned_ref, sems) = refs[:-4], refs[-4:]
    products(n, origins, me_ref, left_ref, pieces, held)
    outs = held.shape[0] // HALF_PITCH
    chans = outs // 2
    size = sources * chans
    copies = []
    for part in range(2):
        for c in range(chans):
            base = (part * chans + c) * HALF_PITCH
            turned = held[base : base + HALF, :].T * scale
            rows_at = pl.ds(part * size + c, sources, stride=chans)
            for half in range(2):
                turned_ref.at[half][rows_at, :] = turned[half * sources : (half + 1) * sources]
        for half in range(2):
            span = pl.ds(part * size, size)
            copy = pltpu.make_async_copy(
                turned_ref.at[half, span],
                out_ref.at[span, pl.ds(half * HALF, HALF)],
                sems.at[part, half],
            )
            copy.start()
            copies.append(copy)
    for copy in copies:
        copy.wait()


def gather_pieces(own, multiply, after_products):
    n = lax.axis_size("chan")
    groups = own.shape[0]
    cut = max(1, groups * 3 // 4)
    most, rest = list(range(cut)), list(range(cut, groups))
    core, x, y = 1, 2, 4
    column = [8 * k for k in range(1, n // 8)]
    place = {}

    def keep(array, names):
        for i, name in enumerate(names):
            place[name] = (array, i)
        return array, names

    def pack(names):
        parts = []
        for name in names:
            array, i = place[name]
            if parts and parts[-1][0] is array and parts[-1][2] == i:
                parts[-1][2] = i + 1
            else:
                parts.append([array, i, i + 1])
        blocks = [array[i:j] for array, i, j in parts]
        return blocks[0] if len(blocks) == 1 else jnp.concatenate(blocks, axis=0)

    def send(names, flip):
        route = [(i, i ^ flip) for i in range(n)]
        return lax.ppermute(pack(names), "chan", route), [(f ^ flip, g) for f, g in names]

    def lists(pairs):
        return [array for array, _ in pairs], [names for _, names in pairs]

    everything = [(f, g) for f in range(0, n, 2) for g in range(groups)]
    near = [keep(own, [(0, g) for g in range(groups)])]
    first_x, first_y = most[:1] + rest, most[1:2] + rest
    far = [send([(0, g) for g in most], flip) for flip in column]
    first = [send([(0, g) for g in first_x], x), send([(0, g) for g in first_y], y)] + far
    arrays = lax.optimization_barrier(lists(first)[0])
    near += [keep(array, names) for array, (_, names) in zip(arrays, first)]

    from_far = [(flip, g) for flip in column for g in most]
    other_x = [(0, g) for g in range(groups) if g not in first_x]
    other_y = [(0, g) for g in range(groups) if g not in first_y]
    mid = [
        send(from_far + other_x + [(y, g) for g in first_y], x),
        send(from_far + other_y + [(x, g) for g in most[:1]], y),
    ]
    mid += [send([(f, g) for f in (0, x, y) for g in rest], flip) for flip in column]
    multiply(*lists(near))
    arrays = after_products(*lists(mid)[0])
    mid = [keep(array, names) for array, (_, names) in zip(arrays, mid)]

    lacking = [name for name in everything if name not in place]
    by_x, by_y = lacking[::2], lacking[1::2]
    last = [send([(f ^ x, g) for f, g in by_x], x), send([(f ^ y, g) for f, g in by_y], y)]
    known = [name for pair in near + mid for name in pair[1]]
    theirs = send(known, core)
    multiply(*lists(mid))
    arrays = after_products(*lists(last)[0])
    last = [keep(array, names) for array, (_, names) in zip(arrays, last)]
    assert sorted(place) == everything
    final = send(by_x + by_y, core)
    multiply(*lists([theirs] + last))
    return lists([final])


def plan_slots(source_index, chans, slots):
    n = lax.axis_size("chan")
    channels = jnp.arange(n * chans, dtype=jnp.int32)
    hits = source_index[:, None] == channels[None, :]
    listed = jnp.any(hits, axis=0).reshape(n, chans).astype(jnp.int32)
    below = (jnp.arange(chans)[:, None] < jnp.arange(chans)[None, :]).astype(jnp.int32)
    rank = jnp.sum(listed[:, :, None] * below[None], axis=1)
    device = jnp.arange(n, dtype=jnp.int32)[:, None]
    place = (rank // slots * n + device) * slots + rank % slots
    places = jnp.sum(jnp.where(hits, place.reshape(1, -1), 0), axis=1, keepdims=True)
    most = jnp.max(jnp.sum(listed, axis=1))
    mine = device == lax.axis_index("chan")
    order = jnp.arange(chans, dtype=jnp.int32)
    is_slot = (mine & (listed > 0))[:, :, None] & (rank[:, :, None] == order)
    held = jnp.sum(jnp.where(is_slot, order[None, :, None], 0), axis=(0, 1))
    return jnp.concatenate([held, most[None]]), places, most


def per_device(traces, source_index):
    chans, wins, length = traces.shape
    n = lax.axis_size("chan")
    sources = source_index.shape[0]
    route = [(i + 1, i) for i in range(n - 1)]
    halo = lax.ppermute(traces[:GAUGE], "chan", route)
    table = jnp.asarray(make_table(length))
    band, inv = make_band()
    band, inv = jnp.asarray(band), jnp.asarray(inv)
    steps = chans // GAUGE
    depth = 2 * wins
    row_width = HALF * 2 * depth // n
    block = (GAUGE, wins, length)
    vmem = pl.BlockSpec(memory_space=pltpu.VMEM)
    smem = pl.BlockSpec(memory_space=pltpu.SMEM)
    consts = [vmem] * 3
    params = pltpu.CompilerParams(vmem_limit_bytes=VMEM_LIMIT)
    pairs = HALF // n // 2
    slots = chans // pairs
    slot_list, places, most = plan_slots(source_index, chans, slots)
    turned = jax.ShapeDtypeStruct((chans * PITCH, LANES), jnp.float32)
    some = pl.pallas_call(
        whiten_kernel,
        grid=(steps - 1,),
        in_specs=[
            pl.BlockSpec(block, lambda i: (i, 0, 0)),
            pl.BlockSpec(block, lambda i: (i + 1, 0, 0)),
            *consts,
        ],
        out_specs=vmem,
        out_shape=turned,
        compiler_params=params,
        cost_estimate=pl.CostEstimate(
            flops=2 * (chans - GAUGE) * wins * (length + F // 2) * 2 * F,
            bytes_accessed=8 * 1024 * 1024,
            transcendentals=0,
        ),
        name="whiten",
    )(traces, traces, table, band, inv)
    rows_shape = jax.ShapeDtypeStruct((n, chans, row_width // pairs), jnp.bfloat16)
    spectra, *rounds = pl.pallas_call(
        functools.partial(finish_kernel, chans, slots),
        grid=(1,),
        in_specs=[
            smem,
            pl.BlockSpec(block, lambda i: (steps - 1, 0, 0)),
            vmem,
            *consts,
            vmem,
        ],
        out_specs=[vmem] * (1 + pairs),
        out_shape=[turned] + [rows_shape] * pairs,
        scratch_shapes=[pltpu.VMEM((slots * PITCH, LANES), jnp.float32)],
        input_output_aliases={6: 0},
        compiler_params=params,
        name="finish",
    )(slot_list, traces, halo, table, band, inv, some)

    def exchange(number, rows):
        rows = lax.all_to_all(rows, "chan", 0, 0, tiled=True)
        return pl.pallas_call(
            functools.partial(pick_kernel, slots, number * n * slots),
            out_shape=jax.ShapeDtypeStruct((HALF // n, depth, 2 * sources), jnp.bfloat16),
            compiler_params=params,
            name="pick",
        )(places, rows)

    picked = exchange(0, rounds[0])
    for number in range(1, pairs):
        picked = lax.cond(
            most > number * slots,
            lambda p, r, number=number: p + exchange(number, r),
            lambda p, r: p,
            picked,
            rounds[number],
        )
    picked, spectra = lax.optimization_barrier((picked, spectra))
    left = pl.pallas_call(
        functools.partial(left_kernel, chans, depth),
        in_specs=[vmem],
        out_specs=vmem,
        out_shape=jax.ShapeDtypeStruct((HALF, 4 * chans, LANES), jnp.bfloat16),
        compiler_params=params,
        cost_estimate=pl.CostEstimate(
            flops=10 * 1000 * 1000, bytes_accessed=8 * 1024 * 1024, transcendentals=0
        ),
        name="left",
    )(spectra)
    me = lax.axis_index("chan").astype(jnp.int32).reshape(1)
    total_windows = wins * lax.axis_size("win")
    held_shape = jax.ShapeDtypeStruct((2 * chans * HALF_PITCH, LANES), jnp.float32)
    held = []

    def multiply(pieces, origins):
        held[:] = [
            pl.pallas_call(
                functools.partial(partial_kernel, n, origins, len(held)),
                in_specs=[smem, vmem] + [vmem] * (len(held) + len(pieces)),
                out_specs=vmem,
                out_shape=held_shape,
                input_output_aliases={2: 0} if held else {},
                compiler_params=params,
                cost_estimate=pl.CostEstimate(
                    flops=100 * 1000 * 1000, bytes_accessed=4 * 1024 * 1024, transcendentals=0
                ),
                name="products",
            )(me, left, *held, *pieces)
        ]

    def after_products(*arrays):
        *arrays, held[0] = lax.optimization_barrier((*arrays, held[0]))
        return arrays

    pieces, origins = gather_pieces(picked, multiply, after_products)
    flat, _ = pl.pallas_call(
        functools.partial(correlate_kernel, 1.0 / total_windows, n, origins, sources),
        in_specs=[smem, vmem, vmem] + [vmem] * len(pieces),
        out_specs=[pl.BlockSpec(memory_space=pl.ANY), vmem],
        out_shape=[jax.ShapeDtypeStruct((2 * sources * chans, F), jnp.float32), held_shape],
        scratch_shapes=[
            pltpu.VMEM((2, 2 * sources * chans, HALF), jnp.float32),
            pltpu.SemaphoreType.DMA((2, 2)),
        ],
        input_output_aliases={2: 1},
        compiler_params=params,
        name="correlate",
    )(me, left, *held, *pieces)
    stack = flat.reshape(2, sources, chans, F)
    if lax.axis_size("win") == 1:
        return stack
    return lax.psum_scatter(stack, "win", scatter_dimension=1, tiled=True)


def solution(mesh):
    return jax.shard_map(
        per_device,
        mesh=mesh,
        in_specs=(P("chan", "win", None), P()),
        out_specs=P(None, "win", "chan", None),
        check_vma=False,
    )
```

```python
import functools
import math

import jax
import jax.numpy as jnp
import ml_dtypes
import numpy as np
from jax import lax
from jax.experimental import pallas as pl
from jax.experimental.pallas import tpu as pltpu
from jax.sharding import PartitionSpec as P

F = 256
HALF = 128
F0 = 1
K = 64
GAUGE = 4
SHIFT = 2
LANES = 128
PITCH = F + 8
HALF_PITCH = HALF + 8
VMEM_LIMIT = 24 * 1024 * 1024


def make_table(length):
    times = np.arange(length, dtype=np.int64)[:, None]
    bins = np.arange(F, dtype=np.int64)[None, :] + F0
    phase = (times * bins % length).astype(np.float32) * np.float32(2.0 * math.pi / length)
    phase = phase.astype(np.float64)
    return np.concatenate([np.cos(phase), -np.sin(phase)], axis=1).astype(ml_dtypes.bfloat16)


def make_band():
    rows = np.arange(F)[:, None]
    cols = np.arange(F)[None, :]
    return (np.abs(rows - cols) <= K).astype(ml_dtypes.bfloat16)


def owner_of(channel, chans, n):
    shifted = channel + SHIFT
    owner = jnp.minimum(lax.div(shifted, jnp.int32(chans)), n - 1)
    return owner, shifted - owner * chans


def whiten_block(cur, upper, table_ref, band_ref, turned_ref, blocks):
    chans, wins, length = cur.shape
    rows = chans * wins
    diff = (upper.astype(jnp.float32) - cur.astype(jnp.float32)).reshape(rows, length)
    power = jnp.sum(diff * diff, axis=1, keepdims=True) * (1.0 / length)
    normed = (diff * lax.rsqrt(power + 1e-05)).astype(jnp.bfloat16)
    spec = jnp.dot(normed, table_ref[...], preferred_element_type=jnp.float32)
    real = spec[:, :F]
    imag = spec[:, F:]
    magnitude = jnp.sqrt(real * real + imag * imag).astype(jnp.bfloat16)
    bins = lax.broadcasted_iota(jnp.int32, (1, F), 1)
    counts = (jnp.minimum(bins, K) + jnp.minimum(F - 1 - bins, K) + 1).astype(jnp.float32)
    smooth = jnp.dot(magnitude, band_ref[...], preferred_element_type=jnp.float32) / counts
    gain = 1.0 / (smooth + 1e-06)
    white_re = (real * gain).astype(jnp.bfloat16).astype(jnp.float32)
    white_im = (imag * gain).astype(jnp.bfloat16).astype(jnp.float32)
    pad = jnp.zeros((LANES - 2 * wins, F), jnp.float32)
    for c, block in enumerate(blocks):
        mine = slice(c * wins, (c + 1) * wins)
        both = jnp.concatenate([white_re[mine], white_im[mine], pad], axis=0)
        turned_ref[block * PITCH : block * PITCH + F, :] = both.T


def whiten_kernel(traces_ref, table_ref, band_ref, turned_ref):
    chans = traces_ref.shape[0]
    for c in range(0, chans - GAUGE, GAUGE):
        cur, upper = traces_ref[c : c + GAUGE], traces_ref[c + GAUGE : c + 2 * GAUGE]
        blocks = range(c + SHIFT, c + GAUGE + SHIFT)
        whiten_block(cur, upper, table_ref, band_ref, turned_ref, blocks)
    cur = traces_ref[chans - SHIFT :]
    whiten_block(cur, jnp.zeros_like(cur), table_ref, band_ref, turned_ref, range(chans, chans + SHIFT))


def finish_kernel(
    n, slots, me_ref, index_ref, before_ref, after_ref, traces_ref, table_ref, band_ref, _, *refs
):
    turned_ref, back_ref, rounds, (listed, slot_ref) = refs[0], refs[1], refs[2:-2], refs[-2:]
    chans = traces_ref.shape[0]
    mine = jnp.int32(0)
    for s in range(index_ref.shape[0]):
        owner, block = owner_of(index_ref[s], chans, n)
        mine = mine | jnp.where(owner == me_ref[0], lax.shift_left(jnp.int32(1), block), 0)
    for block in range(chans + SHIFT):
        slot_ref[block] = 0
    count = jnp.int32(0)
    for block in range(chans + SHIFT):
        slot_ref[count] = block
        count = count + (lax.shift_right_logical(mine, block) & 1)
    cur = jnp.concatenate([before_ref[...], traces_ref[chans - GAUGE : chans - SHIFT]], axis=0)
    upper = jnp.concatenate([traces_ref[GAUGE - SHIFT : GAUGE], after_ref[...]], axis=0)
    blocks = [*range(SHIFT), *range(chans - SHIFT, chans)]
    whiten_block(cur, upper, table_ref, band_ref, turned_ref, blocks)
    for block in range(SHIFT):
        back = turned_ref[block * PITCH : block * PITCH + F, :]
        back_ref[block * F : (block + 1) * F, :] = back.astype(jnp.bfloat16)
    dests, _, width = rounds[0].shape
    pairs = HALF // dests // 2
    lane = lax.broadcasted_iota(jnp.int32, (slots, LANES), 1)

    def fill(number, rows_ref):
        for k in range(slots):
            channel = slot_ref[number * slots + k]
            listed[k * PITCH : k * PITCH + F, :] = turned_ref[pl.ds(channel * PITCH, F), :]

        def relayout(dest, carry):
            block = []
            for pair in range(pairs):
                piece = []
                for j in range(2):
                    for half in range(2):
                        at = half * HALF + (dest * pairs + pair) * 2 + j
                        piece.append(listed[pl.ds(at, slots, stride=PITCH), :])
                a, b, c, d = piece
                b = pltpu.roll(b, 96, 1)
                c = pltpu.roll(c, 64, 1)
                d = pltpu.roll(d, 32, 1)
                first = jnp.where(lane < 96, a, b)
                second = jnp.where(lane < 64, b, c)
                third = jnp.where(lane < 32, c, d)
                block.append(jnp.concatenate([first, second, third], axis=1))
            rows_ref[dest] = jnp.concatenate(block, axis=0).astype(jnp.bfloat16)
            return carry

        lax.fori_loop(0, dests, relayout, 0, unroll=4)

    def clear(rows_ref):
        rows_ref[...] = jnp.zeros_like(rows_ref)

    fill(0, rounds[0])
    for number in range(1, len(rounds)):
        more = count > number * slots
        pl.when(more)(functools.partial(fill, number, rounds[number]))
        pl.when(jnp.logical_not(more))(functools.partial(clear, rounds[number]))


def left_kernel(n, chans, depth, me_ref, back_ref, _, left_ref, turned_ref):
    @pl.when(me_ref[0] < n - 1)
    def _():
        for block in range(SHIFT):
            at = (chans + block) * PITCH
            turned_ref[at : at + F, :] = back_ref[block * F : (block + 1) * F, :].astype(jnp.float32)

    lane = lax.broadcasted_iota(jnp.int32, (chans, LANES), 1)

    def one(g, carry):
        stack = []
        for half in range(2):
            at = SHIFT * PITCH + half * HALF + g
            real = turned_ref[pl.ds(at, chans, stride=PITCH), :]
            ahead = pltpu.roll(real, depth // 2, 1)
            back = pltpu.roll(real, LANES - depth // 2, 1)
            stack += [real, jnp.where(lane < depth // 2, -back, ahead)]
        left_ref[g] = jnp.concatenate(stack, axis=0).astype(jnp.bfloat16)
        return carry

    lax.fori_loop(0, HALF, one, 0, unroll=8)


def pick_kernel(slots, base, place_ref, rows_ref, out_ref):
    sources = place_ref.shape[0]
    dests, height, width = rows_ref.shape
    groups, depth, _ = out_ref.shape
    rows = rows_ref[...].reshape(dests * height, width)
    ids = lax.broadcasted_iota(jnp.int32, (sources, dests * height), 1)
    place = place_ref[...] - base
    inside = (place >= 0) & (place < dests * slots)
    spot = place // slots * height + place % slots
    for pair in range(groups // 2):
        hit = inside & (ids == spot + pair * slots)
        onehot = jnp.where(hit, 1.0, 0.0).astype(jnp.bfloat16)
        turned = jnp.dot(onehot, rows, preferred_element_type=jnp.float32).T
        for j in range(2):
            low = turned[(2 * j) * depth : (2 * j + 1) * depth]
            high = turned[(2 * j + 1) * depth : (2 * j + 2) * depth]
            out_ref[pair * 2 + j] = jnp.concatenate([low, high], axis=1).astype(jnp.bfloat16)


def products(n, origins, me_ref, left_ref, pieces, held):
    rows = left_ref.shape[1]
    depth, width = pieces[0].shape[-2:]
    groups = HALF // n
    sources = width // 2
    outs = rows // 2
    me = me_ref[0]
    lane = lax.broadcasted_iota(jnp.int32, (outs, width), 1)
    for piece, names in zip(pieces, origins):
        for place, (flip, index) in enumerate(names):
            g = (me ^ flip) * groups + index
            both = jnp.dot(left_ref[g][:, :depth], piece[place], preferred_element_type=jnp.float32)
            mine = jnp.where(lane < sources, both[:outs], both[outs:])
            held[pl.ds(g, outs, stride=HALF_PITCH), :] = mine


def partial_kernel(n, origins, chained, me_ref, left_ref, *refs):
    products(n, origins, me_ref, left_ref, refs[chained:-1], refs[-1])


def correlate_kernel(scale, n, origins, sources, me_ref, left_ref, _, *refs):
    pieces, (out_ref, held, turned_ref, sems) = refs[:-4], refs[-4:]
    products(n, origins, me_ref, left_ref, pieces, held)
    outs = held.shape[0] // HALF_PITCH
    chans = outs // 2
    size = sources * chans
    copies = []
    for part in range(2):
        for c in range(chans):
            base = (part * chans + c) * HALF_PITCH
            turned = held[base : base + HALF, :].T * scale
            rows_at = pl.ds(part * size + c, sources, stride=chans)
            for half in range(2):
                turned_ref.at[half][rows_at, :] = turned[half * sources : (half + 1) * sources]
        for half in range(2):
            span = pl.ds(part * size, size)
            copy = pltpu.make_async_copy(
                turned_ref.at[half, span],
                out_ref.at[span, pl.ds(half * HALF, HALF)],
                sems.at[part, half],
            )
            copy.start()
            copies.append(copy)
    for copy in copies:
        copy.wait()


def gather_pieces(own, multiply, after_products):
    n = lax.axis_size("chan")
    groups = own.shape[0]
    cut = max(1, groups * 3 // 4)
    most, rest = list(range(cut)), list(range(cut, groups))
    core, x, y = 1, 2, 4
    column = [8 * k for k in range(1, n // 8)]
    place = {}

    def keep(array, names):
        for i, name in enumerate(names):
            place[name] = (array, i)
        return array, names

    def pack(names):
        parts = []
        for name in names:
            array, i = place[name]
            if parts and parts[-1][0] is array and parts[-1][2] == i:
                parts[-1][2] = i + 1
            else:
                parts.append([array, i, i + 1])
        blocks = [array[i:j] for array, i, j in parts]
        return blocks[0] if len(blocks) == 1 else jnp.concatenate(blocks, axis=0)

    def send(names, flip):
        route = [(i, i ^ flip) for i in range(n)]
        return lax.ppermute(pack(names), "chan", route), [(f ^ flip, g) for f, g in names]

    def lists(pairs):
        return [array for array, _ in pairs], [names for _, names in pairs]

    everything = [(f, g) for f in range(0, n, 2) for g in range(groups)]
    near = [keep(own, [(0, g) for g in range(groups)])]
    first_x, first_y = most[:1] + rest, most[1:2] + rest
    far = [send([(0, g) for g in most], flip) for flip in column]
    first = [send([(0, g) for g in first_x], x), send([(0, g) for g in first_y], y)] + far
    arrays = lax.optimization_barrier(lists(first)[0])
    near += [keep(array, names) for array, (_, names) in zip(arrays, first)]

    from_far = [(flip, g) for flip in column for g in most]
    other_x = [(0, g) for g in range(groups) if g not in first_x]
    other_y = [(0, g) for g in range(groups) if g not in first_y]
    mid = [
        send(from_far + other_x + [(y, g) for g in first_y], x),
        send(from_far + other_y + [(x, g) for g in most[:1]], y),
    ]
    mid += [send([(f, g) for f in (0, x, y) for g in rest], flip) for flip in column]
    multiply(*lists(near))
    arrays = after_products(*lists(mid)[0])
    mid = [keep(array, names) for array, (_, names) in zip(arrays, mid)]

    lacking = [name for name in everything if name not in place]
    by_x, by_y = lacking[::2], lacking[1::2]
    last = [send([(f ^ x, g) for f, g in by_x], x), send([(f ^ y, g) for f, g in by_y], y)]
    known = [name for pair in near + mid for name in pair[1]]
    theirs = send(known, core)
    multiply(*lists(mid))
    arrays = after_products(*lists(last)[0])
    last = [keep(array, names) for array, (_, names) in zip(arrays, last)]
    assert sorted(place) == everything
    final = send(by_x + by_y, core)
    multiply(*lists([theirs] + last))
    return lists([final])


def plan_places(source_index, chans, slots):
    n = lax.axis_size("chan")
    width = chans + SHIFT
    owner, block = owner_of(source_index, chans, n)
    hits = (owner * width + block)[:, None] == jnp.arange(n * width, dtype=jnp.int32)[None, :]
    listed = jnp.any(hits, axis=0).reshape(n, width).astype(jnp.int32)
    below = (jnp.arange(width)[:, None] < jnp.arange(width)[None, :]).astype(jnp.int32)
    rank = jnp.sum(listed[:, :, None] * below[None], axis=1)
    device = jnp.arange(n, dtype=jnp.int32)[:, None]
    place = (rank // slots * n + device) * slots + rank % slots
    places = jnp.sum(jnp.where(hits, place.reshape(1, -1), 0), axis=1, keepdims=True)
    return places, jnp.max(jnp.sum(listed, axis=1))


def per_device(traces, source_index):
    chans, wins, length = traces.shape
    n = lax.axis_size("chan")
    sources = source_index.shape[0]
    after = lax.ppermute(traces[:SHIFT], "chan", [(i + 1, i) for i in range(n - 1)])
    before = lax.ppermute(traces[chans - SHIFT :], "chan", [(i, i + 1) for i in range(n - 1)])
    me = lax.axis_index("chan").astype(jnp.int32).reshape(1)
    table, band = jnp.asarray(make_table(length)), jnp.asarray(make_band())
    depth = 2 * wins
    row_width = HALF * 2 * depth // n
    vmem = pl.BlockSpec(memory_space=pltpu.VMEM)
    smem = pl.BlockSpec(memory_space=pltpu.SMEM)
    params = pltpu.CompilerParams(vmem_limit_bytes=VMEM_LIMIT)
    pairs = HALF // n // 2
    slots = 16 // pairs
    turns = -(-(chans + SHIFT) // slots)
    turned = jax.ShapeDtypeStruct(((chans + SHIFT) * PITCH, LANES), jnp.float32)
    some = pl.pallas_call(
        whiten_kernel,
        in_specs=[vmem] * 3,
        out_specs=vmem,
        out_shape=turned,
        compiler_params=params,
        cost_estimate=pl.CostEstimate(
            flops=2 * chans * wins * (length + F // 2) * 2 * F,
            bytes_accessed=8 * 1024 * 1024,
            transcendentals=0,
        ),
        name="whiten",
    )(traces, table, band)
    rows_shape = jax.ShapeDtypeStruct((n, slots * pairs, row_width // pairs), jnp.bfloat16)
    back_shape = jax.ShapeDtypeStruct((SHIFT * F, LANES), jnp.bfloat16)
    spectra, back, *rounds = pl.pallas_call(
        functools.partial(finish_kernel, n, slots),
        in_specs=[smem] * 2 + [vmem] * 6,
        out_specs=[vmem] * (2 + turns),
        out_shape=[turned, back_shape] + [rows_shape] * turns,
        scratch_shapes=[
            pltpu.VMEM((slots * PITCH, LANES), jnp.float32),
            pltpu.SMEM((chans + SHIFT + 1,), jnp.int32),
        ],
        input_output_aliases={7: 0},
        compiler_params=params,
        name="finish",
    )(me, source_index, before, after, traces, table, band, some)
    rounds[0], late_index = lax.optimization_barrier((rounds[0], source_index))
    places, most = plan_places(late_index, chans, slots)

    def exchange(number, rows):
        rows = lax.all_to_all(rows, "chan", 0, 0, tiled=True)
        return pl.pallas_call(
            functools.partial(pick_kernel, slots, number * n * slots),
            out_shape=jax.ShapeDtypeStruct((HALF // n, depth, 2 * sources), jnp.bfloat16),
            compiler_params=params,
            name="pick",
        )(places, rows)

    picked = exchange(0, rounds[0])
    for number in range(1, turns):
        picked = lax.cond(
            most > number * slots,
            lambda p, r, number=number: p + exchange(number, r),
            lambda p, r: p,
            picked,
            rounds[number],
        )
    picked, spectra = lax.optimization_barrier((picked, spectra))
    back = lax.ppermute(back, "chan", [(i + 1, i) for i in range(n - 1)])
    left, _ = pl.pallas_call(
        functools.partial(left_kernel, n, chans, depth),
        in_specs=[smem, vmem, vmem],
        out_specs=[vmem] * 2,
        out_shape=[jax.ShapeDtypeStruct((HALF, 4 * chans, LANES), jnp.bfloat16), turned],
        input_output_aliases={2: 1},
        compiler_params=params,
        cost_estimate=pl.CostEstimate(
            flops=10 * 1000 * 1000, bytes_accessed=8 * 1024 * 1024, transcendentals=0
        ),
        name="left",
    )(me, back, spectra)
    total_windows = wins * lax.axis_size("win")
    held_shape = jax.ShapeDtypeStruct((2 * chans * HALF_PITCH, LANES), jnp.float32)
    held = []

    def multiply(pieces, origins):
        held[:] = [
            pl.pallas_call(
                functools.partial(partial_kernel, n, origins, len(held)),
                in_specs=[smem, vmem] + [vmem] * (len(held) + len(pieces)),
                out_specs=vmem,
                out_shape=held_shape,
                input_output_aliases={2: 0} if held else {},
                compiler_params=params,
                cost_estimate=pl.CostEstimate(
                    flops=100 * 1000 * 1000, bytes_accessed=4 * 1024 * 1024, transcendentals=0
                ),
                name="products",
            )(me, left, *held, *pieces)
        ]

    def after_products(*arrays):
        *arrays, held[0] = lax.optimization_barrier((*arrays, held[0]))
        return arrays

    pieces, origins = gather_pieces(picked, multiply, after_products)
    flat, _ = pl.pallas_call(
        functools.partial(correlate_kernel, 1.0 / total_windows, n, origins, sources),
        in_specs=[smem, vmem, vmem] + [vmem] * len(pieces),
        out_specs=[pl.BlockSpec(memory_space=pl.ANY), vmem],
        out_shape=[jax.ShapeDtypeStruct((2 * sources * chans, F), jnp.float32), held_shape],
        scratch_shapes=[
            pltpu.VMEM((2, 2 * sources * chans, HALF), jnp.float32),
            pltpu.SemaphoreType.DMA((2, 2)),
        ],
        input_output_aliases={2: 1},
        compiler_params=params,
        name="correlate",
    )(me, left, *held, *pieces)
    stack = flat.reshape(2, sources, chans, F)
    if lax.axis_size("win") == 1:
        return stack
    return lax.psum_scatter(stack, "win", scatter_dimension=1, tiled=True)


def solution(mesh):
    return jax.shard_map(
        per_device,
        mesh=mesh,
        in_specs=(P("chan", "win", None), P()),
        out_specs=P(None, "win", "chan", None),
        check_vma=False,
    )
```

```python
import functools
import math

import jax
import jax.numpy as jnp
import ml_dtypes
import numpy as np
from jax import lax
from jax.experimental import pallas as pl
from jax.experimental.pallas import tpu as pltpu
from jax.sharding import PartitionSpec as P

F = 256
HALF = 128
F0 = 1
K = 64
GAUGE = 4
LANES = 128
PITCH = F + 8
HALF_PITCH = HALF + 8
VMEM_LIMIT = 24 * 1024 * 1024


def make_table(length):
    times = np.arange(length, dtype=np.int64)[:, None]
    bins = np.arange(F, dtype=np.int64)[None, :] + F0
    phase = (times * bins % length).astype(np.float32) * np.float32(2.0 * math.pi / length)
    phase = phase.astype(np.float64)
    return np.concatenate([np.cos(phase), -np.sin(phase)], axis=1).astype(ml_dtypes.bfloat16)


def make_band():
    rows = np.arange(F)[:, None]
    cols = np.arange(F)[None, :]
    return (np.abs(rows - cols) <= K).astype(ml_dtypes.bfloat16)


def whiten_block(cur, upper, table_ref, band_ref, turned_ref, first):
    chans, wins, length = cur.shape
    rows = chans * wins
    diff = (upper.astype(jnp.float32) - cur.astype(jnp.float32)).reshape(rows, length)
    power = jnp.sum(diff * diff, axis=1, keepdims=True) * (1.0 / length)
    normed = (diff * lax.rsqrt(power + 1e-05)).astype(jnp.bfloat16)
    spec = jnp.dot(normed, table_ref[...], preferred_element_type=jnp.float32)
    real = spec[:, :F]
    imag = spec[:, F:]
    magnitude = jnp.sqrt(real * real + imag * imag).astype(jnp.bfloat16)
    bins = lax.broadcasted_iota(jnp.int32, (1, F), 1)
    counts = (jnp.minimum(bins, K) + jnp.minimum(F - 1 - bins, K) + 1).astype(jnp.float32)
    smooth = jnp.dot(magnitude, band_ref[...], preferred_element_type=jnp.float32) / counts
    gain = 1.0 / (smooth + 1e-06)
    white_re = (real * gain).astype(jnp.bfloat16).astype(jnp.float32)
    white_im = (imag * gain).astype(jnp.bfloat16).astype(jnp.float32)
    pad = jnp.zeros((LANES - 2 * wins, F), jnp.float32)
    for c in range(chans):
        mine = slice(c * wins, (c + 1) * wins)
        both = jnp.concatenate([white_re[mine], white_im[mine], pad], axis=0)
        turned_ref[(first + c) * PITCH : (first + c) * PITCH + F, :] = both.T


def list_slots(chans, me_ref, index_ref, slot_ref):
    mine = jnp.int32(0)
    for s in range(index_ref.shape[0]):
        local = index_ref[s] - me_ref[0] * chans
        bit = lax.shift_left(jnp.int32(1), jnp.clip(local, 0, chans - 1))
        mine = mine | jnp.where((local >= 0) & (local < chans), bit, 0)
    early = count = jnp.int32(0)
    for c in range(chans):
        slot_ref[count] = c
        count = count + (lax.shift_right_logical(mine, c) & 1)
        if c < chans - GAUGE:
            early = count
    return early, count


def lay_out(slot, channel, turned_ref, stage_ref, height, slots):
    dests = stage_ref.shape[1] // height
    per_dest = HALF // dests
    lane = lax.broadcasted_iota(jnp.int32, (dests, LANES), 1)
    for pair in range(per_dest // 2):
        piece = []
        for j in range(2):
            for half in range(2):
                at = channel * PITCH + half * HALF + pair * 2 + j
                piece.append(turned_ref[pl.ds(at, dests, stride=per_dest), :])
        a, b, c, d = piece
        b = pltpu.roll(b, 96, 1)
        c = pltpu.roll(c, 64, 1)
        d = pltpu.roll(d, 32, 1)
        rows_at = pl.ds(pair * slots + slot, dests, stride=height)
        stage_ref.at[0][rows_at, :] = jnp.where(lane < 96, a, b)
        stage_ref.at[1][rows_at, :] = jnp.where(lane < 64, b, c)
        stage_ref.at[2][rows_at, :] = jnp.where(lane < 32, c, d)


def whiten_kernel(
    height, slots, me_ref, index_ref, traces_ref, table_ref, band_ref, turned_ref, stage_ref, slot_ref
):
    chans = traces_ref.shape[0]
    stage_ref[...] = jnp.zeros_like(stage_ref)
    early, _ = list_slots(chans, me_ref, index_ref, slot_ref)
    for c in range(0, chans - GAUGE, GAUGE):
        cur, upper = traces_ref[c : c + GAUGE], traces_ref[c + GAUGE : c + 2 * GAUGE]
        whiten_block(cur, upper, table_ref, band_ref, turned_ref, c)

    def one(slot, carry):
        lay_out(slot, slot_ref[slot], turned_ref, stage_ref, height, slots)
        return carry

    lax.fori_loop(0, jnp.minimum(early, slots), one, 0)


def finish_kernel(
    height, slots, me_ref, index_ref, traces_ref, halo_ref, table_ref, band_ref, _, __, *refs
):
    turned_ref, stage_ref, rounds, slot_ref = refs[0], refs[1], refs[2:-1], refs[-1]
    chans = traces_ref.shape[0]
    early, count = list_slots(chans, me_ref, index_ref, slot_ref)
    cur = traces_ref[chans - GAUGE :]
    whiten_block(cur, halo_ref[...], table_ref, band_ref, turned_ref, chans - GAUGE)

    def fill(first, start, rows_ref):
        def one(slot, carry):
            channel = slot_ref[first + slot]
            lay_out(slot, channel, turned_ref, stage_ref, height, slots)
            return carry

        lax.fori_loop(start, jnp.minimum(count - first, slots), one, 0)
        for dest in range(rows_ref.shape[0]):
            for tile in range(3):
                block = stage_ref[tile, dest * height : (dest + 1) * height, :]
                rows_ref[dest, :, tile * LANES : (tile + 1) * LANES] = block.astype(jnp.bfloat16)

    def clear(rows_ref):
        rows_ref[...] = jnp.zeros_like(rows_ref)

    fill(0, early, rounds[0])
    for number in range(1, len(rounds)):
        more = count > number * slots
        pl.when(more)(functools.partial(fill, number * slots, 0, rounds[number]))
        pl.when(jnp.logical_not(more))(functools.partial(clear, rounds[number]))


def left_kernel(chans, depth, turned_ref, left_ref):
    lane = lax.broadcasted_iota(jnp.int32, (chans, LANES), 1)

    def one(g, carry):
        stack = []
        for half in range(2):
            real = turned_ref[pl.ds(half * HALF + g, chans, stride=PITCH), :]
            ahead = pltpu.roll(real, depth // 2, 1)
            back = pltpu.roll(real, LANES - depth // 2, 1)
            stack += [real, jnp.where(lane < depth // 2, -back, ahead)]
        left_ref[g] = jnp.concatenate(stack, axis=0).astype(jnp.bfloat16)
        return carry

    lax.fori_loop(0, HALF, one, 0, unroll=8)


def pick_kernel(slots, base, place_ref, rows_ref, out_ref):
    sources = place_ref.shape[0]
    dests, height, width = rows_ref.shape
    groups, depth, _ = out_ref.shape
    rows = rows_ref[...].reshape(dests * height, width)
    ids = lax.broadcasted_iota(jnp.int32, (sources, dests * height), 1)
    place = place_ref[...] - base
    inside = (place >= 0) & (place < dests * slots)
    spot = place // slots * height + place % slots
    for pair in range(groups // 2):
        hit = inside & (ids == spot + pair * slots)
        onehot = jnp.where(hit, 1.0, 0.0).astype(jnp.bfloat16)
        turned = jnp.dot(onehot, rows, preferred_element_type=jnp.float32).T
        for j in range(2):
            low = turned[(2 * j) * depth : (2 * j + 1) * depth]
            high = turned[(2 * j + 1) * depth : (2 * j + 2) * depth]
            out_ref[pair * 2 + j] = jnp.concatenate([low, high], axis=1).astype(jnp.bfloat16)


def products(n, origins, me_ref, left_ref, pieces, held):
    rows = left_ref.shape[1]
    depth, width = pieces[0].shape[-2:]
    groups = HALF // n
    sources = width // 2
    outs = rows // 2
    me = me_ref[0]
    lane = lax.broadcasted_iota(jnp.int32, (outs, width), 1)
    for piece, names in zip(pieces, origins):
        for place, (flip, index) in enumerate(names):
            g = (me ^ flip) * groups + index
            both = jnp.dot(left_ref[g][:, :depth], piece[place], preferred_element_type=jnp.float32)
            mine = jnp.where(lane < sources, both[:outs], both[outs:])
            held[pl.ds(g, outs, stride=HALF_PITCH), :] = mine


def partial_kernel(n, origins, chained, me_ref, left_ref, *refs):
    products(n, origins, me_ref, left_ref, refs[chained:-1], refs[-1])


def correlate_kernel(scale, n, origins, sources, me_ref, left_ref, _, *refs):
    pieces, (out_ref, held, turned_ref, sems) = refs[:-4], refs[-4:]
    products(n, origins, me_ref, left_ref, pieces, held)
    outs = held.shape[0] // HALF_PITCH
    chans = outs // 2
    size = sources * chans
    copies = []
    for part in range(2):
        for c in range(chans):
            base = (part * chans + c) * HALF_PITCH
            turned = held[base : base + HALF, :].T * scale
            rows_at = pl.ds(part * size + c, sources, stride=chans)
            for half in range(2):
                turned_ref.at[half][rows_at, :] = turned[half * sources : (half + 1) * sources]
        for half in range(2):
            span = pl.ds(part * size, size)
            copy = pltpu.make_async_copy(
                turned_ref.at[half, span],
                out_ref.at[span, pl.ds(half * HALF, HALF)],
                sems.at[part, half],
            )
            copy.start()
            copies.append(copy)
    for copy in copies:
        copy.wait()


def gather_pieces(own, multiply, after_products):
    n = lax.axis_size("chan")
    groups = own.shape[0]
    cut = max(1, groups * 3 // 4)
    most, rest = list(range(cut)), list(range(cut, groups))
    core, x, y = 1, 2, 4
    column = [8 * k for k in range(1, n // 8)]
    place = {}

    def keep(array, names):
        for i, name in enumerate(names):
            place[name] = (array, i)
        return array, names

    def pack(names):
        parts = []
        for name in names:
            array, i = place[name]
            if parts and parts[-1][0] is array and parts[-1][2] == i:
                parts[-1][2] = i + 1
            else:
                parts.append([array, i, i + 1])
        blocks = [array[i:j] for array, i, j in parts]
        return blocks[0] if len(blocks) == 1 else jnp.concatenate(blocks, axis=0)

    def send(names, flip):
        route = [(i, i ^ flip) for i in range(n)]
        return lax.ppermute(pack(names), "chan", route), [(f ^ flip, g) for f, g in names]

    def lists(pairs):
        return [array for array, _ in pairs], [names for _, names in pairs]

    everything = [(f, g) for f in range(0, n, 2) for g in range(groups)]
    near = [keep(own, [(0, g) for g in range(groups)])]
    first_x, first_y = most[:1] + rest, most[1:2] + rest
    far = [send([(0, g) for g in most], flip) for flip in column]
    first = [send([(0, g) for g in first_x], x), send([(0, g) for g in first_y], y)] + far
    arrays = lax.optimization_barrier(lists(first)[0])
    near += [keep(array, names) for array, (_, names) in zip(arrays, first)]

    from_far = [(flip, g) for flip in column for g in most]
    other_x = [(0, g) for g in range(groups) if g not in first_x]
    other_y = [(0, g) for g in range(groups) if g not in first_y]
    mid = [
        send(from_far + other_x + [(y, g) for g in first_y], x),
        send(from_far + other_y + [(x, g) for g in most[:1]], y),
    ]
    mid += [send([(f, g) for f in (0, x, y) for g in rest], flip) for flip in column]
    multiply(*lists(near))
    arrays = after_products(*lists(mid)[0])
    mid = [keep(array, names) for array, (_, names) in zip(arrays, mid)]

    lacking = [name for name in everything if name not in place]
    by_x, by_y = lacking[::2], lacking[1::2]
    last = [send([(f ^ x, g) for f, g in by_x], x), send([(f ^ y, g) for f, g in by_y], y)]
    known = [name for pair in near + mid for name in pair[1]]
    theirs = send(known, core)
    multiply(*lists(mid))
    arrays = after_products(*lists(last)[0])
    last = [keep(array, names) for array, (_, names) in zip(arrays, last)]
    assert sorted(place) == everything
    final = send(by_x + by_y, core)
    multiply(*lists([theirs] + last))
    return lists([final])


def plan_places(source_index, chans, slots):
    n = lax.axis_size("chan")
    channels = jnp.arange(n * chans, dtype=jnp.int32)
    hits = source_index[:, None] == channels[None, :]
    listed = jnp.any(hits, axis=0).reshape(n, chans).astype(jnp.int32)
    below = (jnp.arange(chans)[:, None] < jnp.arange(chans)[None, :]).astype(jnp.int32)
    rank = jnp.sum(listed[:, :, None] * below[None], axis=1)
    device = jnp.arange(n, dtype=jnp.int32)[:, None]
    place = (rank // slots * n + device) * slots + rank % slots
    places = jnp.sum(jnp.where(hits, place.reshape(1, -1), 0), axis=1, keepdims=True)
    return places, jnp.max(jnp.sum(listed, axis=1))


def per_device(traces, source_index):
    chans, wins, length = traces.shape
    n = lax.axis_size("chan")
    sources = source_index.shape[0]
    halo = lax.ppermute(traces[:GAUGE], "chan", [(i + 1, i) for i in range(n - 1)])
    me = lax.axis_index("chan").astype(jnp.int32).reshape(1)
    table, band = jnp.asarray(make_table(length)), jnp.asarray(make_band())
    depth = 2 * wins
    row_width = HALF * 2 * depth // n
    vmem = pl.BlockSpec(memory_space=pltpu.VMEM)
    smem = pl.BlockSpec(memory_space=pltpu.SMEM)
    params = pltpu.CompilerParams(vmem_limit_bytes=VMEM_LIMIT)
    pairs = HALF // n // 2
    slots = chans // pairs
    turned = jax.ShapeDtypeStruct((chans * PITCH, LANES), jnp.float32)
    stage = jax.ShapeDtypeStruct((3, n * chans, LANES), jnp.float32)
    slot_scratch = pltpu.SMEM((chans + 1,), jnp.int32)
    some, staged = pl.pallas_call(
        functools.partial(whiten_kernel, chans, slots),
        in_specs=[smem] * 2 + [vmem] * 3,
        out_specs=[vmem] * 2,
        out_shape=[turned, stage],
        scratch_shapes=[slot_scratch],
        compiler_params=params,
        cost_estimate=pl.CostEstimate(
            flops=2 * (chans - GAUGE) * wins * (length + F // 2) * 2 * F,
            bytes_accessed=8 * 1024 * 1024,
            transcendentals=0,
        ),
        name="whiten",
    )(me, source_index, traces, table, band)
    rows_shape = jax.ShapeDtypeStruct((n, chans, row_width // pairs), jnp.bfloat16)
    spectra, _, *rounds = pl.pallas_call(
        functools.partial(finish_kernel, chans, slots),
        in_specs=[smem] * 2 + [vmem] * 6,
        out_specs=[vmem] * (2 + pairs),
        out_shape=[turned, stage] + [rows_shape] * pairs,
        scratch_shapes=[slot_scratch],
        input_output_aliases={6: 0, 7: 1},
        compiler_params=params,
        name="finish",
    )(me, source_index, traces, halo, table, band, some, staged)
    rounds[0], late_index = lax.optimization_barrier((rounds[0], source_index))
    places, most = plan_places(late_index, chans, slots)

    def exchange(number, rows):
        rows = lax.all_to_all(rows, "chan", 0, 0, tiled=True)
        return pl.pallas_call(
            functools.partial(pick_kernel, slots, number * n * slots),
            out_shape=jax.ShapeDtypeStruct((HALF // n, depth, 2 * sources), jnp.bfloat16),
            compiler_params=params,
            name="pick",
        )(places, rows)

    picked = exchange(0, rounds[0])
    for number in range(1, pairs):
        picked = lax.cond(
            most > number * slots,
            lambda p, r, number=number: p + exchange(number, r),
            lambda p, r: p,
            picked,
            rounds[number],
        )
    picked, spectra = lax.optimization_barrier((picked, spectra))
    left = pl.pallas_call(
        functools.partial(left_kernel, chans, depth),
        in_specs=[vmem],
        out_specs=vmem,
        out_shape=jax.ShapeDtypeStruct((HALF, 4 * chans, LANES), jnp.bfloat16),
        compiler_params=params,
        cost_estimate=pl.CostEstimate(
            flops=10 * 1000 * 1000, bytes_accessed=8 * 1024 * 1024, transcendentals=0
        ),
        name="left",
    )(spectra)
    total_windows = wins * lax.axis_size("win")
    held_shape = jax.ShapeDtypeStruct((2 * chans * HALF_PITCH, LANES), jnp.float32)
    held = []

    def multiply(pieces, origins):
        held[:] = [
            pl.pallas_call(
                functools.partial(partial_kernel, n, origins, len(held)),
                in_specs=[smem, vmem] + [vmem] * (len(held) + len(pieces)),
                out_specs=vmem,
                out_shape=held_shape,
                input_output_aliases={2: 0} if held else {},
                compiler_params=params,
                cost_estimate=pl.CostEstimate(
                    flops=100 * 1000 * 1000, bytes_accessed=4 * 1024 * 1024, transcendentals=0
                ),
                name="products",
            )(me, left, *held, *pieces)
        ]

    def after_products(*arrays):
        *arrays, held[0] = lax.optimization_barrier((*arrays, held[0]))
        return arrays

    pieces, origins = gather_pieces(picked, multiply, after_products)
    flat, _ = pl.pallas_call(
        functools.partial(correlate_kernel, 1.0 / total_windows, n, origins, sources),
        in_specs=[smem, vmem, vmem] + [vmem] * len(pieces),
        out_specs=[pl.BlockSpec(memory_space=pl.ANY), vmem],
        out_shape=[jax.ShapeDtypeStruct((2 * sources * chans, F), jnp.float32), held_shape],
        scratch_shapes=[
            pltpu.VMEM((2, 2 * sources * chans, HALF), jnp.float32),
            pltpu.SemaphoreType.DMA((2, 2)),
        ],
        input_output_aliases={2: 1},
        compiler_params=params,
        name="correlate",
    )(me, left, *held, *pieces)
    stack = flat.reshape(2, sources, chans, F)
    if lax.axis_size("win") == 1:
        return stack
    return lax.psum_scatter(stack, "win", scatter_dimension=1, tiled=True)


def solution(mesh):
    return jax.shard_map(
        per_device,
        mesh=mesh,
        in_specs=(P("chan", "win", None), P()),
        out_specs=P(None, "win", "chan", None),
        check_vma=False,
    )
```

```python
import functools
import math

import jax
import jax.numpy as jnp
import ml_dtypes
import numpy as np
from jax import lax
from jax.experimental import pallas as pl
from jax.experimental.pallas import tpu as pltpu
from jax.sharding import PartitionSpec as P

F = 256
HALF = 128
F0 = 1
K = 64
GAUGE = 4
LANES = 128
PITCH = F + 8
HALF_PITCH = HALF + 8
VMEM_LIMIT = 24 * 1024 * 1024


def make_table(length):
    times = np.arange(length, dtype=np.int64)[:, None]
    bins = np.arange(F, dtype=np.int64)[None, :] + F0
    phase = (times * bins % length).astype(np.float32) * np.float32(2.0 * math.pi / length)
    phase = phase.astype(np.float64)
    return np.concatenate([np.cos(phase), -np.sin(phase)], axis=1).astype(ml_dtypes.bfloat16)


def make_band():
    rows = np.arange(F)[:, None]
    cols = np.arange(F)[None, :]
    return (np.abs(rows - cols) <= K).astype(ml_dtypes.bfloat16)


def whiten_block(cur, upper, table_ref, band_ref, turned_ref, first):
    chans, wins, length = cur.shape
    rows = chans * wins
    diff = (upper.astype(jnp.float32) - cur.astype(jnp.float32)).reshape(rows, length)
    power = jnp.sum(diff * diff, axis=1, keepdims=True) * (1.0 / length)
    normed = (diff * lax.rsqrt(power + 1e-05)).astype(jnp.bfloat16)
    spec = jnp.dot(normed, table_ref[...], preferred_element_type=jnp.float32)
    real = spec[:, :F]
    imag = spec[:, F:]
    magnitude = jnp.sqrt(real * real + imag * imag).astype(jnp.bfloat16)
    bins = lax.broadcasted_iota(jnp.int32, (1, F), 1)
    counts = (jnp.minimum(bins, K) + jnp.minimum(F - 1 - bins, K) + 1).astype(jnp.float32)
    smooth = jnp.dot(magnitude, band_ref[...], preferred_element_type=jnp.float32) / counts
    gain = 1.0 / (smooth + 1e-06)
    white_re = (real * gain).astype(jnp.bfloat16).astype(jnp.float32)
    white_im = (imag * gain).astype(jnp.bfloat16).astype(jnp.float32)
    pad = jnp.zeros((LANES - 2 * wins, F), jnp.float32)
    for c in range(chans):
        mine = slice(c * wins, (c + 1) * wins)
        both = jnp.concatenate([white_re[mine], white_im[mine], pad], axis=0)
        turned_ref[(first + c) * PITCH : (first + c) * PITCH + F, :] = both.T


def list_slots(chans, me_ref, index_ref, slot_ref):
    mine = jnp.int32(0)
    for s in range(index_ref.shape[0]):
        local = index_ref[s] - me_ref[0] * chans
        bit = lax.shift_left(jnp.int32(1), jnp.clip(local, 0, chans - 1))
        mine = mine | jnp.where((local >= 0) & (local < chans), bit, 0)
    early = count = jnp.int32(0)
    for c in range(chans):
        slot_ref[count] = c
        count = count + (lax.shift_right_logical(mine, c) & 1)
        if c < chans - GAUGE:
            early = count
    slot_ref[chans + 1] = early
    slot_ref[chans + 2] = count


def lay_out(slot, channel, turned_ref, stage_ref, height, slots):
    dests = stage_ref.shape[1] // height
    per_dest = HALF // dests
    lane = lax.broadcasted_iota(jnp.int32, (dests, LANES), 1)
    for pair in range(per_dest // 2):
        piece = []
        for j in range(2):
            for half in range(2):
                at = channel * PITCH + half * HALF + pair * 2 + j
                piece.append(turned_ref[pl.ds(at, dests, stride=per_dest), :])
        a, b, c, d = piece
        b = pltpu.roll(b, 96, 1)
        c = pltpu.roll(c, 64, 1)
        d = pltpu.roll(d, 32, 1)
        rows_at = pl.ds(pair * slots + slot, dests, stride=height)
        stage_ref.at[0][rows_at, :] = jnp.where(lane < 96, a, b)
        stage_ref.at[1][rows_at, :] = jnp.where(lane < 64, b, c)
        stage_ref.at[2][rows_at, :] = jnp.where(lane < 32, c, d)


def whiten_kernel(
    height, slots, me_ref, index_ref, traces_ref, table_ref, band_ref, turned_ref, stage_ref, slot_ref
):
    chans = traces_ref.shape[0]
    stage_ref[...] = jnp.zeros_like(stage_ref)
    list_slots(chans, me_ref, index_ref, slot_ref)
    for c in range(0, chans - GAUGE, GAUGE):
        cur, upper = traces_ref[c : c + GAUGE], traces_ref[c + GAUGE : c + 2 * GAUGE]
        whiten_block(cur, upper, table_ref, band_ref, turned_ref, c)

    def one(slot, carry):
        lay_out(slot, slot_ref[slot], turned_ref, stage_ref, height, slots)
        return carry

    lax.fori_loop(0, jnp.minimum(slot_ref[chans + 1], slots), one, 0)


def finish_kernel(
    height, slots, slot_ref, traces_ref, halo_ref, table_ref, band_ref, _, __, turned_ref, stage_ref, *rounds
):
    chans = traces_ref.shape[0]
    early, count = slot_ref[chans + 1], slot_ref[chans + 2]
    cur = traces_ref[chans - GAUGE :]
    whiten_block(cur, halo_ref[...], table_ref, band_ref, turned_ref, chans - GAUGE)

    def fill(first, start, rows_ref):
        def one(slot, carry):
            channel = slot_ref[first + slot]
            lay_out(slot, channel, turned_ref, stage_ref, height, slots)
            return carry

        lax.fori_loop(start, jnp.minimum(count - first, slots), one, 0)
        for dest in range(rows_ref.shape[0]):
            for tile in range(3):
                block = stage_ref[tile, dest * height : (dest + 1) * height, :]
                rows_ref[dest, :, tile * LANES : (tile + 1) * LANES] = block.astype(jnp.bfloat16)

    def clear(rows_ref):
        rows_ref[...] = jnp.zeros_like(rows_ref)

    fill(0, early, rounds[0])
    for number in range(1, len(rounds)):
        more = count > number * slots
        pl.when(more)(functools.partial(fill, number * slots, 0, rounds[number]))
        pl.when(jnp.logical_not(more))(functools.partial(clear, rounds[number]))


def left_kernel(chans, depth, turned_ref, left_ref):
    lane = lax.broadcasted_iota(jnp.int32, (chans, LANES), 1)

    def one(g, carry):
        stack = []
        for half in range(2):
            real = turned_ref[pl.ds(half * HALF + g, chans, stride=PITCH), :]
            ahead = pltpu.roll(real, depth // 2, 1)
            back = pltpu.roll(real, LANES - depth // 2, 1)
            stack += [real, jnp.where(lane < depth // 2, -back, ahead)]
        left_ref[g] = jnp.concatenate(stack, axis=0).astype(jnp.bfloat16)
        return carry

    lax.fori_loop(0, HALF, one, 0, unroll=8)


def pick_kernel(slots, base, place_ref, rows_ref, out_ref):
    sources = place_ref.shape[0]
    dests, height, width = rows_ref.shape
    groups, depth, _ = out_ref.shape
    rows = rows_ref[...].reshape(dests * height, width)
    ids = lax.broadcasted_iota(jnp.int32, (sources, dests * height), 1)
    place = place_ref[...] - base
    inside = (place >= 0) & (place < dests * slots)
    spot = place // slots * height + place % slots
    for pair in range(groups // 2):
        hit = inside & (ids == spot + pair * slots)
        onehot = jnp.where(hit, 1.0, 0.0).astype(jnp.bfloat16)
        turned = jnp.dot(onehot, rows, preferred_element_type=jnp.float32).T
        for j in range(2):
            low = turned[(2 * j) * depth : (2 * j + 1) * depth]
            high = turned[(2 * j + 1) * depth : (2 * j + 2) * depth]
            out_ref[pair * 2 + j] = jnp.concatenate([low, high], axis=1).astype(jnp.bfloat16)


def products(n, origins, me_ref, left_ref, pieces, held):
    rows = left_ref.shape[1]
    depth, width = pieces[0].shape[-2:]
    groups = HALF // n
    sources = width // 2
    outs = rows // 2
    me = me_ref[0]
    lane = lax.broadcasted_iota(jnp.int32, (outs, width), 1)
    for piece, names in zip(pieces, origins):
        for place, (flip, index) in enumerate(names):
            g = (me ^ flip) * groups + index
            both = jnp.dot(left_ref[g][:, :depth], piece[place], preferred_element_type=jnp.float32)
            mine = jnp.where(lane < sources, both[:outs], both[outs:])
            held[pl.ds(g, outs, stride=HALF_PITCH), :] = mine


def partial_kernel(n, origins, chained, me_ref, left_ref, *refs):
    products(n, origins, me_ref, left_ref, refs[chained:-1], refs[-1])


def correlate_kernel(scale, n, origins, sources, me_ref, left_ref, _, *refs):
    pieces, (out_ref, held, turned_ref, sems) = refs[:-4], refs[-4:]
    products(n, origins, me_ref, left_ref, pieces, held)
    outs = held.shape[0] // HALF_PITCH
    chans = outs // 2
    group = 8
    copies = []
    for part in range(2):
        for c in range(chans):
            base = (part * chans + c) * HALF_PITCH
            turned = held[base : base + HALF, :].T * scale
            rows_at = pl.ds(part * sources * chans + c, sources, stride=chans)
            for half in range(2):
                turned_ref.at[half][rows_at, :] = turned[half * sources : (half + 1) * sources]
            if c % group == group - 1:
                span = pl.ds(c + 1 - group, group)
                for half in range(2):
                    block = turned_ref.at[half].reshape(2, sources, chans, HALF)
                    copy = pltpu.make_async_copy(
                        block.at[part, :, span, :],
                        out_ref.at[part, :, span, pl.ds(half * HALF, HALF)],
                        sems.at[part * (chans // group) + c // group, half],
                    )
                    copy.start()
                    copies.append(copy)
    for copy in copies:
        copy.wait()


def gather_pieces(own, multiply, after_products):
    n = lax.axis_size("chan")
    groups = own.shape[0]
    cut = max(1, groups * 3 // 4)
    most, rest = list(range(cut)), list(range(cut, groups))
    core, x, y = 1, 2, 4
    column = [8 * k for k in range(1, n // 8)]
    place = {}

    def keep(array, names):
        for i, name in enumerate(names):
            place[name] = (array, i)
        return array, names

    def pack(names):
        parts = []
        for name in names:
            array, i = place[name]
            if parts and parts[-1][0] is array and parts[-1][2] == i:
                parts[-1][2] = i + 1
            else:
                parts.append([array, i, i + 1])
        blocks = [array[i:j] for array, i, j in parts]
        return blocks[0] if len(blocks) == 1 else jnp.concatenate(blocks, axis=0)

    def send(names, flip):
        route = [(i, i ^ flip) for i in range(n)]
        return lax.ppermute(pack(names), "chan", route), [(f ^ flip, g) for f, g in names]

    def lists(pairs):
        return [array for array, _ in pairs], [names for _, names in pairs]

    everything = [(f, g) for f in range(0, n, 2) for g in range(groups)]
    near = [keep(own, [(0, g) for g in range(groups)])]
    first_x, first_y = most[:1] + rest, most[1:2] + rest
    far = [send([(0, g) for g in most], flip) for flip in column]
    first = [send([(0, g) for g in first_x], x), send([(0, g) for g in first_y], y)] + far
    arrays = lax.optimization_barrier(lists(first)[0])
    near += [keep(array, names) for array, (_, names) in zip(arrays, first)]

    from_far = [(flip, g) for flip in column for g in most]
    other_x = [(0, g) for g in range(groups) if g not in first_x]
    other_y = [(0, g) for g in range(groups) if g not in first_y]
    mid = [
        send(from_far + other_x + [(y, g) for g in first_y], x),
        send(from_far + other_y + [(x, g) for g in most[:1]], y),
    ]
    mid += [send([(f, g) for f in (0, x) for g in rest], flip) for flip in column]
    multiply(*lists(near))
    arrays = after_products(*lists(mid)[0])
    mid = [keep(array, names) for array, (_, names) in zip(arrays, mid)]

    by_x, by_y, either = [], [], []
    for f, g in everything:
        if (f, g) not in place:
            at_x, at_y = (f ^ x, g) in place, (f ^ y, g) in place
            (either if at_x and at_y else by_x if at_x else by_y).append((f, g))
    for name in either:
        (by_x if len(by_x) < len(by_y) else by_y).append(name)
    last = [send([(f ^ x, g) for f, g in by_x], x), send([(f ^ y, g) for f, g in by_y], y)]
    known = [name for pair in near + mid for name in pair[1]]
    theirs = send(known, core)
    multiply(*lists(mid))
    arrays = after_products(*lists(last)[0])
    last = [keep(array, names) for array, (_, names) in zip(arrays, last)]
    assert sorted(place) == everything
    final = send(by_x + by_y, core)
    multiply(*lists([theirs] + last))
    return lists([final])


def plan_places(source_index, chans, slots):
    n = lax.axis_size("chan")
    channels = jnp.arange(n * chans, dtype=jnp.int32)
    hits = source_index[:, None] == channels[None, :]
    listed = jnp.any(hits, axis=0).reshape(n, chans).astype(jnp.int32)
    below = (jnp.arange(chans)[:, None] < jnp.arange(chans)[None, :]).astype(jnp.int32)
    rank = jnp.sum(listed[:, :, None] * below[None], axis=1)
    device = jnp.arange(n, dtype=jnp.int32)[:, None]
    place = (rank // slots * n + device) * slots + rank % slots
    places = jnp.sum(jnp.where(hits, place.reshape(1, -1), 0), axis=1, keepdims=True)
    return places, jnp.max(jnp.sum(listed, axis=1))


def per_device(traces, source_index):
    chans, wins, length = traces.shape
    n = lax.axis_size("chan")
    sources = source_index.shape[0]
    halo = lax.ppermute(traces[:GAUGE], "chan", [(i + 1, i) for i in range(n - 1)])
    me = lax.axis_index("chan").astype(jnp.int32).reshape(1)
    table, band = jnp.asarray(make_table(length)), jnp.asarray(make_band())
    depth = 2 * wins
    row_width = HALF * 2 * depth // n
    vmem = pl.BlockSpec(memory_space=pltpu.VMEM)
    smem = pl.BlockSpec(memory_space=pltpu.SMEM)
    params = pltpu.CompilerParams(vmem_limit_bytes=VMEM_LIMIT)
    pairs = HALF // n // 2
    slots = chans // pairs
    turned = jax.ShapeDtypeStruct((chans * PITCH, LANES), jnp.float32)
    stage = jax.ShapeDtypeStruct((3, n * chans, LANES), jnp.float32)
    slot_list = jax.ShapeDtypeStruct((chans + 3,), jnp.int32)
    some, staged, listed = pl.pallas_call(
        functools.partial(whiten_kernel, chans, slots),
        in_specs=[smem] * 2 + [vmem] * 3,
        out_specs=[vmem, vmem, smem],
        out_shape=[turned, stage, slot_list],
        compiler_params=params,
        cost_estimate=pl.CostEstimate(
            flops=2 * (chans - GAUGE) * wins * (length + F // 2) * 2 * F,
            bytes_accessed=8 * 1024 * 1024,
            transcendentals=0,
        ),
        name="whiten",
    )(me, source_index, traces, table, band)
    rows_shape = jax.ShapeDtypeStruct((n, chans, row_width // pairs), jnp.bfloat16)
    spectra, _, *rounds = pl.pallas_call(
        functools.partial(finish_kernel, chans, slots),
        in_specs=[smem] + [vmem] * 6,
        out_specs=[vmem] * (2 + pairs),
        out_shape=[turned, stage] + [rows_shape] * pairs,
        input_output_aliases={5: 0, 6: 1},
        compiler_params=params,
        name="finish",
    )(listed, traces, halo, table, band, some, staged)
    rounds[0], late_index = lax.optimization_barrier((rounds[0], source_index))
    places, most = plan_places(late_index, chans, slots)

    def exchange(number, rows):
        rows = lax.all_to_all(rows, "chan", 0, 0, tiled=True)
        return pl.pallas_call(
            functools.partial(pick_kernel, slots, number * n * slots),
            out_shape=jax.ShapeDtypeStruct((HALF // n, depth, 2 * sources), jnp.bfloat16),
            compiler_params=params,
            name="pick",
        )(places, rows)

    picked = exchange(0, rounds[0])
    for number in range(1, pairs):
        picked = lax.cond(
            most > number * slots,
            lambda p, r, number=number: p + exchange(number, r),
            lambda p, r: p,
            picked,
            rounds[number],
        )
    picked, spectra = lax.optimization_barrier((picked, spectra))
    left = pl.pallas_call(
        functools.partial(left_kernel, chans, depth),
        in_specs=[vmem],
        out_specs=vmem,
        out_shape=jax.ShapeDtypeStruct((HALF, 4 * chans, LANES), jnp.bfloat16),
        compiler_params=params,
        cost_estimate=pl.CostEstimate(
            flops=10 * 1000 * 1000, bytes_accessed=8 * 1024 * 1024, transcendentals=0
        ),
        name="left",
    )(spectra)
    total_windows = wins * lax.axis_size("win")
    held_shape = jax.ShapeDtypeStruct((2 * chans * HALF_PITCH, LANES), jnp.float32)
    held = []

    def multiply(pieces, origins):
        held[:] = [
            pl.pallas_call(
                functools.partial(partial_kernel, n, origins, len(held)),
                in_specs=[smem, vmem] + [vmem] * (len(held) + len(pieces)),
                out_specs=vmem,
                out_shape=held_shape,
                input_output_aliases={2: 0} if held else {},
                compiler_params=params,
                cost_estimate=pl.CostEstimate(
                    flops=100 * 1000 * 1000, bytes_accessed=4 * 1024 * 1024, transcendentals=0
                ),
                name="products",
            )(me, left, *held, *pieces)
        ]

    def after_products(*arrays):
        *arrays, held[0] = lax.optimization_barrier((*arrays, held[0]))
        return arrays

    pieces, origins = gather_pieces(picked, multiply, after_products)
    stack, _ = pl.pallas_call(
        functools.partial(correlate_kernel, 1.0 / total_windows, n, origins, sources),
        in_specs=[smem, vmem, vmem] + [vmem] * len(pieces),
        out_specs=[pl.BlockSpec(memory_space=pl.ANY), vmem],
        out_shape=[jax.ShapeDtypeStruct((2, sources, chans, F), jnp.float32), held_shape],
        scratch_shapes=[
            pltpu.VMEM((2, 2 * sources * chans, HALF), jnp.float32),
            pltpu.SemaphoreType.DMA((chans // 4, 2)),
        ],
        input_output_aliases={2: 1},
        compiler_params=params,
        name="correlate",
    )(me, left, *held, *pieces)
    if lax.axis_size("win") == 1:
        return stack
    return lax.psum_scatter(stack, "win", scatter_dimension=1, tiled=True)


def solution(mesh):
    return jax.shard_map(
        per_device,
        mesh=mesh,
        in_specs=(P("chan", "win", None), P()),
        out_specs=P(None, "win", "chan", None),
        check_vma=False,
    )
```

```python
import functools
import math

import jax
import jax.numpy as jnp
import ml_dtypes
import numpy as np
from jax import lax
from jax.experimental import pallas as pl
from jax.experimental.pallas import tpu as pltpu
from jax.sharding import PartitionSpec as P

F = 256
HALF = 128
F0 = 1
K = 64
GAUGE = 4
LANES = 128
PITCH = F + 8
HALF_PITCH = HALF + 8
VMEM_LIMIT = 24 * 1024 * 1024


def make_table(length):
    times = np.arange(length, dtype=np.int64)[:, None]
    bins = np.arange(F, dtype=np.int64)[None, :] + F0
    phase = (times * bins % length).astype(np.float32) * np.float32(2.0 * math.pi / length)
    phase = phase.astype(np.float64)
    return np.concatenate([np.cos(phase), -np.sin(phase)], axis=1).astype(ml_dtypes.bfloat16)


def make_band():
    rows = np.arange(F)[:, None]
    cols = np.arange(F)[None, :]
    return (np.abs(rows - cols) <= K).astype(ml_dtypes.bfloat16)


def whiten_block(cur, upper, table_ref, band_ref, turned_ref, first):
    chans, wins, length = cur.shape
    rows = chans * wins
    diff = (upper.astype(jnp.float32) - cur.astype(jnp.float32)).reshape(rows, length)
    power = jnp.sum(diff * diff, axis=1, keepdims=True) * (1.0 / length)
    normed = (diff * lax.rsqrt(power + 1e-05)).astype(jnp.bfloat16)
    spec = jnp.dot(normed, table_ref[...], preferred_element_type=jnp.float32)
    real = spec[:, :F]
    imag = spec[:, F:]
    magnitude = jnp.sqrt(real * real + imag * imag).astype(jnp.bfloat16)
    bins = lax.broadcasted_iota(jnp.int32, (1, F), 1)
    counts = (jnp.minimum(bins, K) + jnp.minimum(F - 1 - bins, K) + 1).astype(jnp.float32)
    smooth = jnp.dot(magnitude, band_ref[...], preferred_element_type=jnp.float32) / counts
    gain = 1.0 / (smooth + 1e-06)
    white_re = (real * gain).astype(jnp.bfloat16).astype(jnp.float32)
    white_im = (imag * gain).astype(jnp.bfloat16).astype(jnp.float32)
    pad = jnp.zeros((LANES - 2 * wins, F), jnp.float32)
    for c in range(chans):
        mine = slice(c * wins, (c + 1) * wins)
        both = jnp.concatenate([white_re[mine], white_im[mine], pad], axis=0)
        turned_ref[(first + c) * PITCH : (first + c) * PITCH + F, :] = both.T


def list_slots(chans, me_ref, index_ref, slot_ref):
    mine = jnp.int32(0)
    for s in range(index_ref.shape[0]):
        local = index_ref[s] - me_ref[0] * chans
        bit = lax.shift_left(jnp.int32(1), jnp.clip(local, 0, chans - 1))
        mine = mine | jnp.where((local >= 0) & (local < chans), bit, 0)
    early = count = jnp.int32(0)
    for c in range(chans):
        slot_ref[count] = c
        count = count + (lax.shift_right_logical(mine, c) & 1)
        if c < chans - GAUGE:
            early = count
    slot_ref[chans + 1] = early
    slot_ref[chans + 2] = count


def lay_out(slot, channel, turned_ref, stage_ref, height, slots):
    dests = stage_ref.shape[1] // height
    per_dest = HALF // dests
    lane = lax.broadcasted_iota(jnp.int32, (dests, LANES), 1)
    for pair in range(per_dest // 2):
        piece = []
        for j in range(2):
            for half in range(2):
                at = channel * PITCH + half * HALF + pair * 2 + j
                piece.append(turned_ref[pl.ds(at, dests, stride=per_dest), :])
        a, b, c, d = piece
        b = pltpu.roll(b, 96, 1)
        c = pltpu.roll(c, 64, 1)
        d = pltpu.roll(d, 32, 1)
        rows_at = pl.ds(pair * slots + slot, dests, stride=height)
        stage_ref.at[0][rows_at, :] = jnp.where(lane < 96, a, b)
        stage_ref.at[1][rows_at, :] = jnp.where(lane < 64, b, c)
        stage_ref.at[2][rows_at, :] = jnp.where(lane < 32, c, d)


def whiten_kernel(
    height, slots, me_ref, index_ref, traces_ref, table_ref, band_ref, turned_ref, stage_ref, slot_ref
):
    chans = traces_ref.shape[0]
    stage_ref[...] = jnp.zeros_like(stage_ref)
    list_slots(chans, me_ref, index_ref, slot_ref)
    for c in range(0, chans - GAUGE, GAUGE):
        cur, upper = traces_ref[c : c + GAUGE], traces_ref[c + GAUGE : c + 2 * GAUGE]
        whiten_block(cur, upper, table_ref, band_ref, turned_ref, c)

    def one(slot, carry):
        lay_out(slot, slot_ref[slot], turned_ref, stage_ref, height, slots)
        return carry

    lax.fori_loop(0, jnp.minimum(slot_ref[chans + 1], slots), one, 0)


def finish_kernel(
    height, slots, slot_ref, traces_ref, halo_ref, table_ref, band_ref, _, __, turned_ref, stage_ref, *rounds
):
    chans = traces_ref.shape[0]
    early, count = slot_ref[chans + 1], slot_ref[chans + 2]
    cur = traces_ref[chans - GAUGE :]
    whiten_block(cur, halo_ref[...], table_ref, band_ref, turned_ref, chans - GAUGE)

    def fill(first, start, rows_ref):
        def one(slot, carry):
            channel = slot_ref[first + slot]
            lay_out(slot, channel, turned_ref, stage_ref, height, slots)
            return carry

        lax.fori_loop(start, jnp.minimum(count - first, slots), one, 0)
        for dest in range(rows_ref.shape[0]):
            for tile in range(3):
                block = stage_ref[tile, dest * height : (dest + 1) * height, :]
                rows_ref[dest, :, tile * LANES : (tile + 1) * LANES] = block.astype(jnp.bfloat16)

    def clear(rows_ref):
        rows_ref[...] = jnp.zeros_like(rows_ref)

    fill(0, early, rounds[0])
    for number in range(1, len(rounds)):
        more = count > number * slots
        pl.when(more)(functools.partial(fill, number * slots, 0, rounds[number]))
        pl.when(jnp.logical_not(more))(functools.partial(clear, rounds[number]))


def left_kernel(chans, depth, turned_ref, left_ref):
    lane = lax.broadcasted_iota(jnp.int32, (chans, LANES), 1)

    def one(g, carry):
        stack = []
        for half in range(2):
            real = turned_ref[pl.ds(half * HALF + g, chans, stride=PITCH), :]
            ahead = pltpu.roll(real, depth // 2, 1)
            back = pltpu.roll(real, LANES - depth // 2, 1)
            stack += [real, jnp.where(lane < depth // 2, -back, ahead)]
        left_ref[g] = jnp.concatenate(stack, axis=0).astype(jnp.bfloat16)
        return carry

    lax.fori_loop(0, HALF, one, 0, unroll=8)


def pick_kernel(slots, base, place_ref, rows_ref, out_ref):
    sources = place_ref.shape[0]
    dests, height, width = rows_ref.shape
    groups, depth, _ = out_ref.shape
    rows = rows_ref[...].reshape(dests * height, width)
    ids = lax.broadcasted_iota(jnp.int32, (sources, dests * height), 1)
    place = place_ref[...] - base
    inside = (place >= 0) & (place < dests * slots)
    spot = place // slots * height + place % slots
    for pair in range(groups // 2):
        hit = inside & (ids == spot + pair * slots)
        onehot = jnp.where(hit, 1.0, 0.0).astype(jnp.bfloat16)
        turned = jnp.dot(onehot, rows, preferred_element_type=jnp.float32).T
        for j in range(2):
            low = turned[(2 * j) * depth : (2 * j + 1) * depth]
            high = turned[(2 * j + 1) * depth : (2 * j + 2) * depth]
            out_ref[pair * 2 + j] = jnp.concatenate([low, high], axis=1).astype(jnp.bfloat16)


def products(n, origins, me_ref, left_ref, pieces, held):
    rows = left_ref.shape[1]
    depth, width = pieces[0].shape[-2:]
    groups = HALF // n
    sources = width // 2
    outs = rows // 2
    me = me_ref[0]
    lane = lax.broadcasted_iota(jnp.int32, (outs, width), 1)
    for piece, names in zip(pieces, origins):
        for place, (flip, index) in enumerate(names):
            g = (me ^ flip) * groups + index
            both = jnp.dot(left_ref[g][:, :depth], piece[place], preferred_element_type=jnp.float32)
            mine = jnp.where(lane < sources, both[:outs], both[outs:])
            held[pl.ds(g, outs, stride=HALF_PITCH), :] = mine


def partial_kernel(n, origins, chained, me_ref, left_ref, *refs):
    products(n, origins, me_ref, left_ref, refs[chained:-1], refs[-1])


def correlate_kernel(scale, n, origins, sources, me_ref, left_ref, _, *refs):
    pieces, (out_ref, held, turned_ref, sems) = refs[:-4], refs[-4:]
    products(n, origins, me_ref, left_ref, pieces, held)
    outs = held.shape[0] // HALF_PITCH
    chans = outs // 2
    group = 8
    copies = []
    for part in range(2):
        for c in range(chans):
            base = (part * chans + c) * HALF_PITCH
            turned = held[base : base + HALF, :].T * scale
            rows_at = pl.ds(part * sources * chans + c, sources, stride=chans)
            for half in range(2):
                turned_ref.at[half][rows_at, :] = turned[half * sources : (half + 1) * sources]
            if c % group == group - 1:
                span = pl.ds(c + 1 - group, group)
                for half in range(2):
                    block = turned_ref.at[half].reshape(2, sources, chans, HALF)
                    copy = pltpu.make_async_copy(
                        block.at[part, :, span, :],
                        out_ref.at[part, :, span, pl.ds(half * HALF, HALF)],
                        sems.at[part * (chans // group) + c // group, half],
                    )
                    copy.start()
                    copies.append(copy)
    for copy in copies:
        copy.wait()


def gather_pieces(own, multiply, after_products):
    n = lax.axis_size("chan")
    groups = own.shape[0]
    cut = max(1, groups * 3 // 4)
    rest = range(cut, groups)
    core, x, y = 1, 2, 4
    column = [8 * k for k in range(1, n // 8)]
    place = {}

    def keep(array, names):
        for i, name in enumerate(names):
            place[name] = (array, i)
        return array, names

    def pack(names):
        parts = []
        for name in names:
            array, i = place[name]
            if parts and parts[-1][0] is array and parts[-1][2] == i:
                parts[-1][2] = i + 1
            else:
                parts.append([array, i, i + 1])
        blocks = [array[i:j] for array, i, j in parts]
        return blocks[0] if len(blocks) == 1 else jnp.concatenate(blocks, axis=0)

    def send(names, flip):
        route = [(i, i ^ flip) for i in range(n)]
        return lax.ppermute(pack(names), "chan", route), [(f ^ flip, g) for f, g in names]

    def lists(pairs):
        return [array for array, _ in pairs], [names for _, names in pairs]

    everything = [(f, g) for f in range(0, n, 2) for g in range(groups)]
    whole = [(0, g) for g in range(groups)]
    near = [keep(own, whole)]
    first = [send(whole[:cut], flip) for flip in column[:-1]]
    first += [send(whole, flip) for flip in (x, y, column[-1])]
    arrays = lax.optimization_barrier(lists(first)[0])
    near += [keep(array, names) for array, (_, names) in zip(arrays, first)]

    from_far = [name for _, names in first for name in names if name[0] not in (x, y)]
    mid = [
        send(from_far + [(y, g) for g in range(1, groups, 2)], x),
        send(from_far + [(x, g) for g in range(0, groups, 2)], y),
    ]
    mid += [send([(f, g) for f in (0, x) for g in rest], flip) for flip in column[:-1]]
    multiply(*lists(near))
    arrays = after_products(*lists(mid)[0])
    mid = [keep(array, names) for array, (_, names) in zip(arrays, mid)]

    by_x, by_y, either = [], [], []
    for f, g in everything:
        if (f, g) not in place:
            at_x, at_y = (f ^ x, g) in place, (f ^ y, g) in place
            (either if at_x and at_y else by_x if at_x else by_y).append((f, g))
    for name in either:
        (by_x if len(by_x) < len(by_y) else by_y).append(name)
    last = [send([(f ^ x, g) for f, g in by_x], x), send([(f ^ y, g) for f, g in by_y], y)]
    known = [name for pair in near + mid for name in pair[1]]
    theirs = send(known, core)
    multiply(*lists(mid))
    arrays = after_products(*lists(last)[0])
    last = [keep(array, names) for array, (_, names) in zip(arrays, last)]
    assert sorted(place) == everything
    final = send(by_x + by_y, core)
    multiply(*lists([theirs] + last))
    return lists([final])


def plan_places(source_index, chans, slots):
    n = lax.axis_size("chan")
    channels = jnp.arange(n * chans, dtype=jnp.int32)
    hits = source_index[:, None] == channels[None, :]
    listed = jnp.any(hits, axis=0).reshape(n, chans).astype(jnp.int32)
    below = (jnp.arange(chans)[:, None] < jnp.arange(chans)[None, :]).astype(jnp.int32)
    rank = jnp.sum(listed[:, :, None] * below[None], axis=1)
    device = jnp.arange(n, dtype=jnp.int32)[:, None]
    place = (rank // slots * n + device) * slots + rank % slots
    places = jnp.sum(jnp.where(hits, place.reshape(1, -1), 0), axis=1, keepdims=True)
    return places, jnp.max(jnp.sum(listed, axis=1))


def per_device(traces, source_index):
    chans, wins, length = traces.shape
    n = lax.axis_size("chan")
    sources = source_index.shape[0]
    halo = lax.ppermute(traces[:GAUGE], "chan", [(i + 1, i) for i in range(n - 1)])
    me = lax.axis_index("chan").astype(jnp.int32).reshape(1)
    table, band = jnp.asarray(make_table(length)), jnp.asarray(make_band())
    depth = 2 * wins
    row_width = HALF * 2 * depth // n
    vmem = pl.BlockSpec(memory_space=pltpu.VMEM)
    smem = pl.BlockSpec(memory_space=pltpu.SMEM)
    params = pltpu.CompilerParams(vmem_limit_bytes=VMEM_LIMIT)
    pairs = HALF // n // 2
    slots = chans // pairs
    turned = jax.ShapeDtypeStruct((chans * PITCH, LANES), jnp.float32)
    stage = jax.ShapeDtypeStruct((3, n * chans, LANES), jnp.float32)
    slot_list = jax.ShapeDtypeStruct((chans + 3,), jnp.int32)
    some, staged, listed = pl.pallas_call(
        functools.partial(whiten_kernel, chans, slots),
        in_specs=[smem] * 2 + [vmem] * 3,
        out_specs=[vmem, vmem, smem],
        out_shape=[turned, stage, slot_list],
        compiler_params=params,
        cost_estimate=pl.CostEstimate(
            flops=2 * (chans - GAUGE) * wins * (length + F // 2) * 2 * F,
            bytes_accessed=8 * 1024 * 1024,
            transcendentals=0,
        ),
        name="whiten",
    )(me, source_index, traces, table, band)
    rows_shape = jax.ShapeDtypeStruct((n, chans, row_width // pairs), jnp.bfloat16)
    spectra, _, *rounds = pl.pallas_call(
        functools.partial(finish_kernel, chans, slots),
        in_specs=[smem] + [vmem] * 6,
        out_specs=[vmem] * (2 + pairs),
        out_shape=[turned, stage] + [rows_shape] * pairs,
        input_output_aliases={5: 0, 6: 1},
        compiler_params=params,
        name="finish",
    )(listed, traces, halo, table, band, some, staged)
    rounds[0], late_index = lax.optimization_barrier((rounds[0], source_index))
    places, most = plan_places(late_index, chans, slots)

    def exchange(number, rows):
        rows = lax.all_to_all(rows, "chan", 0, 0, tiled=True)
        return pl.pallas_call(
            functools.partial(pick_kernel, slots, number * n * slots),
            out_shape=jax.ShapeDtypeStruct((HALF // n, depth, 2 * sources), jnp.bfloat16),
            compiler_params=params,
            name="pick",
        )(places, rows)

    picked = exchange(0, rounds[0])
    for number in range(1, pairs):
        picked = lax.cond(
            most > number * slots,
            lambda p, r, number=number: p + exchange(number, r),
            lambda p, r: p,
            picked,
            rounds[number],
        )
    picked, spectra = lax.optimization_barrier((picked, spectra))
    left = pl.pallas_call(
        functools.partial(left_kernel, chans, depth),
        in_specs=[vmem],
        out_specs=vmem,
        out_shape=jax.ShapeDtypeStruct((HALF, 4 * chans, LANES), jnp.bfloat16),
        compiler_params=params,
        cost_estimate=pl.CostEstimate(
            flops=10 * 1000 * 1000, bytes_accessed=8 * 1024 * 1024, transcendentals=0
        ),
        name="left",
    )(spectra)
    total_windows = wins * lax.axis_size("win")
    held_shape = jax.ShapeDtypeStruct((2 * chans * HALF_PITCH, LANES), jnp.float32)
    held = []

    def multiply(pieces, origins):
        held[:] = [
            pl.pallas_call(
                functools.partial(partial_kernel, n, origins, len(held)),
                in_specs=[smem, vmem] + [vmem] * (len(held) + len(pieces)),
                out_specs=vmem,
                out_shape=held_shape,
                input_output_aliases={2: 0} if held else {},
                compiler_params=params,
                cost_estimate=pl.CostEstimate(
                    flops=100 * 1000 * 1000, bytes_accessed=4 * 1024 * 1024, transcendentals=0
                ),
                name="products",
            )(me, left, *held, *pieces)
        ]

    def after_products(*arrays):
        *arrays, held[0] = lax.optimization_barrier((*arrays, held[0]))
        return arrays

    pieces, origins = gather_pieces(picked, multiply, after_products)
    stack, _ = pl.pallas_call(
        functools.partial(correlate_kernel, 1.0 / total_windows, n, origins, sources),
        in_specs=[smem, vmem, vmem] + [vmem] * len(pieces),
        out_specs=[pl.BlockSpec(memory_space=pl.ANY), vmem],
        out_shape=[jax.ShapeDtypeStruct((2, sources, chans, F), jnp.float32), held_shape],
        scratch_shapes=[
            pltpu.VMEM((2, 2 * sources * chans, HALF), jnp.float32),
            pltpu.SemaphoreType.DMA((chans // 4, 2)),
        ],
        input_output_aliases={2: 1},
        compiler_params=params,
        name="correlate",
    )(me, left, *held, *pieces)
    if lax.axis_size("win") == 1:
        return stack
    return lax.psum_scatter(stack, "win", scatter_dimension=1, tiled=True)


def solution(mesh):
    return jax.shard_map(
        per_device,
        mesh=mesh,
        in_specs=(P("chan", "win", None), P()),
        out_specs=P(None, "win", "chan", None),
        check_vma=False,
    )
```

```python
import functools
import math

import jax
import jax.numpy as jnp
import ml_dtypes
import numpy as np
from jax import lax
from jax.experimental import pallas as pl
from jax.experimental.pallas import tpu as pltpu
from jax.sharding import PartitionSpec as P

F = 256
HALF = 128
F0 = 1
K = 64
GAUGE = 4
LANES = 128
PITCH = F + 8
HALF_PITCH = HALF + 8
VMEM_LIMIT = 24 * 1024 * 1024


def make_table(length):
    times = np.arange(length, dtype=np.int64)[:, None]
    bins = np.arange(F, dtype=np.int64)[None, :] + F0
    phase = (times * bins % length).astype(np.float32) * np.float32(2.0 * math.pi / length)
    phase = phase.astype(np.float64)
    return np.concatenate([np.cos(phase), -np.sin(phase)], axis=1).astype(ml_dtypes.bfloat16)


def make_band():
    rows = np.arange(F)[:, None]
    cols = np.arange(F)[None, :]
    return (np.abs(rows - cols) <= K).astype(ml_dtypes.bfloat16)


def whiten_block(cur, upper, table_ref, band_ref, turned_ref, first):
    chans, wins, length = cur.shape
    rows = chans * wins
    diff = (upper.astype(jnp.float32) - cur.astype(jnp.float32)).reshape(rows, length)
    power = jnp.sum(diff * diff, axis=1, keepdims=True) * (1.0 / length)
    normed = (diff * lax.rsqrt(power + 1e-05)).astype(jnp.bfloat16)
    spec = jnp.dot(normed, table_ref[...], preferred_element_type=jnp.float32)
    real = spec[:, :F]
    imag = spec[:, F:]
    magnitude = jnp.sqrt(real * real + imag * imag).astype(jnp.bfloat16)
    bins = lax.broadcasted_iota(jnp.int32, (1, F), 1)
    counts = (jnp.minimum(bins, K) + jnp.minimum(F - 1 - bins, K) + 1).astype(jnp.float32)
    smooth = jnp.dot(magnitude, band_ref[...], preferred_element_type=jnp.float32) / counts
    gain = 1.0 / (smooth + 1e-06)
    white_re = (real * gain).astype(jnp.bfloat16).astype(jnp.float32)
    white_im = (imag * gain).astype(jnp.bfloat16).astype(jnp.float32)
    pad = jnp.zeros((LANES - 2 * wins, F), jnp.float32)
    for c in range(chans):
        mine = slice(c * wins, (c + 1) * wins)
        both = jnp.concatenate([white_re[mine], white_im[mine], pad], axis=0)
        turned_ref[(first + c) * PITCH : (first + c) * PITCH + F, :] = both.T


def list_slots(chans, me_ref, index_ref, slot_ref):
    mine = jnp.int32(0)
    for s in range(index_ref.shape[0]):
        local = index_ref[s] - me_ref[0] * chans
        bit = lax.shift_left(jnp.int32(1), jnp.clip(local, 0, chans - 1))
        mine = mine | jnp.where((local >= 0) & (local < chans), bit, 0)
    early = count = jnp.int32(0)
    for c in range(chans):
        slot_ref[count] = c
        count = count + (lax.shift_right_logical(mine, c) & 1)
        if c < chans - GAUGE:
            early = count
    slot_ref[chans + 1] = early
    slot_ref[chans + 2] = count


def lay_out(slot, channel, turned_ref, stage_ref, height, slots):
    dests = stage_ref.shape[1] // height
    per_dest = HALF // dests
    lane = lax.broadcasted_iota(jnp.int32, (dests, LANES), 1)
    for pair in range(per_dest // 2):
        piece = []
        for j in range(2):
            for half in range(2):
                at = channel * PITCH + half * HALF + pair * 2 + j
                piece.append(turned_ref[pl.ds(at, dests, stride=per_dest), :])
        a, b, c, d = piece
        b = pltpu.roll(b, 96, 1)
        c = pltpu.roll(c, 64, 1)
        d = pltpu.roll(d, 32, 1)
        rows_at = pl.ds(pair * slots + slot, dests, stride=height)
        stage_ref.at[0][rows_at, :] = jnp.where(lane < 96, a, b)
        stage_ref.at[1][rows_at, :] = jnp.where(lane < 64, b, c)
        stage_ref.at[2][rows_at, :] = jnp.where(lane < 32, c, d)


def whiten_kernel(
    height, slots, me_ref, index_ref, traces_ref, table_ref, band_ref, turned_ref, stage_ref, slot_ref
):
    chans = traces_ref.shape[0]
    stage_ref[...] = jnp.zeros_like(stage_ref)
    list_slots(chans, me_ref, index_ref, slot_ref)
    for c in range(0, chans - GAUGE, GAUGE):
        cur, upper = traces_ref[c : c + GAUGE], traces_ref[c + GAUGE : c + 2 * GAUGE]
        whiten_block(cur, upper, table_ref, band_ref, turned_ref, c)

    def one(slot, carry):
        lay_out(slot, slot_ref[slot], turned_ref, stage_ref, height, slots)
        return carry

    lax.fori_loop(0, jnp.minimum(slot_ref[chans + 1], slots), one, 0)


def finish_kernel(
    height, slots, slot_ref, traces_ref, halo_ref, table_ref, band_ref, _, __, turned_ref, stage_ref, *rounds
):
    chans = traces_ref.shape[0]
    early, count = slot_ref[chans + 1], slot_ref[chans + 2]
    cur = traces_ref[chans - GAUGE :]
    whiten_block(cur, halo_ref[...], table_ref, band_ref, turned_ref, chans - GAUGE)

    def fill(first, start, rows_ref):
        def one(slot, carry):
            channel = slot_ref[first + slot]
            lay_out(slot, channel, turned_ref, stage_ref, height, slots)
            return carry

        lax.fori_loop(start, jnp.minimum(count - first, slots), one, 0)
        for dest in range(rows_ref.shape[0]):
            for tile in range(3):
                block = stage_ref[tile, dest * height : (dest + 1) * height, :]
                rows_ref[dest, :, tile * LANES : (tile + 1) * LANES] = block.astype(jnp.bfloat16)

    def clear(rows_ref):
        rows_ref[...] = jnp.zeros_like(rows_ref)

    fill(0, early, rounds[0])
    for number in range(1, len(rounds)):
        more = count > number * slots
        pl.when(more)(functools.partial(fill, number * slots, 0, rounds[number]))
        pl.when(jnp.logical_not(more))(functools.partial(clear, rounds[number]))


def left_kernel(chans, depth, turned_ref, left_ref):
    lane = lax.broadcasted_iota(jnp.int32, (chans, LANES), 1)

    def one(g, carry):
        stack = []
        for half in range(2):
            real = turned_ref[pl.ds(half * HALF + g, chans, stride=PITCH), :]
            ahead = pltpu.roll(real, depth // 2, 1)
            back = pltpu.roll(real, LANES - depth // 2, 1)
            stack += [real, jnp.where(lane < depth // 2, -back, ahead)]
        left_ref[g] = jnp.concatenate(stack, axis=0).astype(jnp.bfloat16)
        return carry

    lax.fori_loop(0, HALF, one, 0, unroll=8)


def pick_kernel(slots, base, place_ref, rows_ref, out_ref):
    sources = place_ref.shape[0]
    dests, height, width = rows_ref.shape
    groups, depth, _ = out_ref.shape
    rows = rows_ref[...].reshape(dests * height, width)
    ids = lax.broadcasted_iota(jnp.int32, (sources, dests * height), 1)
    place = place_ref[...] - base
    inside = (place >= 0) & (place < dests * slots)
    spot = place // slots * height + place % slots
    for pair in range(groups // 2):
        hit = inside & (ids == spot + pair * slots)
        onehot = jnp.where(hit, 1.0, 0.0).astype(jnp.bfloat16)
        turned = jnp.dot(onehot, rows, preferred_element_type=jnp.float32).T
        for j in range(2):
            low = turned[(2 * j) * depth : (2 * j + 1) * depth]
            high = turned[(2 * j + 1) * depth : (2 * j + 2) * depth]
            out_ref[pair * 2 + j] = jnp.concatenate([low, high], axis=1).astype(jnp.bfloat16)


def products(n, origins, me_ref, left_ref, pieces, held):
    rows = left_ref.shape[1]
    depth, width = pieces[0].shape[-2:]
    groups = HALF // n
    sources = width // 2
    outs = rows // 2
    me = me_ref[0]
    lane = lax.broadcasted_iota(jnp.int32, (outs, width), 1)
    for piece, names in zip(pieces, origins):
        for place, (flip, index) in enumerate(names):
            g = (me ^ flip) * groups + index
            both = jnp.dot(left_ref[g][:, :depth], piece[place], preferred_element_type=jnp.float32)
            mine = jnp.where(lane < sources, both[:outs], both[outs:])
            held[pl.ds(g, outs, stride=HALF_PITCH), :] = mine


def partial_kernel(n, origins, chained, me_ref, left_ref, *refs):
    products(n, origins, me_ref, left_ref, refs[chained:-1], refs[-1])


def correlate_kernel(scale, n, origins, sources, me_ref, left_ref, _, *refs):
    pieces, (out_ref, held, turned_ref, sems) = refs[:-4], refs[-4:]
    products(n, origins, me_ref, left_ref, pieces, held)
    outs = held.shape[0] // HALF_PITCH
    chans = outs // 2
    group = 8
    copies = []
    for part in range(2):
        for c in range(chans):
            base = (part * chans + c) * HALF_PITCH
            turned = held[base : base + HALF, :].T * scale
            rows_at = pl.ds(part * sources * chans + c, sources, stride=chans)
            for half in range(2):
                turned_ref.at[half][rows_at, :] = turned[half * sources : (half + 1) * sources]
            if c % group == group - 1:
                span = pl.ds(c + 1 - group, group)
                for half in range(2):
                    block = turned_ref.at[half].reshape(2, sources, chans, HALF)
                    copy = pltpu.make_async_copy(
                        block.at[part, :, span, :],
                        out_ref.at[part, :, span, pl.ds(half * HALF, HALF)],
                        sems.at[part * (chans // group) + c // group, half],
                    )
                    copy.start()
                    copies.append(copy)
    for copy in copies:
        copy.wait()


def gather_pieces(own, multiply, after_products):
    n = lax.axis_size("chan")
    groups = own.shape[0]
    core, x, y, z, zz = 1, 2, 4, 8, 16
    place = {}

    def keep(array, names):
        for i, name in enumerate(names):
            place[name] = (array, i)
        return array, names

    def pack(names):
        parts = []
        for name in names:
            array, i = place[name]
            if parts and parts[-1][0] is array and parts[-1][2] == i:
                parts[-1][2] = i + 1
            else:
                parts.append([array, i, i + 1])
        blocks = [array[i:j] for array, i, j in parts]
        return blocks[0] if len(blocks) == 1 else jnp.concatenate(blocks, axis=0)

    def send(names, flip):
        route = [(i, i ^ flip) for i in range(n)]
        return lax.ppermute(pack(names), "chan", route), [(f ^ flip, g) for f, g in names]

    def lists(pairs):
        return [array for array, _ in pairs], [names for _, names in pairs]

    def piece(flip, share=slice(None)):
        return [(flip, g) for g in range(groups)[share]]

    near = [keep(own, piece(0))]
    if n != 32:
        flip = 1
        while flip < n:
            near.append(keep(*send(sorted(place), flip)))
            flip *= 2
        multiply(*lists(near[:-1]))
        return lists(near[-1:])

    first = [send(piece(0), flip) for flip in (x ^ y, y, x, z, zz)]
    arrays = lax.optimization_barrier(lists(first)[0])
    near += [keep(array, names) for array, (_, names) in zip(arrays, first)]
    mid = [
        send(piece(z) + piece(zz), x),
        send(piece(z) + piece(zz), y),
        send(piece(zz), z),
        send(piece(x ^ y), zz),
    ]
    multiply(*lists(near))
    arrays = after_products(*lists(mid)[0])
    mid = [keep(array, names) for array, (_, names) in zip(arrays, mid)]
    last = [
        send(piece(z ^ zz) + piece(z ^ y, slice(0, 1)), x),
        send(piece(z ^ zz) + piece(z ^ x, slice(1, 2)), y),
        send(piece(zz ^ x ^ y) + piece(x ^ y, slice(2, None)), z),
    ]
    known = [name for pair in near + mid for name in pair[1]]
    theirs = send(known, core)
    multiply(*lists(mid))
    arrays = after_products(*lists(last)[0])
    last = [keep(array, names) for array, (_, names) in zip(arrays, last)]
    assert sorted(place) == [(f, g) for f in range(0, n, 2) for g in range(groups)]
    final = send([name for pair in last for name in pair[1]], core)
    multiply(*lists([theirs] + last))
    return lists([final])


def plan_places(source_index, chans, slots):
    n = lax.axis_size("chan")
    channels = jnp.arange(n * chans, dtype=jnp.int32)
    hits = source_index[:, None] == channels[None, :]
    listed = jnp.any(hits, axis=0).reshape(n, chans).astype(jnp.int32)
    below = (jnp.arange(chans)[:, None] < jnp.arange(chans)[None, :]).astype(jnp.int32)
    rank = jnp.sum(listed[:, :, None] * below[None], axis=1)
    device = jnp.arange(n, dtype=jnp.int32)[:, None]
    place = (rank // slots * n + device) * slots + rank % slots
    places = jnp.sum(jnp.where(hits, place.reshape(1, -1), 0), axis=1, keepdims=True)
    return places, jnp.max(jnp.sum(listed, axis=1))


def per_device(traces, source_index):
    chans, wins, length = traces.shape
    n = lax.axis_size("chan")
    sources = source_index.shape[0]
    halo = lax.ppermute(traces[:GAUGE], "chan", [(i + 1, i) for i in range(n - 1)])
    me = lax.axis_index("chan").astype(jnp.int32).reshape(1)
    table, band = jnp.asarray(make_table(length)), jnp.asarray(make_band())
    depth = 2 * wins
    row_width = HALF * 2 * depth // n
    vmem = pl.BlockSpec(memory_space=pltpu.VMEM)
    smem = pl.BlockSpec(memory_space=pltpu.SMEM)
    params = pltpu.CompilerParams(vmem_limit_bytes=VMEM_LIMIT)
    pairs = HALF // n // 2
    slots = chans // pairs
    turned = jax.ShapeDtypeStruct((chans * PITCH, LANES), jnp.float32)
    stage = jax.ShapeDtypeStruct((3, n * chans, LANES), jnp.float32)
    slot_list = jax.ShapeDtypeStruct((chans + 3,), jnp.int32)
    some, staged, listed = pl.pallas_call(
        functools.partial(whiten_kernel, chans, slots),
        in_specs=[smem] * 2 + [vmem] * 3,
        out_specs=[vmem, vmem, smem],
        out_shape=[turned, stage, slot_list],
        compiler_params=params,
        cost_estimate=pl.CostEstimate(
            flops=2 * (chans - GAUGE) * wins * (length + F // 2) * 2 * F,
            bytes_accessed=8 * 1024 * 1024,
            transcendentals=0,
        ),
        name="whiten",
    )(me, source_index, traces, table, band)
    rows_shape = jax.ShapeDtypeStruct((n, chans, row_width // pairs), jnp.bfloat16)
    spectra, _, *rounds = pl.pallas_call(
        functools.partial(finish_kernel, chans, slots),
        in_specs=[smem] + [vmem] * 6,
        out_specs=[vmem] * (2 + pairs),
        out_shape=[turned, stage] + [rows_shape] * pairs,
        input_output_aliases={5: 0, 6: 1},
        compiler_params=params,
        name="finish",
    )(listed, traces, halo, table, band, some, staged)
    rounds[0], late_index = lax.optimization_barrier((rounds[0], source_index))
    places, most = plan_places(late_index, chans, slots)

    def exchange(number, rows):
        rows = lax.all_to_all(rows, "chan", 0, 0, tiled=True)
        return pl.pallas_call(
            functools.partial(pick_kernel, slots, number * n * slots),
            out_shape=jax.ShapeDtypeStruct((HALF // n, depth, 2 * sources), jnp.bfloat16),
            compiler_params=params,
            name="pick",
        )(places, rows)

    picked = exchange(0, rounds[0])
    for number in range(1, pairs):
        picked = lax.cond(
            most > number * slots,
            lambda p, r, number=number: p + exchange(number, r),
            lambda p, r: p,
            picked,
            rounds[number],
        )
    picked, spectra = lax.optimization_barrier((picked, spectra))
    left = pl.pallas_call(
        functools.partial(left_kernel, chans, depth),
        in_specs=[vmem],
        out_specs=vmem,
        out_shape=jax.ShapeDtypeStruct((HALF, 4 * chans, LANES), jnp.bfloat16),
        compiler_params=params,
        cost_estimate=pl.CostEstimate(
            flops=10 * 1000 * 1000, bytes_accessed=8 * 1024 * 1024, transcendentals=0
        ),
        name="left",
    )(spectra)
    total_windows = wins * lax.axis_size("win")
    held_shape = jax.ShapeDtypeStruct((2 * chans * HALF_PITCH, LANES), jnp.float32)
    held = []

    def multiply(pieces, origins):
        held[:] = [
            pl.pallas_call(
                functools.partial(partial_kernel, n, origins, len(held)),
                in_specs=[smem, vmem] + [vmem] * (len(held) + len(pieces)),
                out_specs=vmem,
                out_shape=held_shape,
                input_output_aliases={2: 0} if held else {},
                compiler_params=params,
                cost_estimate=pl.CostEstimate(
                    flops=100 * 1000 * 1000, bytes_accessed=4 * 1024 * 1024, transcendentals=0
                ),
                name="products",
            )(me, left, *held, *pieces)
        ]

    def after_products(*arrays):
        *arrays, held[0] = lax.optimization_barrier((*arrays, held[0]))
        return arrays

    pieces, origins = gather_pieces(picked, multiply, after_products)
    stack, _ = pl.pallas_call(
        functools.partial(correlate_kernel, 1.0 / total_windows, n, origins, sources),
        in_specs=[smem, vmem, vmem] + [vmem] * len(pieces),
        out_specs=[pl.BlockSpec(memory_space=pl.ANY), vmem],
        out_shape=[jax.ShapeDtypeStruct((2, sources, chans, F), jnp.float32), held_shape],
        scratch_shapes=[
            pltpu.VMEM((2, 2 * sources * chans, HALF), jnp.float32),
            pltpu.SemaphoreType.DMA((chans // 4, 2)),
        ],
        input_output_aliases={2: 1},
        compiler_params=params,
        name="correlate",
    )(me, left, *held, *pieces)
    if lax.axis_size("win") == 1:
        return stack
    return lax.psum_scatter(stack, "win", scatter_dimension=1, tiled=True)


def solution(mesh):
    return jax.shard_map(
        per_device,
        mesh=mesh,
        in_specs=(P("chan", "win", None), P()),
        out_specs=P(None, "win", "chan", None),
        check_vma=False,
    )
```

```python
import functools
import math

import jax
import jax.numpy as jnp
import ml_dtypes
import numpy as np
from jax import lax
from jax.experimental import pallas as pl
from jax.experimental.pallas import tpu as pltpu
from jax.sharding import PartitionSpec as P

F = 256
HALF = 128
F0 = 1
K = 64
GAUGE = 4
LANES = 128
PITCH = F + 8
HALF_PITCH = HALF + 8
VMEM_LIMIT = 24 * 1024 * 1024


def make_table(length):
    times = np.arange(length, dtype=np.int64)[:, None]
    bins = np.arange(F, dtype=np.int64)[None, :] + F0
    phase = (times * bins % length).astype(np.float32) * np.float32(2.0 * math.pi / length)
    phase = phase.astype(np.float64)
    return np.concatenate([np.cos(phase), -np.sin(phase)], axis=1).astype(ml_dtypes.bfloat16)


def make_band():
    rows = np.arange(F)[:, None]
    cols = np.arange(F)[None, :]
    return (np.abs(rows - cols) <= K).astype(ml_dtypes.bfloat16)


def whiten_block(cur, upper, table_ref, band_ref, turned_ref, first):
    chans, wins, length = cur.shape
    rows = chans * wins
    diff = (upper.astype(jnp.float32) - cur.astype(jnp.float32)).reshape(rows, length)
    power = jnp.sum(diff * diff, axis=1, keepdims=True) * (1.0 / length)
    normed = (diff * lax.rsqrt(power + 1e-05)).astype(jnp.bfloat16)
    spec = jnp.dot(normed, table_ref[...], preferred_element_type=jnp.float32)
    real = spec[:, :F]
    imag = spec[:, F:]
    magnitude = jnp.sqrt(real * real + imag * imag).astype(jnp.bfloat16)
    bins = lax.broadcasted_iota(jnp.int32, (1, F), 1)
    counts = (jnp.minimum(bins, K) + jnp.minimum(F - 1 - bins, K) + 1).astype(jnp.float32)
    smooth = jnp.dot(magnitude, band_ref[...], preferred_element_type=jnp.float32) / counts
    gain = 1.0 / (smooth + 1e-06)
    white_re = (real * gain).astype(jnp.bfloat16).astype(jnp.float32)
    white_im = (imag * gain).astype(jnp.bfloat16).astype(jnp.float32)
    pad = jnp.zeros((LANES - 2 * wins, F), jnp.float32)
    for c in range(chans):
        mine = slice(c * wins, (c + 1) * wins)
        both = jnp.concatenate([white_re[mine], white_im[mine], pad], axis=0)
        turned_ref[(first + c) * PITCH : (first + c) * PITCH + F, :] = both.T


def list_slots(chans, me_ref, index_ref, slot_ref):
    mine = jnp.int32(0)
    for s in range(index_ref.shape[0]):
        local = index_ref[s] - me_ref[0] * chans
        bit = lax.shift_left(jnp.int32(1), jnp.clip(local, 0, chans - 1))
        mine = mine | jnp.where((local >= 0) & (local < chans), bit, 0)
    early = count = jnp.int32(0)
    for c in range(chans):
        slot_ref[count] = c
        count = count + (lax.shift_right_logical(mine, c) & 1)
        if c < chans - GAUGE:
            early = count
    slot_ref[chans + 1] = early
    slot_ref[chans + 2] = count


def lay_out(slot, channel, turned_ref, stage_ref, height, slots):
    dests = stage_ref.shape[1] // height
    per_dest = HALF // dests
    lane = lax.broadcasted_iota(jnp.int32, (dests, LANES), 1)
    for pair in range(per_dest // 2):
        piece = []
        for j in range(2):
            for half in range(2):
                at = channel * PITCH + half * HALF + pair * 2 + j
                piece.append(turned_ref[pl.ds(at, dests, stride=per_dest), :])
        a, b, c, d = piece
        b = pltpu.roll(b, 96, 1)
        c = pltpu.roll(c, 64, 1)
        d = pltpu.roll(d, 32, 1)
        rows_at = pl.ds(pair * slots + slot, dests, stride=height)
        stage_ref.at[0][rows_at, :] = jnp.where(lane < 96, a, b)
        stage_ref.at[1][rows_at, :] = jnp.where(lane < 64, b, c)
        stage_ref.at[2][rows_at, :] = jnp.where(lane < 32, c, d)


def whiten_kernel(
    height, slots, me_ref, index_ref, traces_ref, table_ref, band_ref, turned_ref, stage_ref, slot_ref
):
    chans = traces_ref.shape[0]
    stage_ref[...] = jnp.zeros_like(stage_ref)
    list_slots(chans, me_ref, index_ref, slot_ref)
    for c in range(0, chans - GAUGE, GAUGE):
        cur, upper = traces_ref[c : c + GAUGE], traces_ref[c + GAUGE : c + 2 * GAUGE]
        whiten_block(cur, upper, table_ref, band_ref, turned_ref, c)

    def one(slot, carry):
        lay_out(slot, slot_ref[slot], turned_ref, stage_ref, height, slots)
        return carry

    lax.fori_loop(0, jnp.minimum(slot_ref[chans + 1], slots), one, 0)


def finish_kernel(
    height, slots, slot_ref, traces_ref, halo_ref, table_ref, band_ref, _, __, turned_ref, stage_ref, *rounds
):
    chans = traces_ref.shape[0]
    early, count = slot_ref[chans + 1], slot_ref[chans + 2]
    cur = traces_ref[chans - GAUGE :]
    whiten_block(cur, halo_ref[...], table_ref, band_ref, turned_ref, chans - GAUGE)

    def fill(first, start, rows_ref):
        def one(slot, carry):
            channel = slot_ref[first + slot]
            lay_out(slot, channel, turned_ref, stage_ref, height, slots)
            return carry

        lax.fori_loop(start, jnp.minimum(count - first, slots), one, 0)
        for dest in range(rows_ref.shape[0]):
            for tile in range(3):
                block = stage_ref[tile, dest * height : (dest + 1) * height, :]
                rows_ref[dest, :, tile * LANES : (tile + 1) * LANES] = block.astype(jnp.bfloat16)

    def clear(rows_ref):
        rows_ref[...] = jnp.zeros_like(rows_ref)

    fill(0, early, rounds[0])
    for number in range(1, len(rounds)):
        more = count > number * slots
        pl.when(more)(functools.partial(fill, number * slots, 0, rounds[number]))
        pl.when(jnp.logical_not(more))(functools.partial(clear, rounds[number]))


def left_kernel(chans, depth, turned_ref, left_ref):
    lane = lax.broadcasted_iota(jnp.int32, (chans, LANES), 1)

    def one(g, carry):
        stack = []
        for half in range(2):
            real = turned_ref[pl.ds(half * HALF + g, chans, stride=PITCH), :]
            ahead = pltpu.roll(real, depth // 2, 1)
            back = pltpu.roll(real, LANES - depth // 2, 1)
            stack += [real, jnp.where(lane < depth // 2, -back, ahead)]
        left_ref[g] = jnp.concatenate(stack, axis=0).astype(jnp.bfloat16)
        return carry

    lax.fori_loop(0, HALF, one, 0, unroll=8)


def pick_kernel(slots, base, place_ref, rows_ref, out_ref):
    sources = place_ref.shape[0]
    dests, height, width = rows_ref.shape
    groups, depth, _ = out_ref.shape
    rows = rows_ref[...].reshape(dests * height, width)
    ids = lax.broadcasted_iota(jnp.int32, (sources, dests * height), 1)
    place = place_ref[...] - base
    inside = (place >= 0) & (place < dests * slots)
    spot = place // slots * height + place % slots
    for pair in range(groups // 2):
        hit = inside & (ids == spot + pair * slots)
        onehot = jnp.where(hit, 1.0, 0.0).astype(jnp.bfloat16)
        turned = jnp.dot(onehot, rows, preferred_element_type=jnp.float32).T
        for j in range(2):
            low = turned[(2 * j) * depth : (2 * j + 1) * depth]
            high = turned[(2 * j + 1) * depth : (2 * j + 2) * depth]
            out_ref[pair * 2 + j] = jnp.concatenate([low, high], axis=1).astype(jnp.bfloat16)


def products(n, origins, me_ref, left_ref, pieces, held):
    rows = left_ref.shape[1]
    depth, width = pieces[0].shape[-2:]
    groups = HALF // n
    sources = width // 2
    outs = rows // 2
    me = me_ref[0]
    lane = lax.broadcasted_iota(jnp.int32, (outs, width), 1)
    for piece, names in zip(pieces, origins):
        for place, (flip, index) in enumerate(names):
            g = (me ^ flip) * groups + index
            both = jnp.dot(left_ref[g][:, :depth], piece[place], preferred_element_type=jnp.float32)
            mine = jnp.where(lane < sources, both[:outs], both[outs:])
            held[pl.ds(g, outs, stride=HALF_PITCH), :] = mine


def partial_kernel(n, origins, chained, me_ref, left_ref, *refs):
    products(n, origins, me_ref, left_ref, refs[chained:-1], refs[-1])


def correlate_kernel(scale, n, origins, sources, me_ref, left_ref, _, *refs):
    pieces, (out_ref, held, turned_ref, sems) = refs[:-4], refs[-4:]
    products(n, origins, me_ref, left_ref, pieces, held)
    outs = held.shape[0] // HALF_PITCH
    chans = outs // 2
    group = 8
    copies = []
    for part in range(2):
        for c in range(chans):
            base = (part * chans + c) * HALF_PITCH
            turned = held[base : base + HALF, :].T * scale
            rows_at = pl.ds(part * sources * chans + c, sources, stride=chans)
            for half in range(2):
                turned_ref.at[half][rows_at, :] = turned[half * sources : (half + 1) * sources]
            if c % group == group - 1:
                span = pl.ds(c + 1 - group, group)
                for half in range(2):
                    block = turned_ref.at[half].reshape(2, sources, chans, HALF)
                    copy = pltpu.make_async_copy(
                        block.at[part, :, span, :],
                        out_ref.at[part, :, span, pl.ds(half * HALF, HALF)],
                        sems.at[part * (chans // group) + c // group, half],
                    )
                    copy.start()
                    copies.append(copy)
    for copy in copies:
        copy.wait()


def gather_pieces(own, multiply, after_products):
    n = lax.axis_size("chan")
    groups = own.shape[0]
    core, x, y, z, zz = 1, 2, 4, 8, 16
    place = {}

    def keep(array, names):
        for i, name in enumerate(names):
            place[name] = (array, i)
        return array, names

    def pack(names):
        parts = []
        for name in names:
            array, i = place[name]
            if parts and parts[-1][0] is array and parts[-1][2] == i:
                parts[-1][2] = i + 1
            else:
                parts.append([array, i, i + 1])
        blocks = [array[i:j] for array, i, j in parts]
        return blocks[0] if len(blocks) == 1 else jnp.concatenate(blocks, axis=0)

    def send(names, flip):
        route = [(i, i ^ flip) for i in range(n)]
        return lax.ppermute(pack(names), "chan", route), [(f ^ flip, g) for f, g in names]

    def lists(pairs):
        return [array for array, _ in pairs], [names for _, names in pairs]

    def piece(flip):
        return [(flip, g) for g in range(groups)]

    near = [keep(own, piece(0))]
    if n != 32:
        flip = 1
        while flip < n:
            near.append(keep(*send(sorted(place), flip)))
            flip *= 2
        multiply(*lists(near[:-1]))
        return lists(near[-1:])

    first = [send(piece(0), flip) for flip in (x ^ y, y, x, z, zz)]
    arrays = lax.optimization_barrier(lists(first)[0])
    near += [keep(array, names) for array, (_, names) in zip(arrays, first)]
    mid = [
        send(piece(z) + piece(zz), x),
        send(piece(z) + piece(zz), y),
        send(piece(x ^ y), zz),
        send(piece(zz) + piece(x ^ y), z),
    ]
    their_near = send([name for pair in near for name in pair[1]], core)
    multiply(*lists(near))
    arrays = after_products(*lists(mid)[0])
    mid = [keep(array, names) for array, (_, names) in zip(arrays, mid)]
    last = [
        send(piece(z ^ zz), x),
        send(piece(z ^ zz), y),
        send(piece(zz ^ x ^ y), z),
    ]
    their_mid = send([name for pair in mid for name in pair[1]], core)
    multiply(*lists(mid + [their_near]))
    arrays = after_products(*lists(last)[0])
    last = [keep(array, names) for array, (_, names) in zip(arrays, last)]
    assert sorted(place) == [(f, g) for f in range(0, n, 2) for g in range(groups)]
    final = send([name for pair in last for name in pair[1]], core)
    multiply(*lists([their_mid] + last))
    return lists([final])


def plan_places(source_index, chans, slots):
    n = lax.axis_size("chan")
    channels = jnp.arange(n * chans, dtype=jnp.int32)
    hits = source_index[:, None] == channels[None, :]
    listed = jnp.any(hits, axis=0).reshape(n, chans).astype(jnp.int32)
    below = (jnp.arange(chans)[:, None] < jnp.arange(chans)[None, :]).astype(jnp.int32)
    rank = jnp.sum(listed[:, :, None] * below[None], axis=1)
    device = jnp.arange(n, dtype=jnp.int32)[:, None]
    place = (rank // slots * n + device) * slots + rank % slots
    places = jnp.sum(jnp.where(hits, place.reshape(1, -1), 0), axis=1, keepdims=True)
    return places, jnp.max(jnp.sum(listed, axis=1))


def per_device(traces, source_index):
    chans, wins, length = traces.shape
    n = lax.axis_size("chan")
    sources = source_index.shape[0]
    halo = lax.ppermute(traces[:GAUGE], "chan", [(i + 1, i) for i in range(n - 1)])
    me = lax.axis_index("chan").astype(jnp.int32).reshape(1)
    table, band = jnp.asarray(make_table(length)), jnp.asarray(make_band())
    depth = 2 * wins
    row_width = HALF * 2 * depth // n
    vmem = pl.BlockSpec(memory_space=pltpu.VMEM)
    smem = pl.BlockSpec(memory_space=pltpu.SMEM)
    params = pltpu.CompilerParams(vmem_limit_bytes=VMEM_LIMIT)
    pairs = HALF // n // 2
    slots = chans // pairs
    turned = jax.ShapeDtypeStruct((chans * PITCH, LANES), jnp.float32)
    stage = jax.ShapeDtypeStruct((3, n * chans, LANES), jnp.float32)
    slot_list = jax.ShapeDtypeStruct((chans + 3,), jnp.int32)
    some, staged, listed = pl.pallas_call(
        functools.partial(whiten_kernel, chans, slots),
        in_specs=[smem] * 2 + [vmem] * 3,
        out_specs=[vmem, vmem, smem],
        out_shape=[turned, stage, slot_list],
        compiler_params=params,
        cost_estimate=pl.CostEstimate(
            flops=2 * (chans - GAUGE) * wins * (length + F // 2) * 2 * F,
            bytes_accessed=8 * 1024 * 1024,
            transcendentals=0,
        ),
        name="whiten",
    )(me, source_index, traces, table, band)
    rows_shape = jax.ShapeDtypeStruct((n, chans, row_width // pairs), jnp.bfloat16)
    spectra, _, *rounds = pl.pallas_call(
        functools.partial(finish_kernel, chans, slots),
        in_specs=[smem] + [vmem] * 6,
        out_specs=[vmem] * (2 + pairs),
        out_shape=[turned, stage] + [rows_shape] * pairs,
        input_output_aliases={5: 0, 6: 1},
        compiler_params=params,
        name="finish",
    )(listed, traces, halo, table, band, some, staged)
    rounds[0], late_index = lax.optimization_barrier((rounds[0], source_index))
    places, most = plan_places(late_index, chans, slots)

    def exchange(number, rows):
        rows = lax.all_to_all(rows, "chan", 0, 0, tiled=True)
        return pl.pallas_call(
            functools.partial(pick_kernel, slots, number * n * slots),
            out_shape=jax.ShapeDtypeStruct((HALF // n, depth, 2 * sources), jnp.bfloat16),
            compiler_params=params,
            name="pick",
        )(places, rows)

    picked = exchange(0, rounds[0])
    for number in range(1, pairs):
        picked = lax.cond(
            most > number * slots,
            lambda p, r, number=number: p + exchange(number, r),
            lambda p, r: p,
            picked,
            rounds[number],
        )
    picked, spectra = lax.optimization_barrier((picked, spectra))
    left = pl.pallas_call(
        functools.partial(left_kernel, chans, depth),
        in_specs=[vmem],
        out_specs=vmem,
        out_shape=jax.ShapeDtypeStruct((HALF, 4 * chans, LANES), jnp.bfloat16),
        compiler_params=params,
        cost_estimate=pl.CostEstimate(
            flops=10 * 1000 * 1000, bytes_accessed=8 * 1024 * 1024, transcendentals=0
        ),
        name="left",
    )(spectra)
    total_windows = wins * lax.axis_size("win")
    held_shape = jax.ShapeDtypeStruct((2 * chans * HALF_PITCH, LANES), jnp.float32)
    held = []

    def multiply(pieces, origins):
        held[:] = [
            pl.pallas_call(
                functools.partial(partial_kernel, n, origins, len(held)),
                in_specs=[smem, vmem] + [vmem] * (len(held) + len(pieces)),
                out_specs=vmem,
                out_shape=held_shape,
                input_output_aliases={2: 0} if held else {},
                compiler_params=params,
                cost_estimate=pl.CostEstimate(
                    flops=100 * 1000 * 1000, bytes_accessed=4 * 1024 * 1024, transcendentals=0
                ),
                name="products",
            )(me, left, *held, *pieces)
        ]

    def after_products(*arrays):
        *arrays, held[0] = lax.optimization_barrier((*arrays, held[0]))
        return arrays

    pieces, origins = gather_pieces(picked, multiply, after_products)
    stack, _ = pl.pallas_call(
        functools.partial(correlate_kernel, 1.0 / total_windows, n, origins, sources),
        in_specs=[smem, vmem, vmem] + [vmem] * len(pieces),
        out_specs=[pl.BlockSpec(memory_space=pl.ANY), vmem],
        out_shape=[jax.ShapeDtypeStruct((2, sources, chans, F), jnp.float32), held_shape],
        scratch_shapes=[
            pltpu.VMEM((2, 2 * sources * chans, HALF), jnp.float32),
            pltpu.SemaphoreType.DMA((chans // 4, 2)),
        ],
        input_output_aliases={2: 1},
        compiler_params=params,
        name="correlate",
    )(me, left, *held, *pieces)
    if lax.axis_size("win") == 1:
        return stack
    return lax.psum_scatter(stack, "win", scatter_dimension=1, tiled=True)


def solution(mesh):
    return jax.shard_map(
        per_device,
        mesh=mesh,
        in_specs=(P("chan", "win", None), P()),
        out_specs=P(None, "win", "chan", None),
        check_vma=False,
    )
```

```python
import functools
import math

import jax
import jax.numpy as jnp
import ml_dtypes
import numpy as np
from jax import lax
from jax.experimental import pallas as pl
from jax.experimental.pallas import tpu as pltpu
from jax.sharding import PartitionSpec as P

F = 256
HALF = 128
F0 = 1
K = 64
GAUGE = 4
LANES = 128
PITCH = F + 8
HALF_PITCH = HALF + 8
VMEM_LIMIT = 24 * 1024 * 1024


def make_table(length):
    times = np.arange(length, dtype=np.int64)[:, None]
    bins = np.arange(F, dtype=np.int64)[None, :] + F0
    phase = (times * bins % length).astype(np.float32) * np.float32(2.0 * math.pi / length)
    phase = phase.astype(np.float64)
    return np.concatenate([np.cos(phase), -np.sin(phase)], axis=1).astype(ml_dtypes.bfloat16)


def make_band():
    rows = np.arange(F)[:, None]
    cols = np.arange(F)[None, :]
    return (np.abs(rows - cols) <= K).astype(ml_dtypes.bfloat16)


def whiten_block(cur, upper, table_ref, band_ref, turned_ref, first):
    chans, wins, length = cur.shape
    rows = chans * wins
    diff = (upper.astype(jnp.float32) - cur.astype(jnp.float32)).reshape(rows, length)
    power = jnp.sum(diff * diff, axis=1, keepdims=True) * (1.0 / length)
    normed = (diff * lax.rsqrt(power + 1e-05)).astype(jnp.bfloat16)
    spec = jnp.dot(normed, table_ref[...], preferred_element_type=jnp.float32)
    real = spec[:, :F]
    imag = spec[:, F:]
    magnitude = jnp.sqrt(real * real + imag * imag).astype(jnp.bfloat16)
    bins = lax.broadcasted_iota(jnp.int32, (1, F), 1)
    counts = (jnp.minimum(bins, K) + jnp.minimum(F - 1 - bins, K) + 1).astype(jnp.float32)
    smooth = jnp.dot(magnitude, band_ref[...], preferred_element_type=jnp.float32) / counts
    gain = 1.0 / (smooth + 1e-06)
    white_re = (real * gain).astype(jnp.bfloat16).astype(jnp.float32)
    white_im = (imag * gain).astype(jnp.bfloat16).astype(jnp.float32)
    pad = jnp.zeros((LANES - 2 * wins, F), jnp.float32)
    for c in range(chans):
        mine = slice(c * wins, (c + 1) * wins)
        both = jnp.concatenate([white_re[mine], white_im[mine], pad], axis=0)
        turned_ref[(first + c) * PITCH : (first + c) * PITCH + F, :] = both.T


def list_slots(chans, me_ref, index_ref, slot_ref):
    mine = jnp.int32(0)
    for s in range(index_ref.shape[0]):
        local = index_ref[s] - me_ref[0] * chans
        bit = lax.shift_left(jnp.int32(1), jnp.clip(local, 0, chans - 1))
        mine = mine | jnp.where((local >= 0) & (local < chans), bit, 0)
    early = count = jnp.int32(0)
    for c in range(chans):
        slot_ref[count] = c
        count = count + (lax.shift_right_logical(mine, c) & 1)
        if c < chans - GAUGE:
            early = count
    slot_ref[chans + 1] = early
    slot_ref[chans + 2] = count


def lay_out(slot, channel, turned_ref, stage_ref, height, slots):
    dests = stage_ref.shape[1] // height
    per_dest = HALF // dests
    lane = lax.broadcasted_iota(jnp.int32, (dests, LANES), 1)
    for pair in range(per_dest // 2):
        piece = []
        for j in range(2):
            for half in range(2):
                at = channel * PITCH + half * HALF + pair * 2 + j
                piece.append(turned_ref[pl.ds(at, dests, stride=per_dest), :])
        a, b, c, d = piece
        b = pltpu.roll(b, 96, 1)
        c = pltpu.roll(c, 64, 1)
        d = pltpu.roll(d, 32, 1)
        rows_at = pl.ds(pair * slots + slot, dests, stride=height)
        stage_ref.at[0][rows_at, :] = jnp.where(lane < 96, a, b)
        stage_ref.at[1][rows_at, :] = jnp.where(lane < 64, b, c)
        stage_ref.at[2][rows_at, :] = jnp.where(lane < 32, c, d)


def whiten_kernel(
    height, slots, me_ref, index_ref, traces_ref, table_ref, band_ref, turned_ref, stage_ref, slot_ref
):
    chans = traces_ref.shape[0]
    stage_ref[...] = jnp.zeros_like(stage_ref)
    list_slots(chans, me_ref, index_ref, slot_ref)
    for c in range(0, chans - GAUGE, GAUGE):
        cur, upper = traces_ref[c : c + GAUGE], traces_ref[c + GAUGE : c + 2 * GAUGE]
        whiten_block(cur, upper, table_ref, band_ref, turned_ref, c)

    def one(slot, carry):
        lay_out(slot, slot_ref[slot], turned_ref, stage_ref, height, slots)
        return carry

    lax.fori_loop(0, jnp.minimum(slot_ref[chans + 1], slots), one, 0)


def finish_kernel(
    height, slots, slot_ref, traces_ref, halo_ref, table_ref, band_ref, _, __, turned_ref, stage_ref, *rounds
):
    chans = traces_ref.shape[0]
    early, count = slot_ref[chans + 1], slot_ref[chans + 2]
    cur = traces_ref[chans - GAUGE :]
    whiten_block(cur, halo_ref[...], table_ref, band_ref, turned_ref, chans - GAUGE)

    def fill(first, start, rows_ref):
        def one(slot, carry):
            channel = slot_ref[first + slot]
            lay_out(slot, channel, turned_ref, stage_ref, height, slots)
            return carry

        lax.fori_loop(start, jnp.minimum(count - first, slots), one, 0)
        for dest in range(rows_ref.shape[0]):
            for tile in range(3):
                block = stage_ref[tile, dest * height : (dest + 1) * height, :]
                rows_ref[dest, :, tile * LANES : (tile + 1) * LANES] = block.astype(jnp.bfloat16)

    def clear(rows_ref):
        rows_ref[...] = jnp.zeros_like(rows_ref)

    fill(0, early, rounds[0])
    for number in range(1, len(rounds)):
        more = count > number * slots
        pl.when(more)(functools.partial(fill, number * slots, 0, rounds[number]))
        pl.when(jnp.logical_not(more))(functools.partial(clear, rounds[number]))


def left_kernel(chans, depth, turned_ref, left_ref):
    lane = lax.broadcasted_iota(jnp.int32, (chans, LANES), 1)

    def one(g, carry):
        stack = []
        for half in range(2):
            real = turned_ref[pl.ds(half * HALF + g, chans, stride=PITCH), :]
            ahead = pltpu.roll(real, depth // 2, 1)
            back = pltpu.roll(real, LANES - depth // 2, 1)
            stack += [real, jnp.where(lane < depth // 2, -back, ahead)]
        left_ref[g] = jnp.concatenate(stack, axis=0).astype(jnp.bfloat16)
        return carry

    lax.fori_loop(0, HALF, one, 0, unroll=8)


def pick_kernel(slots, base, place_ref, rows_ref, out_ref):
    sources = place_ref.shape[0]
    dests, height, width = rows_ref.shape
    groups, depth, _ = out_ref.shape
    rows = rows_ref[...].reshape(dests * height, width)
    ids = lax.broadcasted_iota(jnp.int32, (sources, dests * height), 1)
    place = place_ref[...] - base
    inside = (place >= 0) & (place < dests * slots)
    spot = place // slots * height + place % slots
    for pair in range(groups // 2):
        hit = inside & (ids == spot + pair * slots)
        onehot = jnp.where(hit, 1.0, 0.0).astype(jnp.bfloat16)
        turned = jnp.dot(onehot, rows, preferred_element_type=jnp.float32).T
        for j in range(2):
            low = turned[(2 * j) * depth : (2 * j + 1) * depth]
            high = turned[(2 * j + 1) * depth : (2 * j + 2) * depth]
            out_ref[pair * 2 + j] = jnp.concatenate([low, high], axis=1).astype(jnp.bfloat16)


def products(n, origins, me_ref, left_ref, pieces, held):
    rows = left_ref.shape[1]
    depth, width = pieces[0].shape[-2:]
    groups = HALF // n
    sources = width // 2
    outs = rows // 2
    me = me_ref[0]
    lane = lax.broadcasted_iota(jnp.int32, (outs, width), 1)
    for piece, names in zip(pieces, origins):
        for place, (flip, index) in enumerate(names):
            g = (me ^ flip) * groups + index
            both = jnp.dot(left_ref[g][:, :depth], piece[place], preferred_element_type=jnp.float32)
            mine = jnp.where(lane < sources, both[:outs], both[outs:])
            held[pl.ds(g, outs, stride=HALF_PITCH), :] = mine


def partial_kernel(n, origins, chained, me_ref, left_ref, *refs):
    products(n, origins, me_ref, left_ref, refs[chained:-1], refs[-1])


def correlate_kernel(scale, n, origins, sources, me_ref, left_ref, _, *refs):
    pieces, (out_ref, held, turned_ref, sems) = refs[:-4], refs[-4:]
    products(n, origins, me_ref, left_ref, pieces, held)
    outs = held.shape[0] // HALF_PITCH
    chans = outs // 2
    group = 8
    copies = []
    for part in range(2):
        for c in range(chans):
            base = (part * chans + c) * HALF_PITCH
            turned = held[base : base + HALF, :].T * scale
            rows_at = pl.ds(part * sources * chans + c, sources, stride=chans)
            for half in range(2):
                turned_ref.at[half][rows_at, :] = turned[half * sources : (half + 1) * sources]
            if c % group == group - 1:
                span = pl.ds(c + 1 - group, group)
                for half in range(2):
                    block = turned_ref.at[half].reshape(2, sources, chans, HALF)
                    copy = pltpu.make_async_copy(
                        block.at[part, :, span, :],
                        out_ref.at[part, :, span, pl.ds(half * HALF, HALF)],
                        sems.at[part * (chans // group) + c // group, half],
                    )
                    copy.start()
                    copies.append(copy)
    for copy in copies:
        copy.wait()


def gather_pieces(own, multiply, after_products):
    n = lax.axis_size("chan")
    groups = own.shape[0]
    core, x, y, z, zz = 1, 2, 4, 8, 16
    place = {}

    def keep(array, names):
        for i, name in enumerate(names):
            place[name] = (array, i)
        return array, names

    def pack(names):
        parts = []
        for name in names:
            array, i = place[name]
            if parts and parts[-1][0] is array and parts[-1][2] == i:
                parts[-1][2] = i + 1
            else:
                parts.append([array, i, i + 1])
        blocks = [array[i:j] for array, i, j in parts]
        return blocks[0] if len(blocks) == 1 else jnp.concatenate(blocks, axis=0)

    def send(names, flip):
        route = [(i, i ^ flip) for i in range(n)]
        return lax.ppermute(pack(names), "chan", route), [(f ^ flip, g) for f, g in names]

    def lists(pairs):
        return [array for array, _ in pairs], [names for _, names in pairs]

    def piece(flip):
        return [(flip, g) for g in range(groups)]

    near = [keep(own, piece(0))]
    if n != 32:
        flip = 1
        while flip < n:
            near.append(keep(*send(sorted(place), flip)))
            flip *= 2
        multiply(*lists(near[:-1]))
        return lists(near[-1:])

    first = [send(piece(0), flip) for flip in (x ^ y, y, x, z, zz)]
    arrays = lax.optimization_barrier(lists(first)[0])
    near += [keep(array, names) for array, (_, names) in zip(arrays, first)]
    mid = [
        send(piece(z) + piece(zz), x),
        send(piece(z) + piece(zz), y),
        send(piece(x ^ y), zz),
        send(piece(zz) + piece(x ^ y), z),
    ]
    multiply(*lists(near))
    arrays = after_products(*lists(mid)[0])
    mid = [keep(array, names) for array, (_, names) in zip(arrays, mid)]
    last = [
        send(piece(z ^ zz), x),
        send(piece(z ^ zz), y),
        send(piece(zz ^ x ^ y), z),
    ]
    theirs = send([name for pair in near + mid for name in pair[1]], core)
    multiply(*lists(mid))
    arrays = after_products(*lists(last)[0])
    last = [keep(array, names) for array, (_, names) in zip(arrays, last)]
    assert sorted(place) == [(f, g) for f in range(0, n, 2) for g in range(groups)]
    final = send([name for pair in last for name in pair[1]], core)
    multiply(*lists([theirs] + last))
    return lists([final])


def plan_places(source_index, chans, slots):
    n = lax.axis_size("chan")
    channels = jnp.arange(n * chans, dtype=jnp.int32)
    hits = source_index[:, None] == channels[None, :]
    listed = jnp.any(hits, axis=0).reshape(n, chans).astype(jnp.int32)
    below = (jnp.arange(chans)[:, None] < jnp.arange(chans)[None, :]).astype(jnp.int32)
    rank = jnp.sum(listed[:, :, None] * below[None], axis=1)
    device = jnp.arange(n, dtype=jnp.int32)[:, None]
    place = (rank // slots * n + device) * slots + rank % slots
    places = jnp.sum(jnp.where(hits, place.reshape(1, -1), 0), axis=1, keepdims=True)
    return places, jnp.max(jnp.sum(listed, axis=1))


def per_device(traces, source_index):
    chans, wins, length = traces.shape
    n = lax.axis_size("chan")
    sources = source_index.shape[0]
    halo = lax.ppermute(traces[:GAUGE], "chan", [(i + 1, i) for i in range(n - 1)])
    me = lax.axis_index("chan").astype(jnp.int32).reshape(1)
    table, band = jnp.asarray(make_table(length)), jnp.asarray(make_band())
    depth = 2 * wins
    row_width = HALF * 2 * depth // n
    vmem = pl.BlockSpec(memory_space=pltpu.VMEM)
    smem = pl.BlockSpec(memory_space=pltpu.SMEM)
    params = pltpu.CompilerParams(vmem_limit_bytes=VMEM_LIMIT)
    pairs = HALF // n // 2
    slots = chans // pairs
    turned = jax.ShapeDtypeStruct((chans * PITCH, LANES), jnp.float32)
    stage = jax.ShapeDtypeStruct((3, n * chans, LANES), jnp.float32)
    slot_list = jax.ShapeDtypeStruct((chans + 3,), jnp.int32)
    some, staged, listed = pl.pallas_call(
        functools.partial(whiten_kernel, chans, slots),
        in_specs=[smem] * 2 + [vmem] * 3,
        out_specs=[vmem, vmem, smem],
        out_shape=[turned, stage, slot_list],
        compiler_params=params,
        cost_estimate=pl.CostEstimate(
            flops=2 * (chans - GAUGE) * wins * (length + F // 2) * 2 * F,
            bytes_accessed=8 * 1024 * 1024,
            transcendentals=0,
        ),
        name="whiten",
    )(me, source_index, traces, table, band)
    rows_shape = jax.ShapeDtypeStruct((n, chans, row_width // pairs), jnp.bfloat16)
    spectra, _, *rounds = pl.pallas_call(
        functools.partial(finish_kernel, chans, slots),
        in_specs=[smem] + [vmem] * 6,
        out_specs=[vmem] * (2 + pairs),
        out_shape=[turned, stage] + [rows_shape] * pairs,
        input_output_aliases={5: 0, 6: 1},
        compiler_params=params,
        name="finish",
    )(listed, traces, halo, table, band, some, staged)
    rounds[0], late_index = lax.optimization_barrier((rounds[0], source_index))
    places, most = plan_places(late_index, chans, slots)

    def exchange(number, rows):
        rows = lax.all_to_all(rows, "chan", 0, 0, tiled=True)
        return pl.pallas_call(
            functools.partial(pick_kernel, slots, number * n * slots),
            out_shape=jax.ShapeDtypeStruct((HALF // n, depth, 2 * sources), jnp.bfloat16),
            compiler_params=params,
            name="pick",
        )(places, rows)

    picked = exchange(0, rounds[0])
    for number in range(1, pairs):
        picked = lax.cond(
            most > number * slots,
            lambda p, r, number=number: p + exchange(number, r),
            lambda p, r: p,
            picked,
            rounds[number],
        )
    picked, spectra = lax.optimization_barrier((picked, spectra))
    left = pl.pallas_call(
        functools.partial(left_kernel, chans, depth),
        in_specs=[vmem],
        out_specs=vmem,
        out_shape=jax.ShapeDtypeStruct((HALF, 4 * chans, LANES), jnp.bfloat16),
        compiler_params=params,
        cost_estimate=pl.CostEstimate(
            flops=10 * 1000 * 1000, bytes_accessed=8 * 1024 * 1024, transcendentals=0
        ),
        name="left",
    )(spectra)
    total_windows = wins * lax.axis_size("win")
    held_shape = jax.ShapeDtypeStruct((2 * chans * HALF_PITCH, LANES), jnp.float32)
    held = []

    def multiply(pieces, origins):
        held[:] = [
            pl.pallas_call(
                functools.partial(partial_kernel, n, origins, len(held)),
                in_specs=[smem, vmem] + [vmem] * (len(held) + len(pieces)),
                out_specs=vmem,
                out_shape=held_shape,
                input_output_aliases={2: 0} if held else {},
                compiler_params=params,
                cost_estimate=pl.CostEstimate(
                    flops=100 * 1000 * 1000, bytes_accessed=4 * 1024 * 1024, transcendentals=0
                ),
                name="products",
            )(me, left, *held, *pieces)
        ]

    def after_products(*arrays):
        *arrays, held[0] = lax.optimization_barrier((*arrays, held[0]))
        return arrays

    pieces, origins = gather_pieces(picked, multiply, after_products)
    stack, _ = pl.pallas_call(
        functools.partial(correlate_kernel, 1.0 / total_windows, n, origins, sources),
        in_specs=[smem, vmem, vmem] + [vmem] * len(pieces),
        out_specs=[pl.BlockSpec(memory_space=pl.ANY), vmem],
        out_shape=[jax.ShapeDtypeStruct((2, sources, chans, F), jnp.float32), held_shape],
        scratch_shapes=[
            pltpu.VMEM((2, 2 * sources * chans, HALF), jnp.float32),
            pltpu.SemaphoreType.DMA((chans // 4, 2)),
        ],
        input_output_aliases={2: 1},
        compiler_params=params,
        name="correlate",
    )(me, left, *held, *pieces)
    if lax.axis_size("win") == 1:
        return stack
    return lax.psum_scatter(stack, "win", scatter_dimension=1, tiled=True)


def solution(mesh):
    return jax.shard_map(
        per_device,
        mesh=mesh,
        in_specs=(P("chan", "win", None), P()),
        out_specs=P(None, "win", "chan", None),
        check_vma=False,
    )
```

```python
import functools
import math

import jax
import jax.numpy as jnp
import ml_dtypes
import numpy as np
from jax import lax
from jax.experimental import pallas as pl
from jax.experimental.pallas import tpu as pltpu
from jax.sharding import PartitionSpec as P

F = 256
HALF = 128
F0 = 1
K = 64
GAUGE = 4
LANES = 128
PITCH = F + 8
HALF_PITCH = HALF + 8
VMEM_LIMIT = 24 * 1024 * 1024


def make_table(length):
    times = np.arange(length, dtype=np.int64)[:, None]
    bins = np.arange(F, dtype=np.int64)[None, :] + F0
    phase = (times * bins % length).astype(np.float32) * np.float32(2.0 * math.pi / length)
    phase = phase.astype(np.float64)
    return np.concatenate([np.cos(phase), -np.sin(phase)], axis=1).astype(ml_dtypes.bfloat16)


def make_band():
    rows = np.arange(F)[:, None]
    cols = np.arange(F)[None, :]
    return (np.abs(rows - cols) <= K).astype(ml_dtypes.bfloat16)


def whiten_block(cur, upper, table_ref, band_ref, turned_ref, first):
    chans, wins, length = cur.shape
    rows = chans * wins
    diff = (upper.astype(jnp.float32) - cur.astype(jnp.float32)).reshape(rows, length)
    power = jnp.sum(diff * diff, axis=1, keepdims=True) * (1.0 / length)
    normed = (diff * lax.rsqrt(power + 1e-05)).astype(jnp.bfloat16)
    spec = jnp.dot(normed, table_ref[...], preferred_element_type=jnp.float32)
    real = spec[:, :F]
    imag = spec[:, F:]
    magnitude = jnp.sqrt(real * real + imag * imag).astype(jnp.bfloat16)
    bins = lax.broadcasted_iota(jnp.int32, (1, F), 1)
    counts = (jnp.minimum(bins, K) + jnp.minimum(F - 1 - bins, K) + 1).astype(jnp.float32)
    smooth = jnp.dot(magnitude, band_ref[...], preferred_element_type=jnp.float32) * (1.0 / counts)
    gain = 1.0 / (smooth + 1e-06)
    white_re = (real * gain).astype(jnp.bfloat16).astype(jnp.float32)
    white_im = (imag * gain).astype(jnp.bfloat16).astype(jnp.float32)
    pad = jnp.zeros((LANES - 2 * wins, F), jnp.float32)
    for c in range(chans):
        mine = slice(c * wins, (c + 1) * wins)
        both = jnp.concatenate([white_re[mine], white_im[mine], pad], axis=0)
        turned_ref[(first + c) * PITCH : (first + c) * PITCH + F, :] = both.T


def list_slots(chans, me_ref, index_ref, slot_ref):
    mine = jnp.int32(0)
    for s in range(index_ref.shape[0]):
        local = index_ref[s] - me_ref[0] * chans
        bit = lax.shift_left(jnp.int32(1), jnp.clip(local, 0, chans - 1))
        mine = mine | jnp.where((local >= 0) & (local < chans), bit, 0)
    early = count = jnp.int32(0)
    for c in range(chans):
        slot_ref[count] = c
        count = count + (lax.shift_right_logical(mine, c) & 1)
        if c < chans - GAUGE:
            early = count
    slot_ref[chans + 1] = early
    slot_ref[chans + 2] = count


def lay_out(slot, channel, turned_ref, stage_ref, height, slots):
    dests = stage_ref.shape[1] // height - 1
    per_dest = HALF // dests
    lane = lax.broadcasted_iota(jnp.int32, (dests, LANES), 1)
    for pair in range(per_dest // 2):
        piece = []
        for j in range(2):
            for half in range(2):
                at = channel * PITCH + half * HALF + pair * 2 + j
                piece.append(turned_ref[pl.ds(at, dests, stride=per_dest), :])
        a, b, c, d = piece
        b = pltpu.roll(b, 96, 1)
        c = pltpu.roll(c, 64, 1)
        d = pltpu.roll(d, 32, 1)
        rows_at = pl.ds(pair * slots + slot, dests, stride=height)
        stage_ref.at[0][rows_at, :] = jnp.where(lane < 96, a, b)
        stage_ref.at[1][rows_at, :] = jnp.where(lane < 64, b, c)
        stage_ref.at[2][rows_at, :] = jnp.where(lane < 32, c, d)


def whiten_kernel(
    height, slots, me_ref, index_ref, traces_ref, table_ref, band_ref, turned_ref, stage_ref, slot_ref
):
    chans = traces_ref.shape[0]
    stage_ref[...] = jnp.zeros_like(stage_ref)
    list_slots(chans, me_ref, index_ref, slot_ref)
    for c in range(0, chans - GAUGE, GAUGE):
        cur, upper = traces_ref[c : c + GAUGE], traces_ref[c + GAUGE : c + 2 * GAUGE]
        whiten_block(cur, upper, table_ref, band_ref, turned_ref, c)

    def one(slot, carry):
        lay_out(slot, slot_ref[slot], turned_ref, stage_ref, height, slots)
        return carry

    lax.fori_loop(0, jnp.minimum(slot_ref[chans + 1], slots), one, 0)


def finish_kernel(
    height, slots, slot_ref, traces_ref, halo_ref, table_ref, band_ref, _, __, turned_ref, stage_ref, *rounds
):
    chans = traces_ref.shape[0]
    early, count = slot_ref[chans + 1], slot_ref[chans + 2]
    cur = traces_ref[chans - GAUGE :]
    whiten_block(cur, halo_ref[...], table_ref, band_ref, turned_ref, chans - GAUGE)

    def fill(first, start, rows_ref):
        def one(slot, carry):
            channel = slot_ref[first + slot]
            lay_out(slot, channel, turned_ref, stage_ref, height, slots)
            return carry

        lax.fori_loop(start, jnp.minimum(count - first, slots), one, 0)
        for dest in range(rows_ref.shape[0]):
            for tile in range(3):
                block = stage_ref[tile, dest * height : (dest + 1) * height, :]
                rows_ref[dest, :, tile * LANES : (tile + 1) * LANES] = block.astype(jnp.bfloat16)

    def clear(rows_ref):
        rows_ref[...] = jnp.zeros_like(rows_ref)

    fill(0, early, rounds[0])
    for number in range(1, len(rounds)):
        more = count > number * slots
        pl.when(more)(functools.partial(fill, number * slots, 0, rounds[number]))
        pl.when(jnp.logical_not(more))(functools.partial(clear, rounds[number]))


def left_kernel(chans, depth, turned_ref, left_ref):
    lane = lax.broadcasted_iota(jnp.int32, (chans, LANES), 1)

    def one(g, carry):
        stack = []
        for half in range(2):
            real = turned_ref[pl.ds(half * HALF + g, chans, stride=PITCH), :]
            ahead = pltpu.roll(real, depth // 2, 1)
            back = pltpu.roll(real, LANES - depth // 2, 1)
            stack += [real, jnp.where(lane < depth // 2, -back, ahead)]
        left_ref[g] = jnp.concatenate(stack, axis=0).astype(jnp.bfloat16)
        return carry

    lax.fori_loop(0, HALF, one, 0, unroll=8)


def pick_kernel(slots, base, place_ref, rows_ref, out_ref):
    sources = place_ref.shape[0]
    dests, height, width = rows_ref.shape
    groups, depth, _ = out_ref.shape
    rows = rows_ref[...].reshape(dests * height, width)
    ids = lax.broadcasted_iota(jnp.int32, (sources, dests * height), 1)
    place = place_ref[...] - base
    inside = (place >= 0) & (place < dests * slots)
    spot = place // slots * height + place % slots
    for pair in range(groups // 2):
        hit = inside & (ids == spot + pair * slots)
        onehot = jnp.where(hit, 1.0, 0.0).astype(jnp.bfloat16)
        turned = jnp.dot(onehot, rows, preferred_element_type=jnp.float32).T
        for j in range(2):
            low = turned[(2 * j) * depth : (2 * j + 1) * depth]
            high = turned[(2 * j + 1) * depth : (2 * j + 2) * depth]
            out_ref[pair * 2 + j] = jnp.concatenate([low, high], axis=1).astype(jnp.bfloat16)


def products(n, origins, me_ref, left_ref, pieces, held):
    rows = left_ref.shape[1]
    depth, width = pieces[0].shape[-2:]
    groups = HALF // n
    sources = width // 2
    outs = rows // 2
    me = me_ref[0]
    lane = lax.broadcasted_iota(jnp.int32, (outs, width), 1)
    for piece, names in zip(pieces, origins):
        for place, (flip, index) in enumerate(names):
            g = (me ^ flip) * groups + index
            both = jnp.dot(left_ref[g][:, :depth], piece[place], preferred_element_type=jnp.float32)
            mine = jnp.where(lane < sources, both[:outs], both[outs:])
            held[pl.ds(g, outs, stride=HALF_PITCH), :] = mine


def partial_kernel(n, origins, chained, me_ref, left_ref, *refs):
    products(n, origins, me_ref, left_ref, refs[chained:-1], refs[-1])


def correlate_kernel(scale, n, origins, sources, me_ref, left_ref, _, *refs):
    pieces, (out_ref, held, turned_ref, sems) = refs[:-4], refs[-4:]
    products(n, origins, me_ref, left_ref, pieces, held)
    outs = held.shape[0] // HALF_PITCH
    chans = outs // 2
    group = 8
    copies = []
    for part in range(2):
        for c in range(chans):
            base = (part * chans + c) * HALF_PITCH
            turned = held[base : base + HALF, :].T * scale
            rows_at = pl.ds(part * sources * chans + c, sources, stride=chans)
            for half in range(2):
                turned_ref.at[half][rows_at, :] = turned[half * sources : (half + 1) * sources]
            if c % group == group - 1:
                span = pl.ds(c + 1 - group, group)
                for half in range(2):
                    block = turned_ref.at[half].reshape(2, sources, chans, HALF)
                    copy = pltpu.make_async_copy(
                        block.at[part, :, span, :],
                        out_ref.at[part, :, span, pl.ds(half * HALF, HALF)],
                        sems.at[part * (chans // group) + c // group, half],
                    )
                    copy.start()
                    copies.append(copy)
    for copy in copies:
        copy.wait()


def gather_pieces(own, multiply, after_products):
    n = lax.axis_size("chan")
    groups = own.shape[0]
    core, x, y, z, zz = 1, 2, 4, 8, 16
    place = {}

    def keep(array, names):
        for i, name in enumerate(names):
            place[name] = (array, i)
        return array, names

    def pack(names):
        parts = []
        for name in names:
            array, i = place[name]
            if parts and parts[-1][0] is array and parts[-1][2] == i:
                parts[-1][2] = i + 1
            else:
                parts.append([array, i, i + 1])
        blocks = [array[i:j] for array, i, j in parts]
        return blocks[0] if len(blocks) == 1 else jnp.concatenate(blocks, axis=0)

    def send(names, flip):
        route = [(i, i ^ flip) for i in range(n)]
        return lax.ppermute(pack(names), "chan", route), [(f ^ flip, g) for f, g in names]

    def lists(pairs):
        return [array for array, _ in pairs], [names for _, names in pairs]

    def piece(flip):
        return [(flip, g) for g in range(groups)]

    near = [keep(own, piece(0))]
    if n != 32:
        flip = 1
        while flip < n:
            near.append(keep(*send(sorted(place), flip)))
            flip *= 2
        multiply(*lists(near[:-1]))
        return lists(near[-1:])

    first = [send(piece(0), flip) for flip in (x ^ y, y, x, z, zz)]
    arrays = lax.optimization_barrier(lists(first)[0])
    near += [keep(array, names) for array, (_, names) in zip(arrays, first)]
    mid = [
        send(piece(z) + piece(zz), x),
        send(piece(z) + piece(zz), y),
        send(piece(x ^ y), zz),
        send(piece(zz) + piece(x ^ y), z),
    ]
    multiply(*lists(near))
    arrays = after_products(*lists(mid)[0])
    mid = [keep(array, names) for array, (_, names) in zip(arrays, mid)]
    last = [
        send(piece(z ^ zz), x),
        send(piece(z ^ zz), y),
        send(piece(zz ^ x ^ y), z),
    ]
    theirs = send([name for pair in near + mid for name in pair[1]], core)
    multiply(*lists(mid))
    arrays = after_products(*lists(last)[0])
    last = [keep(array, names) for array, (_, names) in zip(arrays, last)]
    assert sorted(place) == [(f, g) for f in range(0, n, 2) for g in range(groups)]
    final = send([name for pair in last for name in pair[1]], core)
    multiply(*lists([theirs] + last))
    return lists([final])


def plan_places(source_index, chans, slots):
    n = lax.axis_size("chan")
    channels = jnp.arange(n * chans, dtype=jnp.int32)
    hits = source_index[:, None] == channels[None, :]
    listed = jnp.any(hits, axis=0).reshape(n, chans).astype(jnp.int32)
    below = (jnp.arange(chans)[:, None] < jnp.arange(chans)[None, :]).astype(jnp.int32)
    rank = jnp.sum(listed[:, :, None] * below[None], axis=1)
    device = jnp.arange(n, dtype=jnp.int32)[:, None]
    place = (rank // slots * n + device) * slots + rank % slots
    places = jnp.sum(jnp.where(hits, place.reshape(1, -1), 0), axis=1, keepdims=True)
    return places, jnp.max(jnp.sum(listed, axis=1))


def per_device(traces, source_index):
    chans, wins, length = traces.shape
    n = lax.axis_size("chan")
    sources = source_index.shape[0]
    halo = lax.ppermute(traces[:GAUGE], "chan", [(i + 1, i) for i in range(n - 1)])
    me = lax.axis_index("chan").astype(jnp.int32).reshape(1)
    table, band = jnp.asarray(make_table(length)), jnp.asarray(make_band())
    depth = 2 * wins
    row_width = HALF * 2 * depth // n
    vmem = pl.BlockSpec(memory_space=pltpu.VMEM)
    smem = pl.BlockSpec(memory_space=pltpu.SMEM)
    params = pltpu.CompilerParams(vmem_limit_bytes=VMEM_LIMIT)
    pairs = HALF // n // 2
    slots = chans // pairs
    turned = jax.ShapeDtypeStruct((chans * PITCH + F, LANES), jnp.float32)
    stage = jax.ShapeDtypeStruct((3, (n + 1) * chans, LANES), jnp.float32)
    slot_list = jax.ShapeDtypeStruct((chans + 3,), jnp.int32)
    some, staged, listed = pl.pallas_call(
        functools.partial(whiten_kernel, chans, slots),
        in_specs=[smem] * 2 + [vmem] * 3,
        out_specs=[vmem, vmem, smem],
        out_shape=[turned, stage, slot_list],
        compiler_params=params,
        cost_estimate=pl.CostEstimate(
            flops=2 * (chans - GAUGE) * wins * (length + F // 2) * 2 * F,
            bytes_accessed=8 * 1024 * 1024,
            transcendentals=0,
        ),
        name="whiten",
    )(me, source_index, traces, table, band)
    rows_shape = jax.ShapeDtypeStruct((n, chans, row_width // pairs), jnp.bfloat16)
    spectra, _, *rounds = pl.pallas_call(
        functools.partial(finish_kernel, chans, slots),
        in_specs=[smem] + [vmem] * 6,
        out_specs=[vmem] * (2 + pairs),
        out_shape=[turned, stage] + [rows_shape] * pairs,
        input_output_aliases={5: 0, 6: 1},
        compiler_params=params,
        name="finish",
    )(listed, traces, halo, table, band, some, staged)
    rounds[0], late_index = lax.optimization_barrier((rounds[0], source_index))
    places, most = plan_places(late_index, chans, slots)

    def exchange(number, rows):
        rows = lax.all_to_all(rows, "chan", 0, 0, tiled=True)
        return pl.pallas_call(
            functools.partial(pick_kernel, slots, number * n * slots),
            out_shape=jax.ShapeDtypeStruct((HALF // n, depth, 2 * sources), jnp.bfloat16),
            compiler_params=params,
            name="pick",
        )(places, rows)

    picked = exchange(0, rounds[0])
    for number in range(1, pairs):
        picked = lax.cond(
            most > number * slots,
            lambda p, r, number=number: p + exchange(number, r),
            lambda p, r: p,
            picked,
            rounds[number],
        )
    picked, spectra = lax.optimization_barrier((picked, spectra))
    left = pl.pallas_call(
        functools.partial(left_kernel, chans, depth),
        in_specs=[vmem],
        out_specs=vmem,
        out_shape=jax.ShapeDtypeStruct((HALF, 4 * chans, LANES), jnp.bfloat16),
        compiler_params=params,
        cost_estimate=pl.CostEstimate(
            flops=10 * 1000 * 1000, bytes_accessed=8 * 1024 * 1024, transcendentals=0
        ),
        name="left",
    )(spectra)
    total_windows = wins * lax.axis_size("win")
    held_shape = jax.ShapeDtypeStruct((2 * chans * HALF_PITCH + HALF, LANES), jnp.float32)
    held = []

    def multiply(pieces, origins):
        held[:] = [
            pl.pallas_call(
                functools.partial(partial_kernel, n, origins, len(held)),
                in_specs=[smem, vmem] + [vmem] * (len(held) + len(pieces)),
                out_specs=vmem,
                out_shape=held_shape,
                input_output_aliases={2: 0} if held else {},
                compiler_params=params,
                cost_estimate=pl.CostEstimate(
                    flops=100 * 1000 * 1000, bytes_accessed=4 * 1024 * 1024, transcendentals=0
                ),
                name="products",
            )(me, left, *held, *pieces)
        ]

    def after_products(*arrays):
        *arrays, held[0] = lax.optimization_barrier((*arrays, held[0]))
        return arrays

    pieces, origins = gather_pieces(picked, multiply, after_products)
    stack, _ = pl.pallas_call(
        functools.partial(correlate_kernel, 1.0 / total_windows, n, origins, sources),
        in_specs=[smem, vmem, vmem] + [vmem] * len(pieces),
        out_specs=[pl.BlockSpec(memory_space=pl.ANY), vmem],
        out_shape=[jax.ShapeDtypeStruct((2, sources, chans, F), jnp.float32), held_shape],
        scratch_shapes=[
            pltpu.VMEM((2, 2 * sources * chans, HALF), jnp.float32),
            pltpu.SemaphoreType.DMA((chans // 4, 2)),
        ],
        input_output_aliases={2: 1},
        compiler_params=params,
        name="correlate",
    )(me, left, *held, *pieces)
    if lax.axis_size("win") == 1:
        return stack
    return lax.psum_scatter(stack, "win", scatter_dimension=1, tiled=True)


def solution(mesh):
    return jax.shard_map(
        per_device,
        mesh=mesh,
        in_specs=(P("chan", "win", None), P()),
        out_specs=P(None, "win", "chan", None),
        check_vma=False,
    )
```

```python
import functools
import math

import jax
import jax.numpy as jnp
import ml_dtypes
import numpy as np
from jax import lax
from jax.experimental import pallas as pl
from jax.experimental.pallas import tpu as pltpu
from jax.sharding import PartitionSpec as P

F = 256
HALF = 128
F0 = 1
K = 64
GAUGE = 4
LANES = 128
PITCH = F + 8
HALF_PITCH = HALF + 8
VMEM_LIMIT = 16 * 1024 * 1024


def make_table(length):
    times = np.arange(length, dtype=np.int64)[:, None]
    bins = np.arange(F, dtype=np.int64)[None, :] + F0
    phase = (times * bins % length).astype(np.float32) * np.float32(2.0 * math.pi / length)
    phase = phase.astype(np.float64)
    return np.concatenate([np.cos(phase), -np.sin(phase)], axis=1).astype(ml_dtypes.bfloat16)


def make_band():
    rows = np.arange(F)[:, None]
    cols = np.arange(F)[None, :]
    return (np.abs(rows - cols) <= K).astype(ml_dtypes.bfloat16)


def whiten_block(cur, upper, table_ref, band_ref, turned_ref, first):
    chans, wins, length = cur.shape
    rows = chans * wins
    diff = (upper.astype(jnp.float32) - cur.astype(jnp.float32)).reshape(rows, length)
    power = jnp.sum(diff * diff, axis=1, keepdims=True) * (1.0 / length)
    normed = (diff * lax.rsqrt(power + 1e-05)).astype(jnp.bfloat16)
    spec = jnp.dot(normed, table_ref[...], preferred_element_type=jnp.float32)
    real = spec[:, :F]
    imag = spec[:, F:]
    magnitude = jnp.sqrt(real * real + imag * imag).astype(jnp.bfloat16)
    bins = lax.broadcasted_iota(jnp.int32, (1, F), 1)
    counts = (jnp.minimum(bins, K) + jnp.minimum(F - 1 - bins, K) + 1).astype(jnp.float32)
    smooth = jnp.dot(magnitude, band_ref[...], preferred_element_type=jnp.float32) * (1.0 / counts)
    gain = 1.0 / (smooth + 1e-06)
    white_re = (real * gain).astype(jnp.bfloat16).astype(jnp.float32)
    white_im = (imag * gain).astype(jnp.bfloat16).astype(jnp.float32)
    pad = jnp.zeros((LANES - 2 * wins, F), jnp.float32)
    for c in range(chans):
        mine = slice(c * wins, (c + 1) * wins)
        both = jnp.concatenate([white_re[mine], white_im[mine], pad], axis=0)
        turned_ref[(first + c) * PITCH : (first + c) * PITCH + F, :] = both.T


def list_slots(chans, me_ref, index_ref, slot_ref):
    mine = jnp.int32(0)
    for s in range(index_ref.shape[0]):
        local = index_ref[s] - me_ref[0] * chans
        bit = lax.shift_left(jnp.int32(1), jnp.clip(local, 0, chans - 1))
        mine = mine | jnp.where((local >= 0) & (local < chans), bit, 0)
    early = count = jnp.int32(0)
    for c in range(chans):
        slot_ref[count] = c
        count = count + (lax.shift_right_logical(mine, c) & 1)
        if c < chans - GAUGE:
            early = count
    slot_ref[chans + 1] = early
    slot_ref[chans + 2] = count


def lay_out(slot, channel, turned_ref, stage_ref, height, slots):
    dests = stage_ref.shape[1] // height - 1
    per_dest = HALF // dests
    lane = lax.broadcasted_iota(jnp.int32, (dests, LANES), 1)
    for pair in range(per_dest // 2):
        piece = []
        for j in range(2):
            for half in range(2):
                at = channel * PITCH + half * HALF + pair * 2 + j
                piece.append(turned_ref[pl.ds(at, dests, stride=per_dest), :])
        a, b, c, d = piece
        b = pltpu.roll(b, 96, 1)
        c = pltpu.roll(c, 64, 1)
        d = pltpu.roll(d, 32, 1)
        rows_at = pl.ds(pair * slots + slot, dests, stride=height)
        stage_ref.at[0][rows_at, :] = jnp.where(lane < 96, a, b)
        stage_ref.at[1][rows_at, :] = jnp.where(lane < 64, b, c)
        stage_ref.at[2][rows_at, :] = jnp.where(lane < 32, c, d)


def whiten_kernel(
    height, slots, me_ref, index_ref, traces_ref, table_ref, band_ref, turned_ref, stage_ref, slot_ref
):
    chans = traces_ref.shape[0]
    stage_ref[...] = jnp.zeros_like(stage_ref)
    list_slots(chans, me_ref, index_ref, slot_ref)
    for c in range(0, chans - GAUGE, GAUGE):
        cur, upper = traces_ref[c : c + GAUGE], traces_ref[c + GAUGE : c + 2 * GAUGE]
        whiten_block(cur, upper, table_ref, band_ref, turned_ref, c)

    def one(slot, carry):
        lay_out(slot, slot_ref[slot], turned_ref, stage_ref, height, slots)
        return carry

    lax.fori_loop(0, jnp.minimum(slot_ref[chans + 1], slots), one, 0)


def finish_kernel(
    height, slots, slot_ref, traces_ref, halo_ref, table_ref, band_ref, _, __, turned_ref, stage_ref, *rounds
):
    chans = traces_ref.shape[0]
    early, count = slot_ref[chans + 1], slot_ref[chans + 2]
    cur = traces_ref[chans - GAUGE :]
    whiten_block(cur, halo_ref[...], table_ref, band_ref, turned_ref, chans - GAUGE)

    def fill(first, start, rows_ref):
        def one(slot, carry):
            channel = slot_ref[first + slot]
            lay_out(slot, channel, turned_ref, stage_ref, height, slots)
            return carry

        lax.fori_loop(start, jnp.minimum(count - first, slots), one, 0)
        for dest in range(rows_ref.shape[0]):
            for tile in range(3):
                block = stage_ref[tile, dest * height : (dest + 1) * height, :]
                rows_ref[dest, :, tile * LANES : (tile + 1) * LANES] = block.astype(jnp.bfloat16)

    def clear(rows_ref):
        rows_ref[...] = jnp.zeros_like(rows_ref)

    fill(0, early, rounds[0])
    for number in range(1, len(rounds)):
        more = count > number * slots
        pl.when(more)(functools.partial(fill, number * slots, 0, rounds[number]))
        pl.when(jnp.logical_not(more))(functools.partial(clear, rounds[number]))


def left_kernel(chans, depth, turned_ref, left_ref):
    lane = lax.broadcasted_iota(jnp.int32, (chans, LANES), 1)

    def one(g, carry):
        stack = []
        for half in range(2):
            real = turned_ref[pl.ds(half * HALF + g, chans, stride=PITCH), :]
            ahead = pltpu.roll(real, depth // 2, 1)
            back = pltpu.roll(real, LANES - depth // 2, 1)
            stack += [real, jnp.where(lane < depth // 2, -back, ahead)]
        left_ref[g] = jnp.concatenate(stack, axis=0).astype(jnp.bfloat16)
        return carry

    lax.fori_loop(0, HALF, one, 0, unroll=8)


def pick_kernel(slots, base, place_ref, rows_ref, out_ref):
    sources = place_ref.shape[0]
    dests, height, width = rows_ref.shape
    groups, depth, _ = out_ref.shape
    rows = rows_ref[...].reshape(dests * height, width)
    ids = lax.broadcasted_iota(jnp.int32, (sources, dests * height), 1)
    place = place_ref[...] - base
    inside = (place >= 0) & (place < dests * slots)
    spot = place // slots * height + place % slots
    for pair in range(groups // 2):
        hit = inside & (ids == spot + pair * slots)
        onehot = jnp.where(hit, 1.0, 0.0).astype(jnp.bfloat16)
        turned = jnp.dot(onehot, rows, preferred_element_type=jnp.float32).T
        for j in range(2):
            low = turned[(2 * j) * depth : (2 * j + 1) * depth]
            high = turned[(2 * j + 1) * depth : (2 * j + 2) * depth]
            out_ref[pair * 2 + j] = jnp.concatenate([low, high], axis=1).astype(jnp.bfloat16)


def products(n, origins, me_ref, left_ref, pieces, held):
    rows = left_ref.shape[1]
    depth, width = pieces[0].shape[-2:]
    groups = HALF // n
    sources = width // 2
    outs = rows // 2
    me = me_ref[0]
    lane = lax.broadcasted_iota(jnp.int32, (outs, width), 1)
    for piece, names in zip(pieces, origins):
        for place, (flip, index) in enumerate(names):
            g = (me ^ flip) * groups + index
            both = jnp.dot(left_ref[g][:, :depth], piece[place], preferred_element_type=jnp.float32)
            mine = jnp.where(lane < sources, both[:outs], both[outs:])
            held[pl.ds(g, outs, stride=HALF_PITCH), :] = mine


def partial_kernel(n, origins, chained, me_ref, left_ref, *refs):
    products(n, origins, me_ref, left_ref, refs[chained:-1], refs[-1])


def correlate_kernel(scale, n, origins, sources, me_ref, left_ref, _, *refs):
    pieces, (out_ref, held, turned_ref, sems) = refs[:-4], refs[-4:]
    products(n, origins, me_ref, left_ref, pieces, held)
    outs = held.shape[0] // HALF_PITCH
    chans = outs // 2
    group = 8
    copies = []
    for part in range(2):
        for c in range(chans):
            base = (part * chans + c) * HALF_PITCH
            turned = held[base : base + HALF, :].T * scale
            rows_at = pl.ds(part * sources * chans + c, sources, stride=chans)
            for half in range(2):
                turned_ref.at[half][rows_at, :] = turned[half * sources : (half + 1) * sources]
            if c % group == group - 1:
                span = pl.ds(c + 1 - group, group)
                for half in range(2):
                    block = turned_ref.at[half].reshape(2, sources, chans, HALF)
                    copy = pltpu.make_async_copy(
                        block.at[part, :, span, :],
                        out_ref.at[part, :, span, pl.ds(half * HALF, HALF)],
                        sems.at[part * (chans // group) + c // group, half],
                    )
                    copy.start()
                    copies.append(copy)
    for copy in copies:
        copy.wait()


def gather_pieces(own, multiply, after_products):
    n = lax.axis_size("chan")
    groups = own.shape[0]
    core, x, y, z, zz = 1, 2, 4, 8, 16
    place = {}

    def keep(array, names):
        for i, name in enumerate(names):
            place[name] = (array, i)
        return array, names

    def pack(names):
        parts = []
        for name in names:
            array, i = place[name]
            if parts and parts[-1][0] is array and parts[-1][2] == i:
                parts[-1][2] = i + 1
            else:
                parts.append([array, i, i + 1])
        blocks = [array[i:j] for array, i, j in parts]
        return blocks[0] if len(blocks) == 1 else jnp.concatenate(blocks, axis=0)

    def send(names, flip):
        route = [(i, i ^ flip) for i in range(n)]
        return lax.ppermute(pack(names), "chan", route), [(f ^ flip, g) for f, g in names]

    def lists(pairs):
        return [array for array, _ in pairs], [names for _, names in pairs]

    def piece(flip):
        return [(flip, g) for g in range(groups)]

    near = [keep(own, piece(0))]
    if n != 32:
        flip = 1
        while flip < n:
            near.append(keep(*send(sorted(place), flip)))
            flip *= 2
        multiply(*lists(near[:-1]))
        return lists(near[-1:])

    first = [send(piece(0), flip) for flip in (x ^ y, y, x, z, zz)]
    arrays = lax.optimization_barrier(lists(first)[0])
    near += [keep(array, names) for array, (_, names) in zip(arrays, first)]
    mid = [
        send(piece(z) + piece(zz), x),
        send(piece(z) + piece(zz), y),
        send(piece(x ^ y), zz),
        send(piece(zz) + piece(x ^ y), z),
    ]
    multiply(*lists(near))
    arrays = after_products(*lists(mid)[0])
    mid = [keep(array, names) for array, (_, names) in zip(arrays, mid)]
    last = [
        send(piece(z ^ zz), x),
        send(piece(z ^ zz), y),
        send(piece(zz ^ x ^ y), z),
    ]
    theirs = send([name for pair in near + mid for name in pair[1]], core)
    multiply(*lists(mid))
    arrays = after_products(*lists(last)[0])
    last = [keep(array, names) for array, (_, names) in zip(arrays, last)]
    assert sorted(place) == [(f, g) for f in range(0, n, 2) for g in range(groups)]
    final = send([name for pair in last for name in pair[1]], core)
    multiply(*lists([theirs] + last))
    return lists([final])


def plan_places(source_index, chans, slots):
    n = lax.axis_size("chan")
    channels = jnp.arange(n * chans, dtype=jnp.int32)
    hits = source_index[:, None] == channels[None, :]
    listed = jnp.any(hits, axis=0).reshape(n, chans).astype(jnp.int32)
    below = (jnp.arange(chans)[:, None] < jnp.arange(chans)[None, :]).astype(jnp.int32)
    rank = jnp.sum(listed[:, :, None] * below[None], axis=1)
    device = jnp.arange(n, dtype=jnp.int32)[:, None]
    place = (rank // slots * n + device) * slots + rank % slots
    places = jnp.sum(jnp.where(hits, place.reshape(1, -1), 0), axis=1, keepdims=True)
    return places, jnp.max(jnp.sum(listed, axis=1))


def per_device(traces, source_index):
    chans, wins, length = traces.shape
    n = lax.axis_size("chan")
    sources = source_index.shape[0]
    halo = lax.ppermute(traces[:GAUGE], "chan", [(i + 1, i) for i in range(n - 1)])
    me = lax.axis_index("chan").astype(jnp.int32).reshape(1)
    table, band = jnp.asarray(make_table(length)), jnp.asarray(make_band())
    depth = 2 * wins
    row_width = HALF * 2 * depth // n
    vmem = pl.BlockSpec(memory_space=pltpu.VMEM)
    smem = pl.BlockSpec(memory_space=pltpu.SMEM)
    params = pltpu.CompilerParams(vmem_limit_bytes=VMEM_LIMIT)
    pairs = HALF // n // 2
    slots = chans // pairs
    turned = jax.ShapeDtypeStruct((chans * PITCH + F, LANES), jnp.float32)
    stage = jax.ShapeDtypeStruct((3, (n + 1) * chans, LANES), jnp.float32)
    slot_list = jax.ShapeDtypeStruct((chans + 3,), jnp.int32)
    some, staged, listed = pl.pallas_call(
        functools.partial(whiten_kernel, chans, slots),
        in_specs=[smem] * 2 + [vmem] * 3,
        out_specs=[vmem, vmem, smem],
        out_shape=[turned, stage, slot_list],
        compiler_params=params,
        cost_estimate=pl.CostEstimate(
            flops=2 * (chans - GAUGE) * wins * (length + F // 2) * 2 * F,
            bytes_accessed=8 * 1024 * 1024,
            transcendentals=0,
        ),
        name="whiten",
    )(me, source_index, traces, table, band)
    rows_shape = jax.ShapeDtypeStruct((n, chans, row_width // pairs), jnp.bfloat16)
    spectra, _, *rounds = pl.pallas_call(
        functools.partial(finish_kernel, chans, slots),
        in_specs=[smem] + [vmem] * 6,
        out_specs=[vmem] * (2 + pairs),
        out_shape=[turned, stage] + [rows_shape] * pairs,
        input_output_aliases={5: 0, 6: 1},
        compiler_params=params,
        name="finish",
    )(listed, traces, halo, table, band, some, staged)
    rounds[0], late_index = lax.optimization_barrier((rounds[0], source_index))
    places, most = plan_places(late_index, chans, slots)

    def exchange(number, rows):
        rows = lax.all_to_all(rows, "chan", 0, 0, tiled=True)
        return pl.pallas_call(
            functools.partial(pick_kernel, slots, number * n * slots),
            out_shape=jax.ShapeDtypeStruct((HALF // n, depth, 2 * sources), jnp.bfloat16),
            compiler_params=params,
            name="pick",
        )(places, rows)

    picked = exchange(0, rounds[0])
    for number in range(1, pairs):
        picked = lax.cond(
            most > number * slots,
            lambda p, r, number=number: p + exchange(number, r),
            lambda p, r: p,
            picked,
            rounds[number],
        )
    picked, spectra = lax.optimization_barrier((picked, spectra))
    left = pl.pallas_call(
        functools.partial(left_kernel, chans, depth),
        in_specs=[vmem],
        out_specs=vmem,
        out_shape=jax.ShapeDtypeStruct((HALF, 4 * chans, LANES), jnp.bfloat16),
        compiler_params=params,
        cost_estimate=pl.CostEstimate(
            flops=10 * 1000 * 1000, bytes_accessed=8 * 1024 * 1024, transcendentals=0
        ),
        name="left",
    )(spectra)
    total_windows = wins * lax.axis_size("win")
    held_shape = jax.ShapeDtypeStruct((2 * chans * HALF_PITCH + HALF, LANES), jnp.float32)
    held = []

    def multiply(pieces, origins):
        held[:] = [
            pl.pallas_call(
                functools.partial(partial_kernel, n, origins, len(held)),
                in_specs=[smem, vmem] + [vmem] * (len(held) + len(pieces)),
                out_specs=vmem,
                out_shape=held_shape,
                input_output_aliases={2: 0} if held else {},
                compiler_params=params,
                cost_estimate=pl.CostEstimate(
                    flops=100 * 1000 * 1000, bytes_accessed=4 * 1024 * 1024, transcendentals=0
                ),
                name="products",
            )(me, left, *held, *pieces)
        ]

    def after_products(*arrays):
        *arrays, held[0] = lax.optimization_barrier((*arrays, held[0]))
        return arrays

    pieces, origins = gather_pieces(picked, multiply, after_products)
    stack, _ = pl.pallas_call(
        functools.partial(correlate_kernel, 1.0 / total_windows, n, origins, sources),
        in_specs=[smem, vmem, vmem] + [vmem] * len(pieces),
        out_specs=[pl.BlockSpec(memory_space=pl.ANY), vmem],
        out_shape=[jax.ShapeDtypeStruct((2, sources, chans, F), jnp.float32), held_shape],
        scratch_shapes=[
            pltpu.VMEM((2, 2 * sources * chans, HALF), jnp.float32),
            pltpu.SemaphoreType.DMA((chans // 4, 2)),
        ],
        input_output_aliases={2: 1},
        compiler_params=params,
        name="correlate",
    )(me, left, *held, *pieces)
    if lax.axis_size("win") == 1:
        return stack
    return lax.psum_scatter(stack, "win", scatter_dimension=1, tiled=True)


def solution(mesh):
    return jax.shard_map(
        per_device,
        mesh=mesh,
        in_specs=(P("chan", "win", None), P()),
        out_specs=P(None, "win", "chan", None),
        check_vma=False,
    )
```

```python
import functools
import math

import jax
import jax.numpy as jnp
import ml_dtypes
import numpy as np
from jax import lax
from jax.experimental import pallas as pl
from jax.experimental.pallas import tpu as pltpu
from jax.sharding import PartitionSpec as P

F = 256
HALF = 128
F0 = 1
K = 64
GAUGE = 4
LANES = 128
PITCH = F + 8
HALF_PITCH = HALF + 8
VMEM_LIMIT = 24 * 1024 * 1024


def make_table(length):
    times = np.arange(length, dtype=np.int64)[:, None]
    bins = np.arange(F, dtype=np.int64)[None, :] + F0
    phase = (times * bins % length).astype(np.float32) * np.float32(2.0 * math.pi / length)
    phase = phase.astype(np.float64)
    return np.concatenate([np.cos(phase), -np.sin(phase)], axis=1).astype(ml_dtypes.bfloat16)


def make_band():
    rows = np.arange(F)[:, None]
    cols = np.arange(F)[None, :]
    return (np.abs(rows - cols) <= K).astype(ml_dtypes.bfloat16)


def whiten_block(cur, upper, table_ref, band_ref, turned_ref, first):
    chans, wins, length = cur.shape
    rows = chans * wins
    diff = (upper.astype(jnp.float32) - cur.astype(jnp.float32)).reshape(rows, length)
    power = jnp.sum(diff * diff, axis=1, keepdims=True) * (1.0 / length)
    normed = (diff * lax.rsqrt(power + 1e-05)).astype(jnp.bfloat16)
    spec = jnp.dot(normed, table_ref[...], preferred_element_type=jnp.float32)
    real = spec[:, :F]
    imag = spec[:, F:]
    magnitude = jnp.sqrt(real * real + imag * imag).astype(jnp.bfloat16)
    bins = lax.broadcasted_iota(jnp.int32, (1, F), 1)
    counts = (jnp.minimum(bins, K) + jnp.minimum(F - 1 - bins, K) + 1).astype(jnp.float32)
    smooth = jnp.dot(magnitude, band_ref[...], preferred_element_type=jnp.float32) / counts
    gain = 1.0 / (smooth + 1e-06)
    white_re = (real * gain).astype(jnp.bfloat16).astype(jnp.float32)
    white_im = (imag * gain).astype(jnp.bfloat16).astype(jnp.float32)
    pad = jnp.zeros((LANES - 2 * wins, F), jnp.float32)
    for c in range(chans):
        mine = slice(c * wins, (c + 1) * wins)
        both = jnp.concatenate([white_re[mine], white_im[mine], pad], axis=0)
        turned_ref[(first + c) * PITCH : (first + c) * PITCH + F, :] = both.T


def list_slots(chans, me_ref, index_ref, slot_ref):
    mine = jnp.int32(0)
    for s in range(index_ref.shape[0]):
        local = index_ref[s] - me_ref[0] * chans
        bit = lax.shift_left(jnp.int32(1), jnp.clip(local, 0, chans - 1))
        mine = mine | jnp.where((local >= 0) & (local < chans), bit, 0)
    early = count = jnp.int32(0)
    for c in range(chans):
        slot_ref[count] = c
        count = count + (lax.shift_right_logical(mine, c) & 1)
        if c < chans - GAUGE:
            early = count
    slot_ref[chans + 1] = early
    slot_ref[chans + 2] = count


def lay_out(slot, channel, turned_ref, stage_ref, height, slots):
    dests = stage_ref.shape[1] // height
    per_dest = HALF // dests
    lane = lax.broadcasted_iota(jnp.int32, (dests, LANES), 1)
    for pair in range(per_dest // 2):
        piece = []
        for j in range(2):
            for half in range(2):
                at = channel * PITCH + half * HALF + pair * 2 + j
                piece.append(turned_ref[pl.ds(at, dests, stride=per_dest), :])
        a, b, c, d = piece
        b = pltpu.roll(b, 96, 1)
        c = pltpu.roll(c, 64, 1)
        d = pltpu.roll(d, 32, 1)
        rows_at = pl.ds(pair * slots + slot, dests, stride=height)
        stage_ref.at[0][rows_at, :] = jnp.where(lane < 96, a, b)
        stage_ref.at[1][rows_at, :] = jnp.where(lane < 64, b, c)
        stage_ref.at[2][rows_at, :] = jnp.where(lane < 32, c, d)


def whiten_kernel(
    height, slots, me_ref, index_ref, traces_ref, table_ref, band_ref, turned_ref, stage_ref, slot_ref
):
    chans = traces_ref.shape[0]
    stage_ref[...] = jnp.zeros_like(stage_ref)
    list_slots(chans, me_ref, index_ref, slot_ref)
    for c in range(0, chans - GAUGE, GAUGE):
        cur, upper = traces_ref[c : c + GAUGE], traces_ref[c + GAUGE : c + 2 * GAUGE]
        whiten_block(cur, upper, table_ref, band_ref, turned_ref, c)

    def one(slot, carry):
        lay_out(slot, slot_ref[slot], turned_ref, stage_ref, height, slots)
        return carry

    lax.fori_loop(0, jnp.minimum(slot_ref[chans + 1], slots), one, 0)


def finish_kernel(
    height, slots, slot_ref, traces_ref, halo_ref, table_ref, band_ref, _, __, turned_ref, stage_ref, *rounds
):
    chans = traces_ref.shape[0]
    early, count = slot_ref[chans + 1], slot_ref[chans + 2]
    cur = traces_ref[chans - GAUGE :]
    whiten_block(cur, halo_ref[...], table_ref, band_ref, turned_ref, chans - GAUGE)

    def fill(first, start, rows_ref):
        def one(slot, carry):
            channel = slot_ref[first + slot]
            lay_out(slot, channel, turned_ref, stage_ref, height, slots)
            return carry

        lax.fori_loop(start, jnp.minimum(count - first, slots), one, 0)
        for dest in range(rows_ref.shape[0]):
            for tile in range(3):
                block = stage_ref[tile, dest * height : (dest + 1) * height, :]
                rows_ref[dest, :, tile * LANES : (tile + 1) * LANES] = block.astype(jnp.bfloat16)

    def clear(rows_ref):
        rows_ref[...] = jnp.zeros_like(rows_ref)

    fill(0, early, rounds[0])
    for number in range(1, len(rounds)):
        more = count > number * slots
        pl.when(more)(functools.partial(fill, number * slots, 0, rounds[number]))
        pl.when(jnp.logical_not(more))(functools.partial(clear, rounds[number]))


def left_kernel(chans, depth, turned_ref, left_ref):
    lane = lax.broadcasted_iota(jnp.int32, (chans, LANES), 1)

    def one(g, carry):
        stack = []
        for half in range(2):
            real = turned_ref[pl.ds(half * HALF + g, chans, stride=PITCH), :]
            ahead = pltpu.roll(real, depth // 2, 1)
            back = pltpu.roll(real, LANES - depth // 2, 1)
            stack += [real, jnp.where(lane < depth // 2, -back, ahead)]
        left_ref[g] = jnp.concatenate(stack, axis=0).astype(jnp.bfloat16)
        return carry

    lax.fori_loop(0, HALF, one, 0, unroll=8)


def pick_kernel(slots, base, place_ref, rows_ref, out_ref):
    sources = place_ref.shape[0]
    dests, height, width = rows_ref.shape
    groups, depth, _ = out_ref.shape
    rows = rows_ref[...].reshape(dests * height, width)
    ids = lax.broadcasted_iota(jnp.int32, (sources, dests * height), 1)
    place = place_ref[...] - base
    inside = (place >= 0) & (place < dests * slots)
    spot = place // slots * height + place % slots
    for pair in range(groups // 2):
        hit = inside & (ids == spot + pair * slots)
        onehot = jnp.where(hit, 1.0, 0.0).astype(jnp.bfloat16)
        turned = jnp.dot(onehot, rows, preferred_element_type=jnp.float32).T
        for j in range(2):
            low = turned[(2 * j) * depth : (2 * j + 1) * depth]
            high = turned[(2 * j + 1) * depth : (2 * j + 2) * depth]
            out_ref[pair * 2 + j] = jnp.concatenate([low, high], axis=1).astype(jnp.bfloat16)


def products(n, origins, me_ref, left_ref, pieces, held):
    rows = left_ref.shape[1]
    depth, width = pieces[0].shape[-2:]
    groups = HALF // n
    sources = width // 2
    outs = rows // 2
    me = me_ref[0]
    lane = lax.broadcasted_iota(jnp.int32, (outs, width), 1)
    for piece, names in zip(pieces, origins):
        for place, (flip, index) in enumerate(names):
            g = (me ^ flip) * groups + index
            both = jnp.dot(left_ref[g][:, :depth], piece[place], preferred_element_type=jnp.float32)
            mine = jnp.where(lane < sources, both[:outs], both[outs:])
            held[pl.ds(g, outs, stride=HALF_PITCH), :] = mine


def partial_kernel(n, origins, chained, me_ref, left_ref, *refs):
    products(n, origins, me_ref, left_ref, refs[chained:-1], refs[-1])


def correlate_kernel(scale, n, origins, sources, me_ref, left_ref, _, *refs):
    pieces, (out_ref, held, turned_ref, sems) = refs[:-4], refs[-4:]
    products(n, origins, me_ref, left_ref, pieces, held)
    outs = held.shape[0] // HALF_PITCH
    chans = outs // 2
    group = 8
    copies = []
    for part in range(2):
        for c in range(chans):
            base = (part * chans + c) * HALF_PITCH
            turned = held[base : base + HALF, :].T * scale
            rows_at = pl.ds(part * sources * chans + c, sources, stride=chans)
            for half in range(2):
                turned_ref.at[half][rows_at, :] = turned[half * sources : (half + 1) * sources]
            if c % group == group - 1:
                span = pl.ds(c + 1 - group, group)
                for half in range(2):
                    block = turned_ref.at[half].reshape(2, sources, chans, HALF)
                    copy = pltpu.make_async_copy(
                        block.at[part, :, span, :],
                        out_ref.at[part, :, span, pl.ds(half * HALF, HALF)],
                        sems.at[part * (chans // group) + c // group, half],
                    )
                    copy.start()
                    copies.append(copy)
    for copy in copies:
        copy.wait()


def gather_pieces(own, multiply, after_products):
    n = lax.axis_size("chan")
    groups = own.shape[0]
    core, x, y, z, zz = 1, 2, 4, 8, 16
    place = {}

    def keep(array, names):
        for i, name in enumerate(names):
            place[name] = (array, i)
        return array, names

    def pack(names):
        parts = []
        for name in names:
            array, i = place[name]
            if parts and parts[-1][0] is array and parts[-1][2] == i:
                parts[-1][2] = i + 1
            else:
                parts.append([array, i, i + 1])
        blocks = [array[i:j] for array, i, j in parts]
        return blocks[0] if len(blocks) == 1 else jnp.concatenate(blocks, axis=0)

    def send(names, flip):
        route = [(i, i ^ flip) for i in range(n)]
        return lax.ppermute(pack(names), "chan", route), [(f ^ flip, g) for f, g in names]

    def lists(pairs):
        return [array for array, _ in pairs], [names for _, names in pairs]

    def piece(flip):
        return [(flip, g) for g in range(groups)]

    near = [keep(own, piece(0))]
    if n != 32:
        flip = 1
        while flip < n:
            near.append(keep(*send(sorted(place), flip)))
            flip *= 2
        multiply(*lists(near[:-1]))
        return lists(near[-1:])

    first = [send(piece(0), flip) for flip in (y, x, x ^ y, z, zz)]
    arrays = lax.optimization_barrier(lists(first)[0])
    near += [keep(array, names) for array, (_, names) in zip(arrays, first)]
    mid = [
        send(piece(z) + piece(zz), x),
        send(piece(z) + piece(zz), y),
        send(piece(x ^ y), zz),
        send(piece(zz) + piece(x ^ y), z),
    ]
    multiply(*lists(near))
    arrays = after_products(*lists(mid)[0])
    mid = [keep(array, names) for array, (_, names) in zip(arrays, mid)]
    last = [
        send(piece(z ^ zz), x),
        send(piece(z ^ zz), y),
        send(piece(zz ^ x ^ y), z),
    ]
    theirs = send([name for pair in near + mid for name in pair[1]], core)
    multiply(*lists(mid))
    arrays = after_products(*lists(last)[0])
    last = [keep(array, names) for array, (_, names) in zip(arrays, last)]
    assert sorted(place) == [(f, g) for f in range(0, n, 2) for g in range(groups)]
    final = send([name for pair in last for name in pair[1]], core)
    multiply(*lists([theirs] + last))
    return lists([final])


def plan_places(source_index, chans, slots):
    n = lax.axis_size("chan")
    channels = jnp.arange(n * chans, dtype=jnp.int32)
    hits = source_index[:, None] == channels[None, :]
    listed = jnp.any(hits, axis=0).reshape(n, chans).astype(jnp.int32)
    below = (jnp.arange(chans)[:, None] < jnp.arange(chans)[None, :]).astype(jnp.int32)
    rank = jnp.sum(listed[:, :, None] * below[None], axis=1)
    device = jnp.arange(n, dtype=jnp.int32)[:, None]
    place = (rank // slots * n + device) * slots + rank % slots
    places = jnp.sum(jnp.where(hits, place.reshape(1, -1), 0), axis=1, keepdims=True)
    return places, jnp.max(jnp.sum(listed, axis=1))


def per_device(traces, source_index):
    chans, wins, length = traces.shape
    n = lax.axis_size("chan")
    sources = source_index.shape[0]
    halo = lax.ppermute(traces[:GAUGE], "chan", [(i + 1, i) for i in range(n - 1)])
    me = lax.axis_index("chan").astype(jnp.int32).reshape(1)
    table, band = jnp.asarray(make_table(length)), jnp.asarray(make_band())
    depth = 2 * wins
    row_width = HALF * 2 * depth // n
    vmem = pl.BlockSpec(memory_space=pltpu.VMEM)
    smem = pl.BlockSpec(memory_space=pltpu.SMEM)
    params = pltpu.CompilerParams(vmem_limit_bytes=VMEM_LIMIT)
    pairs = HALF // n // 2
    slots = chans // pairs
    turned = jax.ShapeDtypeStruct((chans * PITCH, LANES), jnp.float32)
    stage = jax.ShapeDtypeStruct((3, n * chans, LANES), jnp.float32)
    slot_list = jax.ShapeDtypeStruct((chans + 3,), jnp.int32)
    some, staged, listed = pl.pallas_call(
        functools.partial(whiten_kernel, chans, slots),
        in_specs=[smem] * 2 + [vmem] * 3,
        out_specs=[vmem, vmem, smem],
        out_shape=[turned, stage, slot_list],
        compiler_params=params,
        cost_estimate=pl.CostEstimate(
            flops=2 * (chans - GAUGE) * wins * (length + F // 2) * 2 * F,
            bytes_accessed=8 * 1024 * 1024,
            transcendentals=0,
        ),
        name="whiten",
    )(me, source_index, traces, table, band)
    rows_shape = jax.ShapeDtypeStruct((n, chans, row_width // pairs), jnp.bfloat16)
    spectra, _, *rounds = pl.pallas_call(
        functools.partial(finish_kernel, chans, slots),
        in_specs=[smem] + [vmem] * 6,
        out_specs=[vmem] * (2 + pairs),
        out_shape=[turned, stage] + [rows_shape] * pairs,
        input_output_aliases={5: 0, 6: 1},
        compiler_params=params,
        name="finish",
    )(listed, traces, halo, table, band, some, staged)
    rounds[0], late_index = lax.optimization_barrier((rounds[0], source_index))
    places, most = plan_places(late_index, chans, slots)

    def exchange(number, rows):
        rows = lax.all_to_all(rows, "chan", 0, 0, tiled=True)
        return pl.pallas_call(
            functools.partial(pick_kernel, slots, number * n * slots),
            out_shape=jax.ShapeDtypeStruct((HALF // n, depth, 2 * sources), jnp.bfloat16),
            compiler_params=params,
            name="pick",
        )(places, rows)

    picked = exchange(0, rounds[0])
    for number in range(1, pairs):
        picked = lax.cond(
            most > number * slots,
            lambda p, r, number=number: p + exchange(number, r),
            lambda p, r: p,
            picked,
            rounds[number],
        )
    picked, spectra = lax.optimization_barrier((picked, spectra))
    left = pl.pallas_call(
        functools.partial(left_kernel, chans, depth),
        in_specs=[vmem],
        out_specs=vmem,
        out_shape=jax.ShapeDtypeStruct((HALF, 4 * chans, LANES), jnp.bfloat16),
        compiler_params=params,
        cost_estimate=pl.CostEstimate(
            flops=10 * 1000 * 1000, bytes_accessed=8 * 1024 * 1024, transcendentals=0
        ),
        name="left",
    )(spectra)
    total_windows = wins * lax.axis_size("win")
    held_shape = jax.ShapeDtypeStruct((2 * chans * HALF_PITCH, LANES), jnp.float32)
    held = []

    def multiply(pieces, origins):
        held[:] = [
            pl.pallas_call(
                functools.partial(partial_kernel, n, origins, len(held)),
                in_specs=[smem, vmem] + [vmem] * (len(held) + len(pieces)),
                out_specs=vmem,
                out_shape=held_shape,
                input_output_aliases={2: 0} if held else {},
                compiler_params=params,
                cost_estimate=pl.CostEstimate(
                    flops=100 * 1000 * 1000, bytes_accessed=4 * 1024 * 1024, transcendentals=0
                ),
                name="products",
            )(me, left, *held, *pieces)
        ]

    def after_products(*arrays):
        *arrays, held[0] = lax.optimization_barrier((*arrays, held[0]))
        return arrays

    pieces, origins = gather_pieces(picked, multiply, after_products)
    stack, _ = pl.pallas_call(
        functools.partial(correlate_kernel, 1.0 / total_windows, n, origins, sources),
        in_specs=[smem, vmem, vmem] + [vmem] * len(pieces),
        out_specs=[pl.BlockSpec(memory_space=pl.ANY), vmem],
        out_shape=[jax.ShapeDtypeStruct((2, sources, chans, F), jnp.float32), held_shape],
        scratch_shapes=[
            pltpu.VMEM((2, 2 * sources * chans, HALF), jnp.float32),
            pltpu.SemaphoreType.DMA((chans // 4, 2)),
        ],
        input_output_aliases={2: 1},
        compiler_params=params,
        name="correlate",
    )(me, left, *held, *pieces)
    if lax.axis_size("win") == 1:
        return stack
    return lax.psum_scatter(stack, "win", scatter_dimension=1, tiled=True)


def solution(mesh):
    return jax.shard_map(
        per_device,
        mesh=mesh,
        in_specs=(P("chan", "win", None), P()),
        out_specs=P(None, "win", "chan", None),
        check_vma=False,
    )
```

```python
import functools
import math

import jax
import jax.numpy as jnp
import ml_dtypes
import numpy as np
from jax import lax
from jax.experimental import pallas as pl
from jax.experimental.pallas import tpu as pltpu
from jax.sharding import PartitionSpec as P

F = 256
HALF = 128
F0 = 1
K = 64
GAUGE = 4
LANES = 128
PITCH = F + 8
HALF_PITCH = HALF + 8
VMEM_LIMIT = 24 * 1024 * 1024


def make_table(length):
    times = np.arange(length, dtype=np.int64)[:, None]
    bins = np.arange(F, dtype=np.int64)[None, :] + F0
    phase = (times * bins % length).astype(np.float32) * np.float32(2.0 * math.pi / length)
    phase = phase.astype(np.float64)
    return np.concatenate([np.cos(phase), -np.sin(phase)], axis=1).astype(ml_dtypes.bfloat16)


def make_band():
    rows = np.arange(F)[:, None]
    cols = np.arange(F)[None, :]
    return (np.abs(rows - cols) <= K).astype(ml_dtypes.bfloat16)


def whiten_block(cur, upper, table_ref, band_ref, turned_ref, first):
    chans, wins, length = cur.shape
    rows = chans * wins
    diff = (upper.astype(jnp.float32) - cur.astype(jnp.float32)).reshape(rows, length)
    power = jnp.sum(diff * diff, axis=1, keepdims=True) * (1.0 / length)
    normed = (diff * lax.rsqrt(power + 1e-05)).astype(jnp.bfloat16)
    spec = jnp.dot(normed, table_ref[...], preferred_element_type=jnp.float32)
    real = spec[:, :F]
    imag = spec[:, F:]
    magnitude = jnp.sqrt(real * real + imag * imag).astype(jnp.bfloat16)
    bins = lax.broadcasted_iota(jnp.int32, (1, F), 1)
    counts = (jnp.minimum(bins, K) + jnp.minimum(F - 1 - bins, K) + 1).astype(jnp.float32)
    smooth = jnp.dot(magnitude, band_ref[...], preferred_element_type=jnp.float32) / counts
    gain = 1.0 / (smooth + 1e-06)
    white_re = (real * gain).astype(jnp.bfloat16).astype(jnp.float32)
    white_im = (imag * gain).astype(jnp.bfloat16).astype(jnp.float32)
    pad = jnp.zeros((LANES - 2 * wins, F), jnp.float32)
    for c in range(chans):
        mine = slice(c * wins, (c + 1) * wins)
        both = jnp.concatenate([white_re[mine], white_im[mine], pad], axis=0)
        turned_ref[(first + c) * PITCH : (first + c) * PITCH + F, :] = both.T


def list_slots(chans, me_ref, index_ref, slot_ref):
    mine = jnp.int32(0)
    for s in range(index_ref.shape[0]):
        local = index_ref[s] - me_ref[0] * chans
        bit = lax.shift_left(jnp.int32(1), jnp.clip(local, 0, chans - 1))
        mine = mine | jnp.where((local >= 0) & (local < chans), bit, 0)
    early = count = jnp.int32(0)
    for c in range(chans):
        slot_ref[count] = c
        count = count + (lax.shift_right_logical(mine, c) & 1)
        if c < chans - GAUGE:
            early = count
    slot_ref[chans + 1] = early
    slot_ref[chans + 2] = count


def lay_out(slot, channel, turned_ref, stage_ref, height, slots):
    dests = stage_ref.shape[1] // height
    per_dest = HALF // dests
    lane = lax.broadcasted_iota(jnp.int32, (dests, LANES), 1)
    for pair in range(per_dest // 2):
        piece = []
        for j in range(2):
            for half in range(2):
                at = channel * PITCH + half * HALF + pair * 2 + j
                piece.append(turned_ref[pl.ds(at, dests, stride=per_dest), :])
        a, b, c, d = piece
        b = pltpu.roll(b, 96, 1)
        c = pltpu.roll(c, 64, 1)
        d = pltpu.roll(d, 32, 1)
        rows_at = pl.ds(pair * slots + slot, dests, stride=height)
        stage_ref.at[0][rows_at, :] = jnp.where(lane < 96, a, b)
        stage_ref.at[1][rows_at, :] = jnp.where(lane < 64, b, c)
        stage_ref.at[2][rows_at, :] = jnp.where(lane < 32, c, d)


def whiten_kernel(
    height, slots, me_ref, index_ref, traces_ref, table_ref, band_ref, turned_ref, stage_ref, slot_ref
):
    chans = traces_ref.shape[0]
    stage_ref[...] = jnp.zeros_like(stage_ref)
    list_slots(chans, me_ref, index_ref, slot_ref)
    for c in range(0, chans - GAUGE, GAUGE):
        cur, upper = traces_ref[c : c + GAUGE], traces_ref[c + GAUGE : c + 2 * GAUGE]
        whiten_block(cur, upper, table_ref, band_ref, turned_ref, c)

    def one(slot, carry):
        lay_out(slot, slot_ref[slot], turned_ref, stage_ref, height, slots)
        return carry

    lax.fori_loop(0, jnp.minimum(slot_ref[chans + 1], slots), one, 0)


def finish_kernel(
    height, slots, slot_ref, traces_ref, halo_ref, table_ref, band_ref, _, __, turned_ref, stage_ref, *rounds
):
    chans = traces_ref.shape[0]
    early, count = slot_ref[chans + 1], slot_ref[chans + 2]
    cur = traces_ref[chans - GAUGE :]
    whiten_block(cur, halo_ref[...], table_ref, band_ref, turned_ref, chans - GAUGE)

    def fill(first, start, rows_ref):
        def one(slot, carry):
            channel = slot_ref[first + slot]
            lay_out(slot, channel, turned_ref, stage_ref, height, slots)
            return carry

        lax.fori_loop(start, jnp.minimum(count - first, slots), one, 0)
        for dest in range(rows_ref.shape[0]):
            for tile in range(3):
                block = stage_ref[tile, dest * height : (dest + 1) * height, :]
                rows_ref[dest, :, tile * LANES : (tile + 1) * LANES] = block.astype(jnp.bfloat16)

    def clear(rows_ref):
        rows_ref[...] = jnp.zeros_like(rows_ref)

    fill(0, early, rounds[0])
    for number in range(1, len(rounds)):
        more = count > number * slots
        pl.when(more)(functools.partial(fill, number * slots, 0, rounds[number]))
        pl.when(jnp.logical_not(more))(functools.partial(clear, rounds[number]))


def left_kernel(chans, depth, turned_ref, left_ref):
    lane = lax.broadcasted_iota(jnp.int32, (chans, LANES), 1)

    def one(g, carry):
        stack = []
        for half in range(2):
            real = turned_ref[pl.ds(half * HALF + g, chans, stride=PITCH), :]
            ahead = pltpu.roll(real, depth // 2, 1)
            back = pltpu.roll(real, LANES - depth // 2, 1)
            stack += [real, jnp.where(lane < depth // 2, -back, ahead)]
        left_ref[g] = jnp.concatenate(stack, axis=0).astype(jnp.bfloat16)
        return carry

    lax.fori_loop(0, HALF, one, 0, unroll=8)


def pick_kernel(slots, base, place_ref, rows_ref, out_ref):
    sources = place_ref.shape[0]
    dests, height, width = rows_ref.shape
    groups, depth, _ = out_ref.shape
    rows = rows_ref[...].reshape(dests * height, width)
    ids = lax.broadcasted_iota(jnp.int32, (sources, dests * height), 1)
    place = place_ref[...] - base
    inside = (place >= 0) & (place < dests * slots)
    spot = place // slots * height + place % slots
    for pair in range(groups // 2):
        hit = inside & (ids == spot + pair * slots)
        onehot = jnp.where(hit, 1.0, 0.0).astype(jnp.bfloat16)
        turned = jnp.dot(onehot, rows, preferred_element_type=jnp.float32).T
        for j in range(2):
            low = turned[(2 * j) * depth : (2 * j + 1) * depth]
            high = turned[(2 * j + 1) * depth : (2 * j + 2) * depth]
            out_ref[pair * 2 + j] = jnp.concatenate([low, high], axis=1).astype(jnp.bfloat16)


def products(n, origins, me_ref, left_ref, pieces, held):
    rows = left_ref.shape[1]
    depth, width = pieces[0].shape[-2:]
    groups = HALF // n
    sources = width // 2
    outs = rows // 2
    me = me_ref[0]
    lane = lax.broadcasted_iota(jnp.int32, (outs, width), 1)
    for piece, names in zip(pieces, origins):
        for place, (flip, index) in enumerate(names):
            g = (me ^ flip) * groups + index
            both = jnp.dot(left_ref[g][:, :depth], piece[place], preferred_element_type=jnp.float32)
            mine = jnp.where(lane < sources, both[:outs], both[outs:])
            held[pl.ds(g, outs, stride=HALF_PITCH), :] = mine


def partial_kernel(n, origins, chained, me_ref, left_ref, *refs):
    products(n, origins, me_ref, left_ref, refs[chained:-1], refs[-1])


def correlate_kernel(scale, n, origins, sources, me_ref, left_ref, _, *refs):
    pieces, (out_ref, held, turned_ref, sems) = refs[:-4], refs[-4:]
    products(n, origins, me_ref, left_ref, pieces, held)
    outs = held.shape[0] // HALF_PITCH
    chans = outs // 2
    group = 8
    copies = []
    for part in range(2):
        for c in range(chans):
            base = (part * chans + c) * HALF_PITCH
            turned = held[base : base + HALF, :].T * scale
            rows_at = pl.ds(part * sources * chans + c, sources, stride=chans)
            for half in range(2):
                turned_ref.at[half][rows_at, :] = turned[half * sources : (half + 1) * sources]
            if c % group == group - 1:
                span = pl.ds(c + 1 - group, group)
                for half in range(2):
                    block = turned_ref.at[half].reshape(2, sources, chans, HALF)
                    copy = pltpu.make_async_copy(
                        block.at[part, :, span, :],
                        out_ref.at[part, :, span, pl.ds(half * HALF, HALF)],
                        sems.at[part * (chans // group) + c // group, half],
                    )
                    copy.start()
                    copies.append(copy)
    for copy in copies:
        copy.wait()


def gather_pieces(own, multiply, after_products):
    n = lax.axis_size("chan")
    groups = own.shape[0]
    core, x, y, z, zz = 1, 2, 4, 8, 16
    place = {}

    def keep(array, names):
        for i, name in enumerate(names):
            place[name] = (array, i)
        return array, names

    def pack(names):
        parts = []
        for name in names:
            array, i = place[name]
            if parts and parts[-1][0] is array and parts[-1][2] == i:
                parts[-1][2] = i + 1
            else:
                parts.append([array, i, i + 1])
        blocks = [array[i:j] for array, i, j in parts]
        return blocks[0] if len(blocks) == 1 else jnp.concatenate(blocks, axis=0)

    def send(names, flip):
        route = [(i, i ^ flip) for i in range(n)]
        return lax.ppermute(pack(names), "chan", route), [(f ^ flip, g) for f, g in names]

    def lists(pairs):
        return [array for array, _ in pairs], [names for _, names in pairs]

    def piece(flip):
        return [(flip, g) for g in range(groups)]

    near = [keep(own, piece(0))]
    if n != 32:
        flip = 1
        while flip < n:
            near.append(keep(*send(sorted(place), flip)))
            flip *= 2
        multiply(*lists(near[:-1]))
        return lists(near[-1:])

    first = [send(piece(0), flip) for flip in (x ^ y, y, x, z, zz)]
    arrays = lax.optimization_barrier(lists(first)[0])
    near += [keep(array, names) for array, (_, names) in zip(arrays, first)]
    mid = [
        send(piece(z) + piece(zz), x),
        send(piece(z) + piece(zz), y),
        send(piece(x ^ y), zz),
        send(piece(zz) + piece(x ^ y), z),
    ]
    multiply(*lists(near))
    arrays = after_products(*lists(mid)[0])
    mid = [keep(array, names) for array, (_, names) in zip(arrays, mid)]
    last = [
        send(piece(z ^ zz), x),
        send(piece(z ^ zz), y),
        send(piece(zz ^ x ^ y), z),
    ]
    theirs = send([name for pair in near + mid for name in pair[1]], core)
    multiply(*lists(mid))
    arrays = lists(last)[0]
    arrays[-1:] = after_products(arrays[-1])
    last = [keep(array, names) for array, (_, names) in zip(arrays, last)]
    assert sorted(place) == [(f, g) for f in range(0, n, 2) for g in range(groups)]
    final = [send(names, core) for _, names in last]
    multiply(*lists([theirs] + last))
    return lists(final)


def plan_places(source_index, chans, slots):
    n = lax.axis_size("chan")
    channels = jnp.arange(n * chans, dtype=jnp.int32)
    hits = source_index[:, None] == channels[None, :]
    listed = jnp.any(hits, axis=0).reshape(n, chans).astype(jnp.int32)
    below = (jnp.arange(chans)[:, None] < jnp.arange(chans)[None, :]).astype(jnp.int32)
    rank = jnp.sum(listed[:, :, None] * below[None], axis=1)
    device = jnp.arange(n, dtype=jnp.int32)[:, None]
    place = (rank // slots * n + device) * slots + rank % slots
    places = jnp.sum(jnp.where(hits, place.reshape(1, -1), 0), axis=1, keepdims=True)
    return places, jnp.max(jnp.sum(listed, axis=1))


def per_device(traces, source_index):
    chans, wins, length = traces.shape
    n = lax.axis_size("chan")
    sources = source_index.shape[0]
    halo = lax.ppermute(traces[:GAUGE], "chan", [(i + 1, i) for i in range(n - 1)])
    me = lax.axis_index("chan").astype(jnp.int32).reshape(1)
    table, band = jnp.asarray(make_table(length)), jnp.asarray(make_band())
    depth = 2 * wins
    row_width = HALF * 2 * depth // n
    vmem = pl.BlockSpec(memory_space=pltpu.VMEM)
    smem = pl.BlockSpec(memory_space=pltpu.SMEM)
    params = pltpu.CompilerParams(vmem_limit_bytes=VMEM_LIMIT)
    pairs = HALF // n // 2
    slots = chans // pairs
    turned = jax.ShapeDtypeStruct((chans * PITCH, LANES), jnp.float32)
    stage = jax.ShapeDtypeStruct((3, n * chans, LANES), jnp.float32)
    slot_list = jax.ShapeDtypeStruct((chans + 3,), jnp.int32)
    some, staged, listed = pl.pallas_call(
        functools.partial(whiten_kernel, chans, slots),
        in_specs=[smem] * 2 + [vmem] * 3,
        out_specs=[vmem, vmem, smem],
        out_shape=[turned, stage, slot_list],
        compiler_params=params,
        cost_estimate=pl.CostEstimate(
            flops=2 * (chans - GAUGE) * wins * (length + F // 2) * 2 * F,
            bytes_accessed=8 * 1024 * 1024,
            transcendentals=0,
        ),
        name="whiten",
    )(me, source_index, traces, table, band)
    rows_shape = jax.ShapeDtypeStruct((n, chans, row_width // pairs), jnp.bfloat16)
    spectra, _, *rounds = pl.pallas_call(
        functools.partial(finish_kernel, chans, slots),
        in_specs=[smem] + [vmem] * 6,
        out_specs=[vmem] * (2 + pairs),
        out_shape=[turned, stage] + [rows_shape] * pairs,
        input_output_aliases={5: 0, 6: 1},
        compiler_params=params,
        name="finish",
    )(listed, traces, halo, table, band, some, staged)
    rounds[0], late_index = lax.optimization_barrier((rounds[0], source_index))
    places, most = plan_places(late_index, chans, slots)

    def exchange(number, rows):
        rows = lax.all_to_all(rows, "chan", 0, 0, tiled=True)
        return pl.pallas_call(
            functools.partial(pick_kernel, slots, number * n * slots),
            out_shape=jax.ShapeDtypeStruct((HALF // n, depth, 2 * sources), jnp.bfloat16),
            compiler_params=params,
            name="pick",
        )(places, rows)

    picked = exchange(0, rounds[0])
    for number in range(1, pairs):
        picked = lax.cond(
            most > number * slots,
            lambda p, r, number=number: p + exchange(number, r),
            lambda p, r: p,
            picked,
            rounds[number],
        )
    picked, spectra = lax.optimization_barrier((picked, spectra))
    left = pl.pallas_call(
        functools.partial(left_kernel, chans, depth),
        in_specs=[vmem],
        out_specs=vmem,
        out_shape=jax.ShapeDtypeStruct((HALF, 4 * chans, LANES), jnp.bfloat16),
        compiler_params=params,
        cost_estimate=pl.CostEstimate(
            flops=10 * 1000 * 1000, bytes_accessed=8 * 1024 * 1024, transcendentals=0
        ),
        name="left",
    )(spectra)
    total_windows = wins * lax.axis_size("win")
    held_shape = jax.ShapeDtypeStruct((2 * chans * HALF_PITCH, LANES), jnp.float32)
    held = []

    def multiply(pieces, origins):
        held[:] = [
            pl.pallas_call(
                functools.partial(partial_kernel, n, origins, len(held)),
                in_specs=[smem, vmem] + [vmem] * (len(held) + len(pieces)),
                out_specs=vmem,
                out_shape=held_shape,
                input_output_aliases={2: 0} if held else {},
                compiler_params=params,
                cost_estimate=pl.CostEstimate(
                    flops=100 * 1000 * 1000, bytes_accessed=4 * 1024 * 1024, transcendentals=0
                ),
                name="products",
            )(me, left, *held, *pieces)
        ]

    def after_products(*arrays):
        *arrays, held[0] = lax.optimization_barrier((*arrays, held[0]))
        return arrays

    pieces, origins = gather_pieces(picked, multiply, after_products)
    stack, _ = pl.pallas_call(
        functools.partial(correlate_kernel, 1.0 / total_windows, n, origins, sources),
        in_specs=[smem, vmem, vmem] + [vmem] * len(pieces),
        out_specs=[pl.BlockSpec(memory_space=pl.ANY), vmem],
        out_shape=[jax.ShapeDtypeStruct((2, sources, chans, F), jnp.float32), held_shape],
        scratch_shapes=[
            pltpu.VMEM((2, 2 * sources * chans, HALF), jnp.float32),
            pltpu.SemaphoreType.DMA((chans // 4, 2)),
        ],
        input_output_aliases={2: 1},
        compiler_params=params,
        name="correlate",
    )(me, left, *held, *pieces)
    if lax.axis_size("win") == 1:
        return stack
    return lax.psum_scatter(stack, "win", scatter_dimension=1, tiled=True)


def solution(mesh):
    return jax.shard_map(
        per_device,
        mesh=mesh,
        in_specs=(P("chan", "win", None), P()),
        out_specs=P(None, "win", "chan", None),
        check_vma=False,
    )
```

```python
import functools
import math

import jax
import jax.numpy as jnp
import ml_dtypes
import numpy as np
from jax import lax
from jax.experimental import pallas as pl
from jax.experimental.pallas import tpu as pltpu
from jax.sharding import PartitionSpec as P

F = 256
HALF = 128
F0 = 1
K = 64
GAUGE = 4
LANES = 128
PITCH = F + 8
HALF_PITCH = HALF + 8
VMEM_LIMIT = 24 * 1024 * 1024


def make_table(length):
    times = np.arange(length, dtype=np.int64)[:, None]
    bins = np.arange(F, dtype=np.int64)[None, :] + F0
    phase = (times * bins % length).astype(np.float32) * np.float32(2.0 * math.pi / length)
    phase = phase.astype(np.float64)
    return np.concatenate([np.cos(phase), -np.sin(phase)], axis=1).astype(ml_dtypes.bfloat16)


def make_band():
    rows = np.arange(F)[:, None]
    cols = np.arange(F)[None, :]
    return (np.abs(rows - cols) <= K).astype(ml_dtypes.bfloat16)


def whiten_block(cur, upper, table_ref, band_ref, turned_ref, first):
    chans, wins, length = cur.shape
    rows = chans * wins
    diff = (upper.astype(jnp.float32) - cur.astype(jnp.float32)).reshape(rows, length)
    power = jnp.sum(diff * diff, axis=1, keepdims=True) * (1.0 / length)
    normed = (diff * lax.rsqrt(power + 1e-05)).astype(jnp.bfloat16)
    spec = jnp.dot(normed, table_ref[...], preferred_element_type=jnp.float32)
    real = spec[:, :F]
    imag = spec[:, F:]
    magnitude = jnp.sqrt(real * real + imag * imag).astype(jnp.bfloat16)
    bins = lax.broadcasted_iota(jnp.int32, (1, F), 1)
    counts = (jnp.minimum(bins, K) + jnp.minimum(F - 1 - bins, K) + 1).astype(jnp.float32)
    smooth = jnp.dot(magnitude, band_ref[...], preferred_element_type=jnp.float32) / counts
    gain = 1.0 / (smooth + 1e-06)
    white_re = (real * gain).astype(jnp.bfloat16).astype(jnp.float32)
    white_im = (imag * gain).astype(jnp.bfloat16).astype(jnp.float32)
    pad = jnp.zeros((LANES - 2 * wins, F), jnp.float32)
    for c in range(chans):
        mine = slice(c * wins, (c + 1) * wins)
        both = jnp.concatenate([white_re[mine], white_im[mine], pad], axis=0)
        turned_ref[(first + c) * PITCH : (first + c) * PITCH + F, :] = both.T


def list_slots(chans, me_ref, index_ref, slot_ref):
    mine = jnp.int32(0)
    for s in range(index_ref.shape[0]):
        local = index_ref[s] - me_ref[0] * chans
        bit = lax.shift_left(jnp.int32(1), jnp.clip(local, 0, chans - 1))
        mine = mine | jnp.where((local >= 0) & (local < chans), bit, 0)
    early = count = jnp.int32(0)
    for c in range(chans):
        slot_ref[count] = c
        count = count + (lax.shift_right_logical(mine, c) & 1)
        if c < chans - GAUGE:
            early = count
    slot_ref[chans + 1] = early
    slot_ref[chans + 2] = count


def lay_out(slot, channel, turned_ref, stage_ref, height, slots):
    dests = stage_ref.shape[1] // height
    per_dest = HALF // dests
    lane = lax.broadcasted_iota(jnp.int32, (dests, LANES), 1)
    for pair in range(per_dest // 2):
        piece = []
        for j in range(2):
            for half in range(2):
                at = channel * PITCH + half * HALF + pair * 2 + j
                piece.append(turned_ref[pl.ds(at, dests, stride=per_dest), :])
        a, b, c, d = piece
        b = pltpu.roll(b, 96, 1)
        c = pltpu.roll(c, 64, 1)
        d = pltpu.roll(d, 32, 1)
        rows_at = pl.ds(pair * slots + slot, dests, stride=height)
        stage_ref.at[0][rows_at, :] = jnp.where(lane < 96, a, b)
        stage_ref.at[1][rows_at, :] = jnp.where(lane < 64, b, c)
        stage_ref.at[2][rows_at, :] = jnp.where(lane < 32, c, d)


def whiten_kernel(
    height, slots, me_ref, index_ref, traces_ref, table_ref, band_ref, turned_ref, stage_ref, slot_ref
):
    chans = traces_ref.shape[0]
    stage_ref[...] = jnp.zeros_like(stage_ref)
    list_slots(chans, me_ref, index_ref, slot_ref)
    for c in range(0, chans - GAUGE, GAUGE):
        cur, upper = traces_ref[c : c + GAUGE], traces_ref[c + GAUGE : c + 2 * GAUGE]
        whiten_block(cur, upper, table_ref, band_ref, turned_ref, c)

    def one(slot, carry):
        lay_out(slot, slot_ref[slot], turned_ref, stage_ref, height, slots)
        return carry

    lax.fori_loop(0, jnp.minimum(slot_ref[chans + 1], slots), one, 0)


def finish_kernel(
    height, slots, slot_ref, traces_ref, halo_ref, table_ref, band_ref, _, __, turned_ref, stage_ref, *rounds
):
    chans = traces_ref.shape[0]
    early, count = slot_ref[chans + 1], slot_ref[chans + 2]
    cur = traces_ref[chans - GAUGE :]
    whiten_block(cur, halo_ref[...], table_ref, band_ref, turned_ref, chans - GAUGE)

    def fill(first, start, rows_ref):
        def one(slot, carry):
            channel = slot_ref[first + slot]
            lay_out(slot, channel, turned_ref, stage_ref, height, slots)
            return carry

        lax.fori_loop(start, jnp.minimum(count - first, slots), one, 0)
        for dest in range(rows_ref.shape[0]):
            for tile in range(3):
                block = stage_ref[tile, dest * height : (dest + 1) * height, :]
                rows_ref[dest, :, tile * LANES : (tile + 1) * LANES] = block.astype(jnp.bfloat16)

    def clear(rows_ref):
        rows_ref[...] = jnp.zeros_like(rows_ref)

    fill(0, early, rounds[0])
    for number in range(1, len(rounds)):
        more = count > number * slots
        pl.when(more)(functools.partial(fill, number * slots, 0, rounds[number]))
        pl.when(jnp.logical_not(more))(functools.partial(clear, rounds[number]))


def left_kernel(chans, depth, turned_ref, left_ref):
    lane = lax.broadcasted_iota(jnp.int32, (chans, LANES), 1)

    def one(g, carry):
        stack = []
        for half in range(2):
            real = turned_ref[pl.ds(half * HALF + g, chans, stride=PITCH), :]
            ahead = pltpu.roll(real, depth // 2, 1)
            back = pltpu.roll(real, LANES - depth // 2, 1)
            stack += [real, jnp.where(lane < depth // 2, -back, ahead)]
        left_ref[g] = jnp.concatenate(stack, axis=0).astype(jnp.bfloat16)
        return carry

    lax.fori_loop(0, HALF, one, 0, unroll=8)


def pick_kernel(slots, base, place_ref, rows_ref, out_ref):
    sources = place_ref.shape[0]
    dests, height, width = rows_ref.shape
    groups, depth, _ = out_ref.shape
    rows = rows_ref[...].reshape(dests * height, width)
    ids = lax.broadcasted_iota(jnp.int32, (sources, dests * height), 1)
    place = place_ref[...] - base
    inside = (place >= 0) & (place < dests * slots)
    spot = place // slots * height + place % slots
    for pair in range(groups // 2):
        hit = inside & (ids == spot + pair * slots)
        onehot = jnp.where(hit, 1.0, 0.0).astype(jnp.bfloat16)
        turned = jnp.dot(onehot, rows, preferred_element_type=jnp.float32).T
        for j in range(2):
            low = turned[(2 * j) * depth : (2 * j + 1) * depth]
            high = turned[(2 * j + 1) * depth : (2 * j + 2) * depth]
            out_ref[pair * 2 + j] = jnp.concatenate([low, high], axis=1).astype(jnp.bfloat16)


def products(n, origins, me_ref, left_ref, pieces, held):
    rows = left_ref.shape[1]
    depth, width = pieces[0].shape[-2:]
    groups = HALF // n
    sources = width // 2
    outs = rows // 2
    me = me_ref[0]
    lane = lax.broadcasted_iota(jnp.int32, (outs, width), 1)
    for piece, names in zip(pieces, origins):
        for place, (flip, index) in enumerate(names):
            g = (me ^ flip) * groups + index
            both = jnp.dot(left_ref[g][:, :depth], piece[place], preferred_element_type=jnp.float32)
            mine = jnp.where(lane < sources, both[:outs], both[outs:])
            held[pl.ds(g, outs, stride=HALF_PITCH), :] = mine


def partial_kernel(n, origins, chained, me_ref, left_ref, *refs):
    products(n, origins, me_ref, left_ref, refs[chained:-1], refs[-1])


def correlate_kernel(scale, n, origins, sources, me_ref, left_ref, _, *refs):
    pieces, (out_ref, held, turned_ref, sems) = refs[:-4], refs[-4:]
    products(n, origins, me_ref, left_ref, pieces, held)
    outs = held.shape[0] // HALF_PITCH
    chans = outs // 2
    group = 8
    copies = []
    for part in range(2):
        for c in range(chans):
            base = (part * chans + c) * HALF_PITCH
            turned = held[base : base + HALF, :].T * scale
            rows_at = pl.ds(part * sources * chans + c, sources, stride=chans)
            for half in range(2):
                turned_ref.at[half][rows_at, :] = turned[half * sources : (half + 1) * sources]
            if c % group == group - 1:
                span = pl.ds(c + 1 - group, group)
                for half in range(2):
                    block = turned_ref.at[half].reshape(2, sources, chans, HALF)
                    copy = pltpu.make_async_copy(
                        block.at[part, :, span, :],
                        out_ref.at[part, :, span, pl.ds(half * HALF, HALF)],
                        sems.at[part * (chans // group) + c // group, half],
                    )
                    copy.start()
                    copies.append(copy)
    for copy in copies:
        copy.wait()


def gather_pieces(own, multiply, after_products):
    n = lax.axis_size("chan")
    groups = own.shape[0]
    core, x, y, z, zz = 1, 2, 4, 8, 16
    place = {}

    def keep(array, names):
        for i, name in enumerate(names):
            place[name] = (array, i)
        return array, names

    def pack(names):
        parts = []
        for name in names:
            array, i = place[name]
            if parts and parts[-1][0] is array and parts[-1][2] == i:
                parts[-1][2] = i + 1
            else:
                parts.append([array, i, i + 1])
        blocks = [array[i:j] for array, i, j in parts]
        return blocks[0] if len(blocks) == 1 else jnp.concatenate(blocks, axis=0)

    def send(names, flip):
        route = [(i, i ^ flip) for i in range(n)]
        return lax.ppermute(pack(names), "chan", route), [(f ^ flip, g) for f, g in names]

    def lists(pairs):
        return [array for array, _ in pairs], [names for _, names in pairs]

    def piece(flip):
        return [(flip, g) for g in range(groups)]

    near = [keep(own, piece(0))]
    if n != 32:
        flip = 1
        while flip < n:
            near.append(keep(*send(sorted(place), flip)))
            flip *= 2
        multiply(*lists(near[:-1]))
        return lists(near[-1:])

    first = [send(piece(0), flip) for flip in (x ^ y, y, x, z, zz)]
    arrays = lax.optimization_barrier(lists(first)[0])
    near += [keep(array, names) for array, (_, names) in zip(arrays, first)]
    mid = [
        send(piece(z) + piece(zz), x),
        send(piece(z) + piece(zz), y),
        send(piece(x ^ y), zz),
        send(piece(zz) + piece(x ^ y), z),
    ]
    multiply(*lists(near))
    arrays = after_products(*lists(mid)[0])
    mid = [keep(array, names) for array, (_, names) in zip(arrays, mid)]
    last = [
        send(piece(zz ^ x ^ y), z),
        send(piece(z ^ zz), x),
        send(piece(z ^ zz), y),
    ]
    theirs = send([name for pair in near + mid for name in pair[1]], core)
    multiply(*lists(mid))
    arrays = lists(last)[0]
    arrays[-1:] = after_products(arrays[-1])
    last = [keep(array, names) for array, (_, names) in zip(arrays, last)]
    assert sorted(place) == [(f, g) for f in range(0, n, 2) for g in range(groups)]
    final = [send(names, core) for _, names in last]
    multiply(*lists([theirs] + last))
    return lists(final)


def plan_places(source_index, chans, slots):
    n = lax.axis_size("chan")
    channels = jnp.arange(n * chans, dtype=jnp.int32)
    hits = source_index[:, None] == channels[None, :]
    listed = jnp.any(hits, axis=0).reshape(n, chans).astype(jnp.int32)
    below = (jnp.arange(chans)[:, None] < jnp.arange(chans)[None, :]).astype(jnp.int32)
    rank = jnp.sum(listed[:, :, None] * below[None], axis=1)
    device = jnp.arange(n, dtype=jnp.int32)[:, None]
    place = (rank // slots * n + device) * slots + rank % slots
    places = jnp.sum(jnp.where(hits, place.reshape(1, -1), 0), axis=1, keepdims=True)
    return places, jnp.max(jnp.sum(listed, axis=1))


def per_device(traces, source_index):
    chans, wins, length = traces.shape
    n = lax.axis_size("chan")
    sources = source_index.shape[0]
    halo = lax.ppermute(traces[:GAUGE], "chan", [(i + 1, i) for i in range(n - 1)])
    me = lax.axis_index("chan").astype(jnp.int32).reshape(1)
    table, band = jnp.asarray(make_table(length)), jnp.asarray(make_band())
    depth = 2 * wins
    row_width = HALF * 2 * depth // n
    vmem = pl.BlockSpec(memory_space=pltpu.VMEM)
    smem = pl.BlockSpec(memory_space=pltpu.SMEM)
    params = pltpu.CompilerParams(vmem_limit_bytes=VMEM_LIMIT)
    pairs = HALF // n // 2
    slots = chans // pairs
    turned = jax.ShapeDtypeStruct((chans * PITCH, LANES), jnp.float32)
    stage = jax.ShapeDtypeStruct((3, n * chans, LANES), jnp.float32)
    slot_list = jax.ShapeDtypeStruct((chans + 3,), jnp.int32)
    some, staged, listed = pl.pallas_call(
        functools.partial(whiten_kernel, chans, slots),
        in_specs=[smem] * 2 + [vmem] * 3,
        out_specs=[vmem, vmem, smem],
        out_shape=[turned, stage, slot_list],
        compiler_params=params,
        cost_estimate=pl.CostEstimate(
            flops=2 * (chans - GAUGE) * wins * (length + F // 2) * 2 * F,
            bytes_accessed=8 * 1024 * 1024,
            transcendentals=0,
        ),
        name="whiten",
    )(me, source_index, traces, table, band)
    rows_shape = jax.ShapeDtypeStruct((n, chans, row_width // pairs), jnp.bfloat16)
    spectra, _, *rounds = pl.pallas_call(
        functools.partial(finish_kernel, chans, slots),
        in_specs=[smem] + [vmem] * 6,
        out_specs=[vmem] * (2 + pairs),
        out_shape=[turned, stage] + [rows_shape] * pairs,
        input_output_aliases={5: 0, 6: 1},
        compiler_params=params,
        name="finish",
    )(listed, traces, halo, table, band, some, staged)
    rounds[0], late_index = lax.optimization_barrier((rounds[0], source_index))
    places, most = plan_places(late_index, chans, slots)

    def exchange(number, rows):
        rows = lax.all_to_all(rows, "chan", 0, 0, tiled=True)
        return pl.pallas_call(
            functools.partial(pick_kernel, slots, number * n * slots),
            out_shape=jax.ShapeDtypeStruct((HALF // n, depth, 2 * sources), jnp.bfloat16),
            compiler_params=params,
            name="pick",
        )(places, rows)

    picked = exchange(0, rounds[0])
    for number in range(1, pairs):
        picked = lax.cond(
            most > number * slots,
            lambda p, r, number=number: p + exchange(number, r),
            lambda p, r: p,
            picked,
            rounds[number],
        )
    picked, spectra = lax.optimization_barrier((picked, spectra))
    left = pl.pallas_call(
        functools.partial(left_kernel, chans, depth),
        in_specs=[vmem],
        out_specs=vmem,
        out_shape=jax.ShapeDtypeStruct((HALF, 4 * chans, LANES), jnp.bfloat16),
        compiler_params=params,
        cost_estimate=pl.CostEstimate(
            flops=10 * 1000 * 1000, bytes_accessed=8 * 1024 * 1024, transcendentals=0
        ),
        name="left",
    )(spectra)
    total_windows = wins * lax.axis_size("win")
    held_shape = jax.ShapeDtypeStruct((2 * chans * HALF_PITCH, LANES), jnp.float32)
    held = []

    def multiply(pieces, origins):
        held[:] = [
            pl.pallas_call(
                functools.partial(partial_kernel, n, origins, len(held)),
                in_specs=[smem, vmem] + [vmem] * (len(held) + len(pieces)),
                out_specs=vmem,
                out_shape=held_shape,
                input_output_aliases={2: 0} if held else {},
                compiler_params=params,
                cost_estimate=pl.CostEstimate(
                    flops=100 * 1000 * 1000, bytes_accessed=4 * 1024 * 1024, transcendentals=0
                ),
                name="products",
            )(me, left, *held, *pieces)
        ]

    def after_products(*arrays):
        *arrays, held[0] = lax.optimization_barrier((*arrays, held[0]))
        return arrays

    pieces, origins = gather_pieces(picked, multiply, after_products)
    stack, _ = pl.pallas_call(
        functools.partial(correlate_kernel, 1.0 / total_windows, n, origins, sources),
        in_specs=[smem, vmem, vmem] + [vmem] * len(pieces),
        out_specs=[pl.BlockSpec(memory_space=pl.ANY), vmem],
        out_shape=[jax.ShapeDtypeStruct((2, sources, chans, F), jnp.float32), held_shape],
        scratch_shapes=[
            pltpu.VMEM((2, 2 * sources * chans, HALF), jnp.float32),
            pltpu.SemaphoreType.DMA((chans // 4, 2)),
        ],
        input_output_aliases={2: 1},
        compiler_params=params,
        name="correlate",
    )(me, left, *held, *pieces)
    if lax.axis_size("win") == 1:
        return stack
    return lax.psum_scatter(stack, "win", scatter_dimension=1, tiled=True)


def solution(mesh):
    return jax.shard_map(
        per_device,
        mesh=mesh,
        in_specs=(P("chan", "win", None), P()),
        out_specs=P(None, "win", "chan", None),
        check_vma=False,
    )
```
